32 devices in a mesh: fsdp: 2 (over core), ctx: 4 (over z), tp: 4 (over y, x).
Axes of the slice: x: 2, y: 2, z: 4, core: 2. Of those that a mesh axis runs over, the one named last changes fastest.
Arguments:
- inputs: bfloat16 [8, 1024, 1152], P('fsdp', 'ctx'), may hold values from -6 to 6
- target: bfloat16 [8, 1024, 1152], P('fsdp', 'ctx'), may hold values from -6 to 6
- segment_ids: int32 [8, 1024], P('fsdp', 'ctx'), may hold values from 0 to 16, as said below
- w_query: bfloat16 [1152, 1024], P(('fsdp', 'ctx'), 'tp'), may hold values from -0.1875 to 0.1875
- w_key: bfloat16 [1152, 256], P(('fsdp', 'ctx')), may hold values from -0.1875 to 0.1875
- w_value: bfloat16 [1152, 256], P(('fsdp', 'ctx')), may hold values from -0.1875 to 0.1875
- w_out: bfloat16 [1024, 1152], P('tp', ('fsdp', 'ctx')), may hold values from -0.1875 to 0.1875
- w_gate: bfloat16 [1152, 6912], P(('fsdp', 'ctx'), 'tp'), may hold values from -0.1875 to 0.1875
- w_up: bfloat16 [1152, 6912], P(('fsdp', 'ctx'), 'tp'), may hold values from -0.1875 to 0.1875
- w_down: bfloat16 [6912, 1152], P('tp', ('fsdp', 'ctx')), may hold values from -0.078125 to 0.078125
- gain_input: bfloat16 [1152], P(('fsdp', 'ctx')), may hold values from 0.5 to 1.5
- gain_query: bfloat16 [256], P(('fsdp', 'ctx')), may hold values from 0.5 to 1.5
- gain_key: bfloat16 [256], P(('fsdp', 'ctx')), may hold values from 0.5 to 1.5
- gain_post_attn: bfloat16 [1152], P(('fsdp', 'ctx')), may hold values from 0.5 to 1.5
- gain_pre_ffn: bfloat16 [1152], P(('fsdp', 'ctx')), may hold values from 0.5 to 1.5
- gain_post_ffn: bfloat16 [1152], P(('fsdp', 'ctx')), may hold values from 0.5 to 1.5
Outputs:
- output: bfloat16 [8, 1024, 1152], P('fsdp', ('ctx', 'tp'))
- loss: float32 [], replicated
- grad_input: float32 [8, 1024, 1152], P('fsdp', ('ctx', 'tp'))
- grad_query: float32 [1152, 1024], P(('fsdp', 'ctx'), 'tp')
- grad_key: float32 [1152, 256], P(('fsdp', 'ctx'))
- grad_value: float32 [1152, 256], P(('fsdp', 'ctx'))
- grad_out: float32 [1024, 1152], P('tp', ('fsdp', 'ctx'))
- grad_gate: float32 [1152, 6912], P(('fsdp', 'ctx'), 'tp')
- grad_up: float32 [1152, 6912], P(('fsdp', 'ctx'), 'tp')
- grad_down: float32 [6912, 1152], P('tp', ('fsdp', 'ctx'))
- grad_gain_input: float32 [1152], P(('fsdp', 'ctx'))
- grad_gain_query: float32 [256], P(('fsdp', 'ctx'))
- grad_gain_key: float32 [256], P(('fsdp', 'ctx'))
- grad_gain_post_attn: float32 [1152], P(('fsdp', 'ctx'))
- grad_gain_pre_ffn: float32 [1152], P(('fsdp', 'ctx'))
- grad_gain_post_ffn: float32 [1152], P(('fsdp', 'ctx'))
The draws below stay inside these ranges and needn't reach their ends.
Inputs may be any that keep to these rules, and one draw needn't show every extreme that they name: `segment_ids`: in each sequence the nonzero ids number its 16 documents from 1 in order of position, each document a contiguous run of positions; padding (0) stands only after the last document.
All inputs are finite; a program needn't handle non-finite values.
Results may differ from the reference program's by a relative error of at most 0.018.
Values may be sent and summed in bfloat16 or wider, within the bound.
No kernel may reach another device: no remote copies, remote signals or barrier semaphores. Data moves between devices by JAX's collectives and lax.ppermute only.
A program may use at most 192 MiB of HBM per device.

```python
import jax
import jax.numpy as jnp
from jax import lax

D = 1152
NH = 4
HD = 256
FF = 6912
WIN = 512
DOCS = 16
BLK = 256
SEQ_DEV = 4
SEQS = 8
LEN = 1024
TOKENS = 8192


def draw_segment_ids(key, part):
    key_pad, key_len, key_exp, key_pick = jax.random.split(key, 4)
    pad_rows = BLK * 3 // 4 + jax.random.randint(key_pad, (SEQS,), 0, BLK // 8 + 1)
    content = LEN - pad_rows
    lengths = jnp.left_shift(jax.random.randint(key_len, (SEQS, DOCS), 1, 9), jax.random.randint(key_exp, (SEQS, DOCS), 0, 8))
    before_sum = jnp.cumsum(lengths, axis=1) - lengths
    length_total = jnp.sum(lengths, axis=1, keepdims=True)
    room = (content - DOCS)[:, None]
    starts_spread = jnp.arange(DOCS, dtype=jnp.int32)[None, :] + before_sum * room // length_total
    step_rows = max(1, BLK // (2 * DOCS))
    starts_long = jnp.broadcast_to(jnp.arange(DOCS, dtype=jnp.int32)[None, :] * step_rows, (SEQS, DOCS))
    groups = SEQS // SEQ_DEV
    picked = jnp.arange(groups, dtype=jnp.int32) * SEQ_DEV + jax.random.randint(key_pick, (groups,), 0, SEQ_DEV)
    is_long = jnp.any(jnp.arange(SEQS, dtype=jnp.int32)[:, None] == picked[None, :], axis=1)
    starts = jnp.where(is_long[:, None], starts_long, starts_spread)
    positions = jnp.arange(LEN, dtype=jnp.int32)
    doc_number = jnp.sum((positions[None, :, None] >= starts[:, None, :]).astype(jnp.int32), axis=2)
    return jnp.where(positions[None, :] < content[:, None], doc_number, 0).astype(jnp.int32)


def level_of(stream_key, dims, pieces, smallest, largest):
    level = 1.0
    for position, blocks in pieces:
        draws = jax.random.uniform(jax.random.fold_in(jax.random.fold_in(stream_key, 6), position), (blocks,), jnp.float32, smallest / len(pieces), largest / len(pieces))
        level = level * jnp.repeat(jnp.exp(draws), dims[position] // blocks).reshape((-1,) + (1,) * (len(dims) - 1 - position))
    return level


def bell_draw(rng, dims, width, reach, pieces=(), kind=jnp.bfloat16):
    level = level_of(rng, dims, pieces, -0.22, 0.18) if pieces else 1.0
    entries = jax.random.normal(rng, dims, jnp.float32) * width * level
    return jnp.minimum(jnp.maximum(entries, -reach), reach).astype(kind)


def setup_inputs(seed: int = 0) -> dict:
    seeds = jax.random.split(jax.random.key(seed), 17)
    return {
        "inputs": bell_draw(seeds[0], (SEQS, LEN, D), 1.0, 6.0, ((0, 2), (1, 4))),
        "target": bell_draw(seeds[1], (SEQS, LEN, D), 1.0, 6.0, ((0, 2), (1, 4))),
        "segment_ids": draw_segment_ids(jax.random.fold_in(seeds[16], 71), 0),
        "w_query": bell_draw(seeds[3], (D, NH * HD), D ** -0.5, 0.1875, ((0, 8), (1, 4))),
        "w_key": bell_draw(seeds[4], (D, HD), D ** -0.5, 0.1875, ((0, 8),)),
        "w_value": bell_draw(seeds[5], (D, HD), D ** -0.5, 0.1875, ((0, 8),)),
        "w_out": bell_draw(seeds[6], (NH * HD, D), (NH * HD) ** -0.5, 0.1875, ((0, 4), (1, 8))),
        "w_gate": bell_draw(seeds[7], (D, FF), D ** -0.5, 0.1875, ((0, 8), (1, 4))),
        "w_up": bell_draw(seeds[8], (D, FF), D ** -0.5, 0.1875, ((0, 8), (1, 4))),
        "w_down": bell_draw(seeds[9], (FF, D), FF ** -0.5, 0.078125, ((0, 4), (1, 8))),
        "gain_input": jnp.clip(1.0 + 0.1 * jax.random.normal(seeds[10], (D,), jnp.float32), 0.5, 1.5).astype(jnp.bfloat16),
        "gain_query": jnp.clip(1.0 + 0.1 * jax.random.normal(seeds[11], (HD,), jnp.float32), 0.5, 1.5).astype(jnp.bfloat16),
        "gain_key": jnp.clip(1.0 + 0.1 * jax.random.normal(seeds[12], (HD,), jnp.float32), 0.5, 1.5).astype(jnp.bfloat16),
        "gain_post_attn": jnp.clip(1.0 + 0.1 * jax.random.normal(seeds[13], (D,), jnp.float32), 0.5, 1.5).astype(jnp.bfloat16),
        "gain_pre_ffn": jnp.clip(1.0 + 0.1 * jax.random.normal(seeds[14], (D,), jnp.float32), 0.5, 1.5).astype(jnp.bfloat16),
        "gain_post_ffn": jnp.clip(1.0 + 0.1 * jax.random.normal(seeds[15], (D,), jnp.float32), 0.5, 1.5).astype(jnp.bfloat16),
    }


epsilon = 1e-06
masked_score = -1e+30

@jax.custom_vjp
def low(v):
    return lax.optimization_barrier(v.astype(jnp.bfloat16)).astype(jnp.float32)

@jax.custom_vjp
def low_back(v):
    return v

def low_keep(v):
    return (low(v), None)

def low_pass(kept, grad):
    return (grad,)

def back_keep(v):
    return (v, None)

def back_low(kept, grad):
    return (low(grad),)
low.defvjp(low_keep, low_pass)
low_back.defvjp(back_keep, back_low)

def product(left_side, right_side):
    return jnp.dot(left_side, right_side, precision=lax.Precision.HIGHEST, preferred_element_type=jnp.float32)

def rms_norm(values, gain_row):
    return values * lax.rsqrt(lax.optimization_barrier(jnp.mean(values * values, axis=-1, keepdims=True)) + epsilon) * gain_row

def turn_half(values):
    half_width = values.shape[-1] // 2
    return jnp.concatenate([-values[..., half_width:], values[..., :half_width]], axis=-1)

def rotary_tables(positions, head_width):
    frequency = 10000.0 ** (-2.0 * jnp.arange(head_width // 2, dtype=jnp.float32) / head_width)
    angles = positions.astype(jnp.float32)[:, None] * frequency[None, :]
    angles = jnp.concatenate([angles, angles], axis=-1)
    return (jnp.cos(angles), jnp.sin(angles))

def rotate(values, cos_table, sin_table):
    return values * cos_table + turn_half(values) * sin_table

def attend(query_rot, key_rot, value_low, seg_row):
    halo_blocks = -(-(WIN - 1) // BLK)
    front_rows = halo_blocks * BLK
    span_rows = front_rows + BLK
    key_pad = jnp.concatenate([jnp.zeros((front_rows, HD), jnp.float32), key_rot], axis=0)
    value_pad = jnp.concatenate([jnp.zeros((front_rows, HD), jnp.float32), value_low], axis=0)
    seg_pad = jnp.concatenate([jnp.full((front_rows,), -1, jnp.int32), seg_row.astype(jnp.int32)], axis=0)

    def one_block(block_index):
        start_row = (block_index * BLK).astype(jnp.int32)
        queries = lax.dynamic_slice_in_dim(query_rot, start_row, BLK, 0)
        key_rows = lax.dynamic_slice_in_dim(key_pad, start_row, span_rows, 0)
        value_rows = lax.dynamic_slice_in_dim(value_pad, start_row, span_rows, 0)
        query_seg = lax.dynamic_slice_in_dim(seg_row.astype(jnp.int32), start_row, BLK, 0)
        key_seg = lax.dynamic_slice_in_dim(seg_pad, start_row, span_rows, 0)
        query_pos = start_row + jnp.arange(BLK, dtype=jnp.int32)
        key_pos = start_row - front_rows + jnp.arange(span_rows, dtype=jnp.int32)
        allowed = (query_seg[:, None] == key_seg[None, :]) & (key_pos[None, :] <= query_pos[:, None]) & (key_pos[None, :] > query_pos[:, None] - WIN)
        scores = low_back(jnp.einsum('qhd,kd->hqk', queries, key_rows, precision=lax.Precision.HIGHEST))
        scores = jnp.where(allowed[None], scores, masked_score)
        attn_prob = low(jax.nn.softmax(scores, axis=-1))
        return jnp.einsum('hqk,kd->qhd', attn_prob, value_rows, precision=lax.Precision.HIGHEST)
    blocks = lax.map(jax.checkpoint(one_block), jnp.arange(LEN // BLK, dtype=jnp.int32))
    return blocks.reshape(LEN, NH, HD)

def layer(x_seq, seg_row, params):
    w_query, w_key, w_value, w_out, w_gate, w_up, w_down, gain_input, gain_query, gain_key, gain_post_attn, gain_pre_ffn, gain_post_ffn = params
    positions = jnp.arange(LEN, dtype=jnp.int32)
    cos_table, sin_table = rotary_tables(positions, HD)
    normed = low(rms_norm(x_seq, gain_input))
    query = low_back(product(normed, w_query)).reshape(LEN, NH, HD)
    key_raw = low_back(product(normed, w_key))
    value_low = low(low_back(product(normed, w_value)))
    query_rot = low(rotate(rms_norm(query, gain_query), cos_table[:, None, :], sin_table[:, None, :]) * HD ** (-0.5))
    key_rot = low(rotate(rms_norm(key_raw, gain_key), cos_table, sin_table))
    attended = low(low_back(attend(query_rot, key_rot, value_low, seg_row))).reshape(LEN, NH * HD)
    branch = low_back(product(attended, w_out))
    hidden = x_seq + rms_norm(branch, gain_post_attn)
    ffn_in = low(rms_norm(hidden, gain_pre_ffn))
    gate = low_back(product(ffn_in, w_gate))
    up_proj = low_back(product(ffn_in, w_up))
    act_low = low(jax.nn.gelu(gate, approximate=True) * up_proj)
    ffn_out = low_back(product(act_low, w_down))
    return hidden + rms_norm(ffn_out, gain_post_ffn)

def reference(inputs, target, segment_ids, w_query, w_key, w_value, w_out, w_gate, w_up, w_down, gain_input, gain_query, gain_key, gain_post_attn, gain_pre_ffn, gain_post_ffn):
    weights = tuple((weight_arg.astype(jnp.float32) for weight_arg in (w_query, w_key, w_value, w_out, w_gate, w_up, w_down, gain_input, gain_query, gain_key, gain_post_attn, gain_pre_ffn, gain_post_ffn)))
    valid = (segment_ids != 0).astype(jnp.float32)
    count = jnp.sum(valid)
    factor = TOKENS / (2.0 * count)
    zero_grads = tuple((jnp.zeros_like(weight_arg) for weight_arg in weights))

    def per_sequence(running, members):
        grads_sum, error_sum = running
        x_seq, target_seq, seg_row, valid_row = members

        def objective(x_in, *params):
            result = layer(x_in, seg_row, params)
            mismatch = result - target_seq
            sq_error = jnp.sum(valid_row[:, None] * mismatch * mismatch)
            return (sq_error * factor, (result, sq_error))
        scaled, pullback, aux_out = jax.vjp(objective, x_seq, *weights, has_aux=True)
        cotangents = pullback(jnp.ones_like(scaled))
        new_sum = tuple((total_grad + new_grad for total_grad, new_grad in zip(grads_sum, cotangents[1:])))
        return ((new_sum, error_sum + aux_out[1]), (aux_out[0], cotangents[0]))
    start_state = (zero_grads, jnp.zeros((), jnp.float32))
    (grads, error_total), (results, grad_inputs) = lax.scan(per_sequence, start_state, (inputs.astype(jnp.float32), target.astype(jnp.float32), segment_ids, valid))
    loss = error_total / (2.0 * D * count)
    return (results.astype(jnp.bfloat16), loss, grad_inputs, grads[0], grads[1], grads[2], grads[3], grads[4], grads[5], grads[6], grads[7], grads[8], grads[9], grads[10], grads[11], grads[12])
```

```python
import functools

import jax
import jax.numpy as jnp
from jax import lax
from jax.experimental import pallas as pl
from jax.experimental.pallas import tpu as pltpu
from jax.sharding import PartitionSpec as P

WIN = 512
EPS = 1e-06
MASKED = -1e30
LOW = jnp.bfloat16
F32 = jnp.float32


def swap(values, axis, bits):
    return lax.ppermute(values, axis, [(i, i ^ bits) for i in range(lax.axis_size(axis))])


def shifted(values, axis, by):
    size = lax.axis_size(axis)
    return lax.ppermute(values, axis, [(i, i + by) for i in range(size) if 0 <= i + by < size])


def exchange(values, axes):
    return lax.all_to_all(values, axes, 0, 0, tiled=True)


def dot(left, right, contract):
    return lax.dot_general(left, right, (contract, ((), ())), preferred_element_type=F32)


def mm(left, right):
    return dot(left, right, ((1,), (0,)))


def mm_t(left, right):
    return dot(left, right, ((1,), (1,)))


def t_mm(left, right):
    return dot(left, right, ((0,), (0,)))


def inverse_rms(values):
    return lax.rsqrt(jnp.mean(values * values, axis=-1, keepdims=True) + EPS)


def rms_back(grad, values, inverse, gain_row):
    n = values * inverse
    eg = grad * gain_row
    return inverse * (eg - n * jnp.mean(eg * n, axis=-1, keepdims=True)), grad * n


def turn(values):
    half = values.shape[-1] // 2
    return jnp.concatenate([-values[..., half:], values[..., :half]], axis=-1)


def turn_back(values):
    half = values.shape[-1] // 2
    return jnp.concatenate([values[..., half:], -values[..., :half]], axis=-1)


def rotary_tables(positions, head_width):
    frequency = 10000.0 ** (-2.0 * jnp.arange(head_width // 2, dtype=F32) / head_width)
    angles = positions.astype(F32)[:, None] * frequency[None, :]
    angles = jnp.concatenate([angles, angles], axis=-1)
    return jnp.cos(angles), jnp.sin(angles)


def heads_of(values, heads):
    width = values.shape[1] // heads
    return [values[:, h * width : (h + 1) * width] for h in range(heads)]


def mask_of(qinfo_ref, kinfo_ref):
    qpos, qseg = qinfo_ref[0, :, 0:1], qinfo_ref[0, :, 1:2]
    kpos, kseg = kinfo_ref[0, 0:1, :], kinfo_ref[0, 1:2, :]
    return (kseg == qseg) & (kpos <= qpos) & (kpos > qpos - WIN)


def attend_kernel(heads, qinfo_ref, kinfo_ref, q_ref, gain_ref, cos_ref, sin_ref, kv_ref, rot_ref, out_ref, lse_ref):
    width = q_ref.shape[1] // heads
    scale = width ** (-0.5)
    spans = kv_ref.shape[0] * kv_ref.shape[2]
    rotated = []
    for h, q in enumerate(heads_of(q_ref[...], heads)):
        n = q * inverse_rms(q) * gain_ref[...]
        rot = ((n * cos_ref[...] + turn(n) * sin_ref[...]) * scale).astype(LOW)
        rot_ref[:, h * width : (h + 1) * width] = rot
        rotated.append(rot)
    rows = jnp.concatenate(rotated, axis=0)
    keys = kv_ref[:, 0, :, :width].reshape(spans, width)
    vals = kv_ref[:, 0, :, width:].reshape(spans, width)
    bias = jnp.where(mask_of(qinfo_ref, kinfo_ref), 0.0, MASKED)
    allowed = jnp.concatenate([bias] * heads, axis=0) == 0.0
    scores = jnp.where(allowed, mm_t(rows, keys), MASKED)
    top = jnp.max(scores, axis=1, keepdims=True)
    expos = jnp.exp(scores - top)
    total = jnp.sum(expos, axis=1, keepdims=True)
    lse_ref[0] = top + jnp.log(total)
    probs = (expos / total).astype(LOW)
    attended = mm(probs, vals).astype(LOW)
    count = q_ref.shape[0]
    for h in range(heads):
        out_ref[:, h * width : (h + 1) * width] = attended[h * count : (h + 1) * count]


def attend_back_kernel(heads, chunks, qinfo_ref, kinfo_ref, q_ref, gain_ref, cos_ref, sin_ref, kv_ref, rot_ref, lse_ref, dout_ref,
                       dq_ref, dgain_ref, *dkv_refs):
    width = q_ref.shape[1] // heads
    scale = width ** (-0.5)
    spans = kv_ref.shape[0] * kv_ref.shape[2]
    count = q_ref.shape[0]
    rows = jnp.concatenate(heads_of(rot_ref[...], heads), axis=0)
    douts = jnp.concatenate(heads_of(dout_ref[...], heads), axis=0)
    keys = kv_ref[:, 0, :, :width].reshape(spans, width)
    vals = kv_ref[:, 0, :, width:].reshape(spans, width)
    bias = jnp.where(mask_of(qinfo_ref, kinfo_ref), 0.0, MASKED)
    allowed = jnp.concatenate([bias] * heads, axis=0) == 0.0
    probs = jnp.where(allowed, jnp.exp(mm_t(rows, keys) - lse_ref[0]), 0.0)
    d_probs = mm_t(douts, vals)
    delta = jnp.sum(probs * d_probs, axis=1, keepdims=True)
    d_scores = (probs * (d_probs - delta)).astype(LOW)
    d_rows = mm(d_scores, keys)
    d_keys = t_mm(d_scores, rows)
    d_vals = t_mm(probs.astype(LOW), douts)
    per = kv_ref.shape[2]
    blocks = kv_ref.shape[0] // chunks
    for b in range(blocks):
        for p in range(chunks):
            at = (b * chunks + p) * per
            dkv_refs[p][b, 0, :, :width] = d_keys[at : at + per].astype(dkv_refs[p].dtype)
            dkv_refs[p][b, 0, :, width:] = d_vals[at : at + per].astype(dkv_refs[p].dtype)
    gain_sum = jnp.zeros((1, width), F32)
    for h, q in enumerate(heads_of(q_ref[...], heads)):
        e = d_rows[h * count : (h + 1) * count] * scale
        e = e * cos_ref[...] + turn_back(e * sin_ref[...])
        d_q, d_g = rms_back(e, q, inverse_rms(q), gain_ref[...])
        gain_sum = gain_sum + jnp.sum(d_g, axis=0, keepdims=True)
        dq_ref[:, h * width : (h + 1) * width] = d_q.astype(LOW)
    dgain_ref[0] = gain_sum


def attention_specs(seqs, rows, spans, chunk_count, wide, width):
    whole = lambda *shape: pl.BlockSpec(shape, lambda s: (0,) * len(shape))
    return dict(
        qinfo=pl.BlockSpec((1, rows, 2), lambda s: (s, 0, 0)),
        kinfo=pl.BlockSpec((1, 2, spans), lambda s: (s, 0, 0)),
        q=pl.BlockSpec((rows, wide), lambda s: (s, 0)),
        gain=whole(1, width),
        table=whole(rows, width),
        kv=pl.BlockSpec((chunk_count, 1, rows, 2 * width), lambda s: (0, s, 0, 0)),
        lse=pl.BlockSpec((1, rows * (wide // width), 1), lambda s: (s, 0, 0)),
        dgain=pl.BlockSpec((1, 1, width), lambda s: (s, 0, 0)),
    )


def shards(inputs, target, segment_ids, w_query, w_key, w_value, w_out, w_gate, w_up, w_down,
           gain_input, gain_query, gain_key, gain_post_attn, gain_pre_ffn, gain_post_ffn):
    F, C, T = (lax.axis_size(a) for a in ("fsdp", "ctx", "tp"))
    f, z, t = (lax.axis_index(a) for a in ("fsdp", "ctx", "tp"))
    me = f * C + z
    seqs, block_rows, width_model = inputs.shape
    piece = w_query.shape[0]
    head_width = w_key.shape[1]
    gain_piece = gain_query.shape[0]
    sub = block_rows // T
    own = seqs * sub
    half = C * piece
    halo = -(-(WIN - 1) // block_rows)
    spans = (halo + 1) * block_rows

    packed = jnp.concatenate(
        [gain_input, gain_post_attn, gain_pre_ffn, gain_post_ffn, gain_query, gain_key, segment_ids.astype(LOW).reshape(-1)]
    )
    packed = exchange(jnp.broadcast_to(packed[None], (F * C, packed.shape[0])), ("fsdp", "ctx")).astype(F32)
    at = 4 * piece
    g_input, g_post_attn, g_pre_ffn, g_post_ffn = [
        packed[:, i * piece : (i + 1) * piece].reshape(1, width_model) for i in range(4)
    ]
    g_query, g_key = [
        packed[:, at + i * gain_piece : at + (i + 1) * gain_piece].reshape(1, head_width) for i in range(2)
    ]
    seg_blocks = packed[:, at + 2 * gain_piece :].astype(jnp.int32)
    count = jnp.sum((seg_blocks != 0).astype(F32))

    def both_cores(mine):
        other = swap(mine, "fsdp", 1)
        return jnp.where(f == 0, jnp.concatenate([mine, other], axis=0), jnp.concatenate([other, mine], axis=0))

    near = lax.all_gather(jnp.concatenate([w_query, w_out.T, w_key, w_value], axis=1), "ctx", axis=0, tiled=True)
    kv_full = both_cores(near[:, 2 * head_width :])
    gate_full = lax.all_gather(w_gate, ("fsdp", "ctx"), axis=0, tiled=True)
    up_full = lax.all_gather(w_up, ("fsdp", "ctx"), axis=0, tiled=True)
    down_full = lax.all_gather(w_down.T, ("fsdp", "ctx"), axis=0, tiled=True)
    near = near[:, : 2 * head_width]
    near = [near] + [swap(near, "tp", p) for p in range(1, T)]
    q_full, out_full = [
        both_cores(jnp.concatenate([v[:, i * head_width : (i + 1) * head_width] for v in near], axis=1)) for i in range(2)
    ]

    def sub_rows(values):
        return [lax.dynamic_slice_in_dim(values, (t ^ p) * sub, sub, 1) for p in range(T)]

    x_low = jnp.stack(sub_rows(inputs)).reshape(T * own, width_model)
    target_own = lax.dynamic_slice_in_dim(target, t * sub, sub, 1).reshape(own, width_model).astype(F32)
    positions = jnp.concatenate([z * block_rows + (t ^ p) * sub + jnp.arange(sub, dtype=jnp.int32) for p in range(T)])
    segs = [segment_ids + 1]
    for d in range(1, halo + 1):
        far = lax.dynamic_index_in_dim(seg_blocks, jnp.maximum(me - d, 0), 0, False).reshape(seqs, block_rows)
        segs.append(jnp.where(z >= d, far + 1, 0))
    key_seg = jnp.concatenate([v for seg in segs for v in sub_rows(seg)], axis=1)
    key_pos = jnp.concatenate([positions - d * block_rows for d in range(halo + 1)])
    kinfo = jnp.stack([jnp.broadcast_to(key_pos, (seqs, spans)), key_seg], axis=1)
    qinfo = jnp.stack([jnp.broadcast_to(positions[:sub], (seqs, sub)), key_seg[:, :sub]], axis=2)
    valid_own = (key_seg[:, :sub] != 1).astype(F32).reshape(own, 1)

    cos_all, sin_all = rotary_tables(positions, head_width)
    tile_rows = lambda table: jnp.broadcast_to(table.reshape(T, 1, sub, head_width), (T, seqs, sub, head_width)).reshape(T * own, head_width)
    x_all = x_low.astype(F32)
    normed = (x_all * inverse_rms(x_all) * g_input).astype(LOW)
    kv_raw = mm(normed, kv_full)
    key_raw = kv_raw[:, :head_width]
    key_n = key_raw * inverse_rms(key_raw) * g_key
    key_rot = (key_n * tile_rows(cos_all) + turn(key_n) * tile_rows(sin_all)).astype(LOW)
    pair = jnp.concatenate([key_rot, kv_raw[:, head_width:].astype(LOW)], axis=1).reshape(T, seqs, sub, 2 * head_width)
    pieces = [pair]
    for d in range(1, halo + 1):
        far = shifted(pair[0], "ctx", d)
        pieces.append(jnp.stack([far] + [swap(far, "tp", p) for p in range(1, T)]))
    kv_rows = jnp.concatenate(pieces, axis=0)
    normed_own = normed[:own]
    x_own = x_all[:own]
    q_raw = mm(normed_own, q_full)
    heads = q_raw.shape[1] // head_width
    wide = q_raw.shape[1]
    chunk_count = (halo + 1) * T
    specs = attention_specs(seqs, sub, spans, chunk_count, wide, head_width)
    cos_own, sin_own = cos_all[:sub], sin_all[:sub]
    q_rot, attended, lse = pl.pallas_call(
        functools.partial(attend_kernel, heads),
        grid=(seqs,),
        in_specs=[specs[k] for k in ("qinfo", "kinfo", "q", "gain", "table", "table", "kv")],
        out_specs=[specs["q"], specs["q"], specs["lse"]],
        out_shape=[
            jax.ShapeDtypeStruct((own, wide), LOW),
            jax.ShapeDtypeStruct((own, wide), LOW),
            jax.ShapeDtypeStruct((seqs, sub * heads, 1), F32),
        ],
        compiler_params=pltpu.CompilerParams(vmem_limit_bytes=32 * 1024 * 1024),
        name="attend",
    )(qinfo, kinfo, q_raw, g_query, cos_own, sin_own, kv_rows)
    branch = mm_t(attended, out_full)
    inv_branch = inverse_rms(branch)
    hidden = x_own + branch * inv_branch * g_post_attn
    inv_hidden = inverse_rms(hidden)
    ffn_in = (hidden * inv_hidden * g_pre_ffn).astype(LOW)

    ffn_ins = [ffn_in] + [swap(ffn_in, "tp", p) for p in range(1, T)]
    gates, ups, acts, ffn_out = [], [], [], None
    for p, rows in enumerate(ffn_ins):
        gate, up = mm(rows, gate_full), mm(rows, up_full)
        act = (jax.nn.gelu(gate, approximate=True) * up).astype(LOW)
        part = mm_t(act, down_full)
        ffn_out = part if p == 0 else ffn_out + swap(part.astype(LOW), "tp", p).astype(F32)
        gates.append(gate)
        ups.append(up)
        acts.append(act)
    inv_ffn = inverse_rms(ffn_out)
    result = hidden + ffn_out * inv_ffn * g_post_ffn
    mismatch = result - target_own
    error = jnp.sum(valid_own * mismatch * mismatch)
    all_tokens = seqs * block_rows * F * C
    d_result = (all_tokens / count) * valid_own * mismatch
    d_ffn, dg_post_ffn = rms_back(d_result, ffn_out, inv_ffn, g_post_ffn)
    d_ffn_low = d_ffn.astype(LOW)
    d_outs = [d_ffn_low] + [swap(d_ffn_low, "tp", p) for p in range(1, T)]
    d_gates, d_ups, d_ffn_in = [], [], None
    for p, rows in enumerate(d_outs):
        d_act = mm(rows, down_full)
        _, back = jax.vjp(lambda g, u: jax.nn.gelu(g, approximate=True) * u, gates[p], ups[p])
        d_gate, d_up = (v.astype(LOW) for v in back(d_act))
        part = mm_t(d_gate, gate_full) + mm_t(d_up, up_full)
        d_ffn_in = part if p == 0 else d_ffn_in + swap(part.astype(LOW), "tp", p).astype(F32)
        d_gates.append(d_gate)
        d_ups.append(d_up)

    def collect_core(partial):
        low = partial.astype(LOW).reshape(F, half, partial.shape[1])
        other = swap(lax.dynamic_index_in_dim(low, f ^ 1, 0, False), "fsdp", 1)
        return lax.dynamic_index_in_dim(low, f, 0, False).astype(F32) + other.astype(F32)

    def collect_ctx(sums):
        return jnp.sum(exchange(sums.astype(LOW).reshape(C, piece, sums.shape[1]), "ctx").astype(F32), axis=0)

    def collect(partial):
        return lax.psum_scatter(collect_core(partial).astype(LOW), "ctx", scatter_dimension=0, tiled=True).astype(F32)

    all_rows = lambda parts: jnp.concatenate(parts, axis=0)
    ffn_in_all = all_rows(ffn_ins)
    grad_down = collect(t_mm(all_rows(d_outs), all_rows(acts)))
    grad_gate = collect(t_mm(ffn_in_all, all_rows(d_gates)))
    grad_up = collect(t_mm(ffn_in_all, all_rows(d_ups)))

    d_hidden_add, dg_pre_ffn = rms_back(d_ffn_in, hidden, inv_hidden, g_pre_ffn)
    d_hidden = d_result + d_hidden_add
    d_branch, dg_post_attn = rms_back(d_hidden, branch, inv_branch, g_post_attn)
    d_branch_low = d_branch.astype(LOW)
    d_attended = mm(d_branch_low, out_full).astype(LOW)
    d_query, dg_query, *d_pairs = pl.pallas_call(
        functools.partial(attend_back_kernel, heads, T),
        grid=(seqs,),
        in_specs=[specs[k] for k in ("qinfo", "kinfo", "q", "gain", "table", "table", "kv", "q", "lse", "q")],
        out_specs=[specs["q"], specs["dgain"]]
        + [pl.BlockSpec((halo + 1, 1, sub, 2 * head_width), lambda s: (0, s, 0, 0))] * T,
        out_shape=[
            jax.ShapeDtypeStruct((own, wide), LOW),
            jax.ShapeDtypeStruct((seqs, 1, head_width), F32),
        ]
        + [jax.ShapeDtypeStruct((halo + 1, seqs, sub, 2 * head_width), F32 if p == 0 else LOW) for p in range(T)],
        compiler_params=pltpu.CompilerParams(vmem_limit_bytes=32 * 1024 * 1024),
        name="attend_back",
    )(qinfo, kinfo, q_raw, g_query, cos_own, sin_own, kv_rows, q_rot, lse, d_attended)
    d_pair = d_pairs[0]
    for p in range(1, T):
        d_pair = d_pair + swap(d_pairs[p], "tp", p).astype(F32)
    d_pair_low = d_pair.astype(LOW)
    d_kv = d_pair[0]
    for d in range(1, halo + 1):
        d_kv = d_kv + shifted(d_pair_low[d], "ctx", -d).astype(F32)
    d_kv = d_kv.reshape(own, 2 * head_width)
    own_rows = lambda table: jnp.tile(table[:sub], (seqs, 1))
    e = d_kv[:, :head_width]
    e = e * own_rows(cos_all) + turn_back(e * own_rows(sin_all))
    key_own = key_raw[:own]
    d_key, dg_key = rms_back(e, key_own, inverse_rms(key_own), g_key)
    d_kv_low = jnp.concatenate([d_key.astype(LOW), d_kv[:, head_width:].astype(LOW)], axis=1)
    d_normed = mm_t(d_query, q_full) + mm_t(d_kv_low, kv_full)
    inv_x = inverse_rms(x_own)
    d_x, dg_input = rms_back(d_normed, x_own, inv_x, g_input)
    grad_input = d_hidden + d_x
    output = result.astype(LOW)

    out_sum = collect_core(t_mm(d_branch_low, attended))
    out_low = out_sum.astype(LOW)
    out_head = out_sum[:, :head_width]
    for p in range(1, T):
        out_head = out_head + swap(out_low[:, p * head_width : (p + 1) * head_width], "tp", p).astype(F32)
    grad_out = collect_ctx(out_head)
    d_query_head = all_rows(
        [d_query[:, :head_width]] + [swap(d_query[:, p * head_width : (p + 1) * head_width], "tp", p) for p in range(1, T)]
    )
    grad_qkv = collect_ctx(
        collect_core(jnp.concatenate([t_mm(normed, d_query_head), t_mm(normed_own, d_kv_low)], axis=1))
    )
    grad_query = grad_qkv[:, :head_width]
    kv_low = lax.optimization_barrier(grad_qkv[:, head_width:].astype(LOW))

    kv_sums = {p: (swap(kv_low, "tp", p) if p else kv_low).astype(F32) for p in range(T)}
    bit = 1
    while bit < T:
        kv_sums = {p: kv_sums[p] + kv_sums[p ^ bit] for p in kv_sums if not p & bit}
        bit *= 2
    grad_kv = kv_sums[0]

    sums = [jnp.sum(v, axis=0) for v in (dg_input, dg_post_attn, dg_pre_ffn, dg_post_ffn)]
    small = [jnp.sum(dg_query, axis=(0, 1)), jnp.sum(dg_key, axis=0)]
    rows = [v.reshape(F * C, piece) for v in sums] + [v.reshape(F * C, gain_piece) for v in small]
    rows = jnp.concatenate(rows + [jnp.full((F * C, 1), error)], axis=1)
    total = jnp.sum(exchange(rows, ("fsdp", "ctx")), axis=0)
    total = jnp.sum(exchange(jnp.broadcast_to(total[None], (T, total.shape[0])), "tp"), axis=0)
    loss = total[-1] / (2.0 * width_model * count)
    return (
        output.reshape(seqs, sub, width_model),
        loss,
        grad_input.reshape(seqs, sub, width_model),
        grad_query,
        grad_kv[:, :head_width],
        grad_kv[:, head_width:],
        grad_out.T,
        grad_gate,
        grad_up,
        grad_down.T,
        total[:piece],
        total[at : at + gain_piece],
        total[at + gain_piece : at + 2 * gain_piece],
        total[piece : 2 * piece],
        total[2 * piece : 3 * piece],
        total[3 * piece : 4 * piece],
    )


def solution(mesh):
    rows = P(("fsdp", "ctx"), "tp")
    cols = P("tp", ("fsdp", "ctx"))
    split = P(("fsdp", "ctx"), None)
    gain = P(("fsdp", "ctx"))
    token = P("fsdp", "ctx", None)
    own = P("fsdp", ("ctx", "tp"), None)
    weights = (rows, split, split, cols, rows, rows, cols)
    return jax.shard_map(
        shards,
        mesh=mesh,
        in_specs=(token, token, P("fsdp", "ctx")) + weights + (gain,) * 6,
        out_specs=(own, P(), own) + weights + (gain,) * 6,
        check_vma=False,
    )
```

```python
import functools
import math

import jax
import jax.numpy as jnp
from jax import lax
from jax.experimental import pallas as pl
from jax.experimental.pallas import tpu as pltpu
from jax.sharding import PartitionSpec as P

WIN = 512
EPS = 1e-06
MASKED = -1e30
LOW = jnp.bfloat16
F32 = jnp.float32


def swap(values, axis, bits):
    return lax.ppermute(values, axis, [(i, i ^ bits) for i in range(lax.axis_size(axis))])


def shifted(values, axis, by):
    size = lax.axis_size(axis)
    return lax.ppermute(values, axis, [(i, i + by) for i in range(size) if 0 <= i + by < size])


def exchange(values, axes):
    return lax.all_to_all(values, axes, 0, 0, tiled=True)


def after(value, *earlier):
    return lax.optimization_barrier((value,) + earlier)[0]


def dot(left, right, contract):
    return lax.dot_general(left, right, (contract, ((), ())), preferred_element_type=F32)


def mm(left, right):
    return dot(left, right, ((1,), (0,)))


def mm_t(left, right):
    return dot(left, right, ((1,), (1,)))


def t_mm(left, right):
    return dot(left, right, ((0,), (0,)))


def inverse_rms(values):
    return lax.rsqrt(jnp.mean(values * values, axis=-1, keepdims=True) + EPS)


def rms_back(grad, values, inverse, gain_row):
    n = values * inverse
    eg = grad * gain_row
    return inverse * (eg - n * jnp.mean(eg * n, axis=-1, keepdims=True)), grad * n


def turn(values):
    half = values.shape[-1] // 2
    return jnp.concatenate([-values[..., half:], values[..., :half]], axis=-1)


def turn_back(values):
    half = values.shape[-1] // 2
    return jnp.concatenate([values[..., half:], -values[..., :half]], axis=-1)


def rotary_tables(positions, head_width):
    frequency = 10000.0 ** (-2.0 * jnp.arange(head_width // 2, dtype=F32) / head_width)
    angles = positions.astype(F32)[:, None] * frequency[None, :]
    angles = jnp.concatenate([angles, angles], axis=-1)
    return jnp.cos(angles), jnp.sin(angles)


def heads_of(values, heads):
    width = values.shape[1] // heads
    return [values[:, h * width : (h + 1) * width] for h in range(heads)]


VMEM = pl.BlockSpec(memory_space=pltpu.VMEM)
SMEM = pl.BlockSpec(memory_space=pltpu.SMEM)
ROOM = pltpu.CompilerParams(vmem_limit_bytes=60 * 1024 * 1024)


def cost(multiply_adds, *arrays):
    moved = sum(math.prod(v.shape) * jnp.dtype(v.dtype).itemsize for v in arrays)
    return pl.CostEstimate(flops=2 * multiply_adds, bytes_accessed=moved, transcendentals=0)


def struct(shape, dtype):
    return jax.ShapeDtypeStruct(shape, dtype)


def column_sum(values):
    return jnp.sum(values, axis=0, keepdims=True)


def assemble_kernel(pieces, core_ref, *refs):
    width = refs[0].shape[1] // 2
    results = refs[2 * pieces :]
    for step in range(2):

        @pl.when(pl.program_id(0) == step)
        def _():
            for i, result in enumerate(results):
                for p in range(pieces):
                    result[0, :, p * width : (p + 1) * width] = refs[step * pieces + p][:, i * width : (i + 1) * width]


def assemble(core, mine, others):
    half, width = mine[0].shape
    pieces = len(mine)
    wide = pieces * width // 2
    out = pl.BlockSpec((1, half, wide), lambda i, core: (i ^ core[0], 0, 0))
    results = pl.pallas_call(
        functools.partial(assemble_kernel, pieces),
        grid_spec=pltpu.PrefetchScalarGridSpec(
            num_scalar_prefetch=1,
            grid=(2,),
            in_specs=[pl.BlockSpec((half, width), lambda i, core: (0, 0))] * (2 * pieces),
            out_specs=[out, out],
        ),
        out_shape=[struct((2, half, wide), LOW)] * 2,
        compiler_params=ROOM,
        cost_estimate=cost(0, *mine, *others, *mine, *others),
        name="assemble",
    )(core.reshape(1), *mine, *others)
    return [v.reshape(2 * half, wide) for v in results]


def norm_rows_kernel(chunks, place_ref, x_ref, gain_ref, out_ref):
    sub = x_ref.shape[1] // chunks
    for p in range(chunks):
        x = x_ref[0, pl.ds(pl.multiple_of((place_ref[0] ^ p) * sub, sub), sub), :].astype(F32)
        out_ref[p, 0] = (x * inverse_rms(x) * gain_ref[...]).astype(LOW)


def norm_rows(place, x, gain_row, chunks):
    seqs, rows, width = x.shape
    sub = rows // chunks
    return pl.pallas_call(
        functools.partial(norm_rows_kernel, chunks),
        grid=(seqs,),
        in_specs=[
            pl.BlockSpec(memory_space=pltpu.SMEM),
            pl.BlockSpec((1, rows, width), lambda s: (s, 0, 0)),
            pl.BlockSpec((1, width), lambda s: (0, 0)),
        ],
        out_specs=pl.BlockSpec((chunks, 1, sub, width), lambda s: (0, s, 0, 0)),
        out_shape=jax.ShapeDtypeStruct((chunks, seqs, sub, width), LOW),
        compiler_params=ROOM,
        cost_estimate=cost(0, x, x, x, x),
        name="norm_rows",
    )(place.reshape(1), x, gain_row).reshape(chunks * seqs * sub, width)


def keys_kernel(core_ref, x_ref, near_ref, far_ref, gain_ref, cos_ref, sin_ref, pair_ref, first_ref, raw_ref, full_ref):
    chunks, _, sub, width = x_ref.shape
    half = near_ref.shape[0]
    head = gain_ref.shape[1]

    @pl.when(pl.program_id(0) == 0)
    def _():
        for place, source in ((core_ref[0], near_ref), (1 - core_ref[0], far_ref)):
            full_ref[pl.ds(pl.multiple_of(place * half, half), half), :] = source[...]

    kv = mm(x_ref[...].reshape(chunks * sub, width), full_ref[...])
    key = kv[:, :head]
    n = key * inverse_rms(key) * gain_ref[...]
    rot = (n * cos_ref[...] + turn(n) * sin_ref[...]).astype(LOW)
    value = kv[:, head:].astype(LOW)
    raw_ref[...] = key[:sub]
    pair_ref[:, 0, :, :head] = rot.reshape(chunks, sub, head)
    pair_ref[:, 0, :, head:] = value.reshape(chunks, sub, head)
    first_ref[0, :, :head] = rot[:sub]
    first_ref[0, :, head:] = value[:sub]


def project_keys(core, normed, near, far, gain_row, cos, sin):
    chunks, seqs, sub, width = normed.shape
    half, both = near.shape
    head = both // 2
    whole = lambda *shape: pl.BlockSpec(shape, lambda s: (0,) * len(shape))
    return pl.pallas_call(
        keys_kernel,
        grid=(seqs,),
        in_specs=[
            SMEM,
            pl.BlockSpec((chunks, 1, sub, width), lambda s: (0, s, 0, 0)),
            whole(half, both),
            whole(half, both),
            whole(1, head),
            whole(chunks * sub, head),
            whole(chunks * sub, head),
        ],
        out_specs=[
            pl.BlockSpec((chunks, 1, sub, both), lambda s: (0, s, 0, 0)),
            pl.BlockSpec((1, sub, both), lambda s: (s, 0, 0)),
            pl.BlockSpec((sub, head), lambda s: (s, 0)),
            whole(2 * half, both),
        ],
        out_shape=[
            struct((chunks, seqs, sub, both), LOW),
            struct((seqs, sub, both), LOW),
            struct((seqs * sub, head), F32),
            struct((2 * half, both), LOW),
        ],
        compiler_params=ROOM,
        cost_estimate=cost(seqs * chunks * sub * width * both, normed, normed),
        name="project_keys",
    )(core.reshape(1), normed, near, far, gain_row, cos, sin)


def mask_of(qinfo_ref, kinfo_ref):
    qpos, qseg = qinfo_ref[0, :, 0:1], qinfo_ref[0, :, 1:2]
    kpos, kseg = kinfo_ref[0, 0:1, :], kinfo_ref[0, 1:2, :]
    return (kseg == qseg) & (kpos <= qpos) & (kpos > qpos - WIN)


def key_rows(kv_refs, width):
    own_ref, *far_refs = kv_refs
    sides = []
    for at in (0, width):
        own = own_ref[:, 0, :, at : at + width].reshape(own_ref.shape[0] * own_ref.shape[2], width)
        sides.append(jnp.concatenate([own] + [r[0, :, at : at + width] for r in far_refs], axis=0))
    return sides


def attend_kernel(heads, qinfo_ref, kinfo_ref, q_ref, gain_ref, cos_ref, sin_ref, *refs):
    kv_refs, (rot_ref, out_ref, lse_ref) = refs[:-3], refs[-3:]
    width = q_ref.shape[1] // heads
    scale = width ** (-0.5)
    rotated = []
    for h, q in enumerate(heads_of(q_ref[...], heads)):
        n = q * inverse_rms(q) * gain_ref[...]
        rot = ((n * cos_ref[...] + turn(n) * sin_ref[...]) * scale).astype(LOW)
        rot_ref[:, h * width : (h + 1) * width] = rot
        rotated.append(rot)
    rows = jnp.concatenate(rotated, axis=0)
    keys, vals = key_rows(kv_refs, width)
    bias = jnp.where(mask_of(qinfo_ref, kinfo_ref), 0.0, MASKED)
    allowed = jnp.concatenate([bias] * heads, axis=0) == 0.0
    scores = jnp.where(allowed, mm_t(rows, keys), MASKED)
    top = jnp.max(scores, axis=1, keepdims=True)
    expos = jnp.exp(scores - top)
    total = jnp.sum(expos, axis=1, keepdims=True)
    lse_ref[0] = top + jnp.log(total)
    probs = (expos / total).astype(LOW)
    attended = mm(probs, vals).astype(LOW)
    count = q_ref.shape[0]
    for h in range(heads):
        out_ref[:, h * width : (h + 1) * width] = attended[h * count : (h + 1) * count]


def attend_back_kernel(heads, chunks, blocks, place_ref, qinfo_ref, kinfo_ref, q_ref, gain_ref, cos_ref, sin_ref, rot_ref, lse_ref,
                       dout_ref, *refs):
    far_count = (blocks - 1) * chunks
    kv_refs, (dq_ref, dgain_ref), dkv_refs = refs[: far_count + 1], refs[far_count + 1 : far_count + 3], refs[far_count + 3 :]
    width = q_ref.shape[1] // heads
    scale = width ** (-0.5)
    count = q_ref.shape[0]
    rows = jnp.concatenate(heads_of(rot_ref[...], heads), axis=0)
    douts = jnp.concatenate(heads_of(dout_ref[...], heads), axis=0)
    keys, vals = key_rows(kv_refs, width)
    bias = jnp.where(mask_of(qinfo_ref, kinfo_ref), 0.0, MASKED)
    allowed = jnp.concatenate([bias] * heads, axis=0) == 0.0
    probs = jnp.where(allowed, jnp.exp(mm_t(rows, keys) - lse_ref[0]), 0.0)
    d_probs = mm_t(douts, vals)
    delta = jnp.sum(probs * d_probs, axis=1, keepdims=True)
    d_scores = (probs * (d_probs - delta)).astype(LOW)
    d_rows = mm(d_scores, keys)
    d_keys = t_mm(d_scores, rows)
    d_vals = t_mm(probs.astype(LOW), douts)
    per = kv_refs[0].shape[2]
    for part, at in ((d_keys, 0), (d_vals, width)):
        piece = lambda b, p: part[(b * chunks + p) * per : (b * chunks + p + 1) * per]
        for b in range(blocks):
            dkv_refs[0][b, 0, :, at : at + width] = piece(b, 0)
        for p in range(1, chunks):
            earlier = (place_ref[0] ^ p) < place_ref[0]
            for b in range(1, blocks - 1):
                dkv_refs[p][b - 1, 0, :, at : at + width] = piece(b, p).astype(LOW)
            dkv_refs[p][blocks - 2, 0, :, at : at + width] = jnp.where(earlier, piece(0, p), piece(blocks - 1, p)).astype(LOW)
    gain_sum = jnp.zeros((1, width), F32)
    for h, q in enumerate(heads_of(q_ref[...], heads)):
        e = d_rows[h * count : (h + 1) * count] * scale
        e = e * cos_ref[...] + turn_back(e * sin_ref[...])
        d_q, d_g = rms_back(e, q, inverse_rms(q), gain_ref[...])
        gain_sum = gain_sum + column_sum(d_g)
        dq_ref[:, h * width : (h + 1) * width] = d_q.astype(LOW)
    dgain_ref[0] = gain_sum


def pair_sum_kernel(*refs):
    out = refs[-1]
    for i in range(out.shape[0]):
        out[i] = (refs[2 * i][...].astype(F32) + refs[2 * i + 1][...].astype(F32)).astype(LOW)


def pair_sum(*pairs):
    rows, width = pairs[0][0].shape
    step = rows // 4 if rows % 64 == 0 else rows
    arrays = [v for pair in pairs for v in pair]
    return pl.pallas_call(
        pair_sum_kernel,
        grid=(rows // step,),
        in_specs=[pl.BlockSpec((step, width), lambda j: (j, 0))] * len(arrays),
        out_specs=pl.BlockSpec((len(pairs), step, width), lambda j: (0, j, 0)),
        out_shape=struct((len(pairs), rows, width), LOW),
        compiler_params=ROOM,
        name="pair_sum",
    )(*arrays)


def attention_specs(seqs, rows, spans, chunks, wide, width):
    whole = lambda *shape: pl.BlockSpec(shape, lambda s: (0,) * len(shape))
    return dict(
        qinfo=pl.BlockSpec((1, rows, 2), lambda s: (s, 0, 0)),
        kinfo=pl.BlockSpec((1, 2, spans), lambda s: (s, 0, 0)),
        q=pl.BlockSpec((rows, wide), lambda s: (s, 0)),
        gain=whole(1, width),
        table=whole(rows, width),
        own=pl.BlockSpec((chunks, 1, rows, 2 * width), lambda s: (0, s, 0, 0)),
        far=pl.BlockSpec((1, rows, 2 * width), lambda s: (s, 0, 0)),
        lse=pl.BlockSpec((1, rows * (wide // width), 1), lambda s: (s, 0, 0)),
        dgain=pl.BlockSpec((1, 1, width), lambda s: (s, 0, 0)),
    )


def mix_kernel(att_ref, out_ref, x_ref, gain_attn_ref, gain_ffn_ref, branch_ref, hidden_ref, ffn_ref):
    branch = mm_t(att_ref[...], out_ref[...])
    branch_ref[...] = branch
    hidden = x_ref[...].astype(F32) + branch * inverse_rms(branch) * gain_attn_ref[...]
    hidden_ref[...] = hidden
    ffn_ref[...] = (hidden * inverse_rms(hidden) * gain_ffn_ref[...]).astype(LOW)


def for_blocks(width, step, block):
    full, rest = divmod(width, step)

    @pl.when(pl.program_id(0) < full)
    def _():
        block(step)

    if rest:

        @pl.when(pl.program_id(0) == full)
        def _():
            block(rest)


def ffn_kernel(units, chunks, *refs):
    rows_refs, (gate_ref, up_ref, down_ref) = refs[:chunks], refs[chunks : chunks + 3]
    part_refs, (act_ref, slope_ref, curve_ref, sums) = refs[chunks + 3 : 2 * chunks + 3], refs[2 * chunks + 3 :]

    @pl.when(pl.program_id(0) == 0)
    def _():
        sums[...] = jnp.zeros_like(sums)

    def block(size):
        rows = jnp.concatenate([r[...] for r in rows_refs], axis=0)
        gate, up = mm(rows, gate_ref[0, :, :size]), mm(rows, up_ref[0, :, :size])
        root = (2.0 / math.pi) ** 0.5
        square = gate * gate
        bend = jnp.tanh(root * (gate + 0.044715 * (square * gate)))
        share = 0.5 * (1.0 + bend)
        curve = gate * share
        slope = share + 0.5 * gate * (1.0 - bend * bend) * (root * (1.0 + 3.0 * 0.044715 * square))
        act = (curve * up).astype(LOW)
        act_ref[:, :size] = act
        slope_ref[:, :size] = (slope * up).astype(LOW)
        curve_ref[:, :size] = curve.astype(LOW)
        sums[...] += mm_t(act, down_ref[0, :, :size])

    for_blocks(units, act_ref.shape[1], block)
    split_rows(sums, part_refs)


def split_rows(sums, part_refs):
    @pl.when(pl.program_id(0) == pl.num_programs(0) - 1)
    def _():
        count = part_refs[0].shape[0]
        for p, part in enumerate(part_refs):
            part[...] = sums[p * count : (p + 1) * count].astype(part.dtype)


def ffn_back_kernel(units, chunks, *refs):
    rows_refs, (gate_ref, up_ref, down_ref, slope_ref, curve_ref) = refs[:chunks], refs[chunks : chunks + 5]
    part_refs, (dgate_ref, dup_ref, sums) = refs[chunks + 5 : 2 * chunks + 5], refs[2 * chunks + 5 :]

    @pl.when(pl.program_id(0) == 0)
    def _():
        sums[...] = jnp.zeros_like(sums)

    def block(size):
        rows = jnp.concatenate([r[...] for r in rows_refs], axis=0)
        d_act = mm(rows, down_ref[0, :, :size])
        d_gate = (d_act * slope_ref[:, :size].astype(F32)).astype(LOW)
        d_up = (d_act * curve_ref[:, :size].astype(F32)).astype(LOW)
        dgate_ref[:, :size] = d_gate
        dup_ref[:, :size] = d_up
        sums[...] += mm_t(d_gate, gate_ref[0, :, :size]) + mm_t(d_up, up_ref[0, :, :size])

    for_blocks(units, dgate_ref.shape[1], block)
    split_rows(sums, part_refs)


def ffn_call(kernel, name, rows, weights, saved, results, dtype, step=640):
    chunks = len(rows)
    count, width = rows[0].shape
    units = weights.shape[2]
    whole = pl.BlockSpec((count, width), lambda j: (0, 0))
    strip = pl.BlockSpec((chunks * count, step), lambda j: (0, j))
    flat = pl.pallas_call(
        functools.partial(kernel, units, chunks),
        grid=(pl.cdiv(units, step),),
        in_specs=[whole] * chunks
        + [pl.BlockSpec((1, width, step), lambda j, i=i: (i, 0, j)) for i in range(3)]
        + [strip] * len(saved),
        out_specs=[whole] * chunks + [strip] * results,
        out_shape=[struct((count, width), dtype)] * chunks + [struct((chunks * count, units), LOW)] * results,
        scratch_shapes=[pltpu.VMEM((chunks * count, width), F32)],
        compiler_params=ROOM,
        cost_estimate=cost(3 * chunks * count * width * units, *rows, weights, *saved),
        name=name,
    )(*rows, weights, weights, weights, *saved)
    return flat[:chunks], flat[chunks:]


def loss_kernel(factor_ref, hidden_ref, target_ref, valid_ref, gain_ref, *refs):
    parts, (out_ref, dres_ref, dffn_ref, dgain_ref, error_ref) = refs[:-5], refs[-5:]
    ffn = sum(r[...].astype(F32) for r in parts)
    inverse = inverse_rms(ffn)
    result = hidden_ref[...] + ffn * inverse * gain_ref[...]
    out_ref[...] = result.astype(LOW)
    mismatch = result - target_ref[...].astype(F32)
    marked = valid_ref[...] * mismatch
    error_ref[...] = jnp.broadcast_to(column_sum(jnp.sum(marked * mismatch, axis=1, keepdims=True)), error_ref.shape)
    d_result = factor_ref[0] * marked
    dres_ref[...] = d_result
    d_ffn, d_gain = rms_back(d_result, ffn, inverse, gain_ref[...])
    dffn_ref[...] = d_ffn.astype(LOW)
    dgain_ref[...] = column_sum(d_gain)


def middle_kernel(dres_ref, hidden_ref, branch_ref, out_ref, gain_ffn_ref, gain_attn_ref, *refs):
    parts, (dhid_ref, dbranch_ref, datt_ref, dgain_ffn_ref, dgain_attn_ref) = refs[:-5], refs[-5:]
    d_ffn_in = sum(r[...].astype(F32) for r in parts)
    hidden = hidden_ref[...]
    d_add, d_gain = rms_back(d_ffn_in, hidden, inverse_rms(hidden), gain_ffn_ref[...])
    dgain_ffn_ref[...] = column_sum(d_gain)
    d_hidden = dres_ref[...] + d_add
    dhid_ref[...] = d_hidden
    branch = branch_ref[...]
    d_branch, d_gain = rms_back(d_hidden, branch, inverse_rms(branch), gain_attn_ref[...])
    dgain_attn_ref[...] = column_sum(d_gain)
    low = d_branch.astype(LOW)
    dbranch_ref[...] = low
    datt_ref[...] = mm(low, out_ref[...]).astype(LOW)


def finish_kernel(core_ref, raw_ref, cos_ref, sin_ref, gain_key_ref, dq_ref, q_ref, kv_ref, dhid_ref, x_ref, gain_ref, normed_ref, *refs):
    parts, (din_ref, dgain_ref, dgain_key_ref, send_ref, own_ref, sums) = refs[:-6], refs[-6:]
    head = raw_ref.shape[1]
    d_kv = sum(r[...].astype(F32) for r in parts)
    key = raw_ref[...]
    e = d_kv[:, :head]
    e = e * cos_ref[...] + turn_back(e * sin_ref[...])
    d_key, d_gain = rms_back(e, key, inverse_rms(key), gain_key_ref[...])
    dgain_key_ref[...] = column_sum(d_gain)
    low = jnp.concatenate([d_key.astype(LOW), d_kv[:, head:].astype(LOW)], axis=1)
    sums[...] = mm(normed_ref[...].T, low)
    half = own_ref.shape[0]
    core = core_ref[0]
    own_ref[...] = sums[pl.ds(pl.multiple_of(core * half, half), half), :].astype(LOW)
    send_ref[...] = sums[pl.ds(pl.multiple_of((1 - core) * half, half), half), :].astype(LOW)
    d_normed = mm_t(dq_ref[...], q_ref[...]) + mm_t(low, kv_ref[...])
    x = x_ref[...].astype(F32)
    d_x, d_gain = rms_back(d_normed, x, inverse_rms(x), gain_ref[...])
    dgain_ref[...] = column_sum(d_gain)
    din_ref[...] = dhid_ref[...] + d_x


def weight_grad_kernel(chunks, sets, core_ref, *refs):
    lefts, refs = refs[:chunks], refs[chunks:]
    rights, refs = refs[: chunks * sets], refs[chunks * sets :]
    outs, (turned, sums) = refs[: 2 * sets], refs[2 * sets :]
    rows = lefts[0].shape[0]
    half = outs[0].shape[0]

    @pl.when(pl.program_id(0) == 0)
    def _():
        for p in range(chunks):
            turned[:, p * rows : (p + 1) * rows] = lefts[p][...].T

    core = core_ref[0]
    for i in range(sets):
        right = jnp.concatenate([r[...] for r in rights[i * chunks : (i + 1) * chunks]], axis=0)
        sums[i] = mm(turned[...], right)
        for place, out in ((1 - core, outs[2 * i]), (core, outs[2 * i + 1])):
            out[...] = sums[i, pl.ds(pl.multiple_of(place * half, half), half), :].astype(LOW)


def weight_grad(core, rows, lefts, *rights, step=256):
    chunks, sets = len(lefts), len(rights)
    height = lefts[0][0].shape[1]
    width = rights[0][0][0].shape[1]
    rights = [pair for group in rights for pair in group]
    out = pl.BlockSpec((height // 2, step), lambda j: (0, j))
    flat = pl.pallas_call(
        functools.partial(weight_grad_kernel, chunks, sets),
        grid=(pl.cdiv(width, step),),
        in_specs=[SMEM]
        + [pl.BlockSpec((rows, height), lambda j, at=at: (at, 0)) for _, at in lefts]
        + [pl.BlockSpec((rows, step), lambda j, at=at: (at, j)) for _, at in rights],
        out_specs=[out] * (2 * sets),
        out_shape=[struct((height // 2, width), LOW)] * (2 * sets),
        scratch_shapes=[pltpu.VMEM((height, chunks * rows), LOW), pltpu.VMEM((sets, height, step), F32)],
        compiler_params=ROOM,
        cost_estimate=cost(sets * chunks * rows * height * width, *[v for v, _ in lefts], struct((height, sets * width), LOW)),
        name="weight_grad",
    )(core.reshape(1), *[v for v, _ in lefts], *[v for v, _ in rights])
    return [flat[2 * i : 2 * i + 2] for i in range(sets)]


def shards(inputs, target, segment_ids, w_query, w_key, w_value, w_out, w_gate, w_up, w_down,
           gain_input, gain_query, gain_key, gain_post_attn, gain_pre_ffn, gain_post_ffn):
    F, C, T = (lax.axis_size(a) for a in ("fsdp", "ctx", "tp"))
    f, z, t = (lax.axis_index(a) for a in ("fsdp", "ctx", "tp"))
    me = f * C + z
    seqs, block_rows, width_model = inputs.shape
    piece = w_query.shape[0]
    head_width = w_key.shape[1]
    gain_piece = gain_query.shape[0]
    sub = block_rows // T
    own = seqs * sub
    half = C * piece
    halo = -(-(WIN - 1) // block_rows)
    spans = (halo + 1) * block_rows

    both = 2 * head_width
    blocks = jnp.stack([jnp.concatenate([w_query, w_out.T], axis=1), jnp.concatenate([w_key, w_value], axis=1)])
    near = lax.all_gather(blocks, "ctx", axis=1, tiled=True)
    weights = lax.all_gather(jnp.stack([w_gate, w_up, w_down.T]), ("fsdp", "ctx"), axis=1, tiled=True)
    packed = jnp.concatenate(
        [gain_input, gain_post_attn, gain_pre_ffn, gain_post_ffn, gain_query, gain_key, segment_ids.astype(LOW).reshape(-1)]
    )
    packed = exchange(jnp.broadcast_to(packed[None], (F * C, packed.shape[0])), ("fsdp", "ctx")).astype(F32)
    at = 4 * piece
    g_input, g_post_attn, g_pre_ffn, g_post_ffn = [
        packed[:, i * piece : (i + 1) * piece].reshape(1, width_model) for i in range(4)
    ]
    g_query, g_key = [
        packed[:, at + i * gain_piece : at + (i + 1) * gain_piece].reshape(1, head_width) for i in range(2)
    ]
    seg_blocks = packed[:, at + 2 * gain_piece :].astype(jnp.int32)
    count = jnp.sum((seg_blocks != 0).astype(F32))
    normed = norm_rows(t, inputs, g_input, T)
    def sub_rows(values):
        return [lax.dynamic_slice_in_dim(values, (t ^ p) * sub, sub, 1) for p in range(T)]

    x_own = lax.dynamic_slice_in_dim(inputs, t * sub, sub, 1).reshape(own, width_model)
    target_own = lax.dynamic_slice_in_dim(target, t * sub, sub, 1).reshape(own, width_model)
    positions = jnp.concatenate([z * block_rows + (t ^ p) * sub + jnp.arange(sub, dtype=jnp.int32) for p in range(T)])
    segs = [segment_ids + 1]
    for d in range(1, halo + 1):
        far = lax.dynamic_index_in_dim(seg_blocks, jnp.maximum(me - d, 0), 0, False).reshape(seqs, block_rows)
        segs.append(jnp.where(z >= d, far + 1, 0))
    key_seg = jnp.concatenate([v for seg in segs for v in sub_rows(seg)], axis=1)
    key_pos = jnp.concatenate([positions - d * block_rows for d in range(halo + 1)])
    kinfo = jnp.stack([jnp.broadcast_to(key_pos, (seqs, spans)), key_seg], axis=1)
    qinfo = jnp.stack([jnp.broadcast_to(positions[:sub], (seqs, sub)), key_seg[:, :sub]], axis=2)
    valid_own = (key_seg[:, :sub] != 1).astype(F32).reshape(own, 1)
    cos_all, sin_all = rotary_tables(positions, head_width)
    cos_own, sin_own = cos_all[:sub], sin_all[:sub]

    ready = (normed, kinfo, qinfo, cos_all, sin_all, cos_own, sin_own, g_query, g_key, g_post_attn, g_pre_ffn, x_own)
    (near, *ready) = lax.optimization_barrier((near,) + ready)
    normed, kinfo, qinfo, cos_all, sin_all, cos_own, sin_own, g_query, g_key, g_post_attn, g_pre_ffn, x_own = ready
    near_qo, near_kv = near
    far_kv = swap(near_kv, "fsdp", 1)
    near_qo = [near_qo] + [swap(near_qo, "tp", p) for p in range(1, T)]
    pair, first, key_own, kv_full = project_keys(f, normed.reshape(T, seqs, sub, width_model), near_kv, far_kv, g_key, cos_all, sin_all)
    q_full, out_full = assemble(f, near_qo, [swap(after(v, first), "fsdp", 1) for v in near_qo])
    kv_rows, far = [pair], first
    for d in range(halo):
        far = shifted(far, "ctx", 1)
        kv_rows += [swap(far, "tp", p) if p else far for p in range(T)]
    normed_own = normed[:own]
    q_raw = mm(normed_own, q_full)
    wide = q_raw.shape[1]
    heads = wide // head_width
    specs = attention_specs(seqs, sub, spans, T, wide, head_width)
    kv_specs = [specs["own"]] + [specs["far"]] * (halo * T)
    q_rot, attended, lse = pl.pallas_call(
        functools.partial(attend_kernel, heads),
        grid=(seqs,),
        in_specs=[specs[k] for k in ("qinfo", "kinfo", "q", "gain", "table", "table")] + kv_specs,
        out_specs=[specs["q"], specs["q"], specs["lse"]],
        out_shape=[struct((own, wide), LOW), struct((own, wide), LOW), struct((seqs, sub * heads, 1), F32)],
        compiler_params=ROOM,
        cost_estimate=cost(4 * own * spans * wide // seqs, *kv_rows, q_raw),
        name="attend",
    )(qinfo, kinfo, q_raw, g_query, cos_own, sin_own, *kv_rows)
    token = struct((own, width_model), F32)
    token_low = struct((own, width_model), LOW)
    gain_row = struct((1, width_model), F32)
    branch, hidden, ffn_in = pl.pallas_call(
        mix_kernel, out_shape=[token, token, token_low], compiler_params=ROOM, cost_estimate=cost(own * wide * width_model, out_full, out_full), name="mix"
    )(attended, out_full, x_own, g_post_attn, g_pre_ffn)

    from_tp = lambda parts: parts[:1] + [swap(v, "tp", p) for p, v in enumerate(parts) if p]
    ffn_ins = from_tp([ffn_in] * T)
    groups = [[0], [1], list(range(2, T))]
    place = {p: (g, i) for g, group in enumerate(groups) for i, p in enumerate(group)}
    done = [ffn_call(ffn_kernel, "ffn", [ffn_ins[p] for p in group], weights, (), 3, LOW if g else F32) for g, group in enumerate(groups)]
    parts = [done[place[p][0]][0][place[p][1]] for p in range(T)]
    acts, slopes, curves = zip(*[results for _, results in done])
    acts = [(acts[place[p][0]], place[p][1]) for p in range(T)]
    all_tokens = seqs * block_rows * F * C
    output, d_result, d_ffn_low, dg_post_ffn, error = pl.pallas_call(
        loss_kernel,
        in_specs=[SMEM] + [VMEM] * (4 + T),
        out_shape=[token_low, token, token_low, gain_row, struct((1, 128), F32)],
        compiler_params=ROOM,
        cost_estimate=cost(own, *parts, *parts),
        name="loss",
    )((all_tokens / count).reshape(1), hidden, target_own, valid_own, g_post_ffn, *from_tp(parts))

    def collect_core(send, mine, *earlier):
        other = swap(send, "fsdp", 1)
        return mine.astype(F32) + (after(other, *earlier) if earlier else other).astype(F32)

    def scatter_ctx(sums):
        return lax.psum_scatter(sums, "ctx", scatter_dimension=1, tiled=True).astype(F32)

    d_outs = from_tp([d_ffn_low] * T)
    done = []
    for g, group in enumerate(groups):
        rows = [d_outs[p] for p in group]
        if g == 1:
            rows[0] = after(rows[0], done[0][0][0])
        if g == 2:
            (down_halves,) = weight_grad(f, own, [(after(v, done[1][0][0]) if p == 2 else v, 0) for p, v in enumerate(d_outs)], acts)
            down_sum = pair_sum((down_halves[1], swap(down_halves[0], "fsdp", 1)))
            rows[0] = after(rows[0], down_sum)
        done.append(ffn_call(ffn_back_kernel, "ffn_back", rows, weights, (slopes[g], curves[g]), 2, LOW if g else F32))
    (grad_down,) = scatter_ctx(down_sum)
    parts = [done[place[p][0]][0][place[p][1]] for p in range(T)]
    d_gates, d_ups = [[(done[place[p][0]][1][i], place[p][1]) for p in range(T)] for i in range(2)]
    first_in = after(ffn_ins[0], parts[-1])
    gate_halves, up_halves = weight_grad(f, own, [(v, 0) for v in [first_in] + ffn_ins[1:]], d_gates, d_ups)

    parts = [after(v, *gate_halves, *up_halves) if p == 0 else v for p, v in enumerate(from_tp(parts))]
    d_hidden, d_branch, d_attended, dg_pre_ffn, dg_post_attn = pl.pallas_call(
        middle_kernel,
        out_shape=[token, token_low, struct((own, wide), LOW), gain_row, gain_row],
        compiler_params=ROOM,
        name="middle",
    )(d_result, hidden, branch, out_full, g_pre_ffn, g_post_attn, *parts)
    assert halo * block_rows == WIN
    others = [after(swap(after(v[0], *parts[1:]), "fsdp", 1), d_branch) for v in (gate_halves, up_halves)]
    both_sums = pair_sum((gate_halves[1], others[0]), (up_halves[1], others[1]))
    grad_gate, grad_up = scatter_ctx(both_sums)
    d_attended = after(d_attended, both_sums)
    (out_halves,) = weight_grad(f, own, [(d_branch, 0)], [(attended, 0)])
    out_sum = collect_core(*out_halves)
    out_low = out_sum.astype(LOW)
    d_query, dg_query, *d_pairs = pl.pallas_call(
        functools.partial(attend_back_kernel, heads, T, halo + 1),
        grid=(seqs,),
        in_specs=[SMEM] + [specs[k] for k in ("qinfo", "kinfo", "q", "gain", "table", "table", "q", "lse", "q")] + kv_specs,
        out_specs=[specs["q"], specs["dgain"]]
        + [pl.BlockSpec((halo + (p == 0), 1, sub, 2 * head_width), lambda s: (0, s, 0, 0)) for p in range(T)],
        out_shape=[struct((own, wide), LOW), struct((seqs, 1, head_width), F32)]
        + [struct((halo + (p == 0), seqs, sub, 2 * head_width), F32 if p == 0 else LOW) for p in range(T)],
        compiler_params=ROOM,
        name="attend_back",
    )(t.reshape(1), qinfo, kinfo, q_raw, g_query, cos_own, sin_own, q_rot, lse, d_attended, *kv_rows)
    d_blocks = [d_pairs[0][b] for b in range(halo + 1)]
    for p in range(1, T):
        got = after(swap(d_pairs[p], "tp", p), out_low).astype(F32)
        for b in range(1, halo):
            d_blocks[b] = d_blocks[b] + got[b - 1]
        later = (t ^ p) > t
        d_blocks[0] = d_blocks[0] + jnp.where(later, got[halo - 1], 0.0)
        d_blocks[halo] = d_blocks[halo] + jnp.where(later, 0.0, got[halo - 1])
    d_kv = d_blocks[halo]
    for d in range(halo, 0, -1):
        come = shifted(d_kv.astype(LOW), "ctx", -1)
        if d == halo:
            d_query_late, out_low = after(d_query, come), after(out_low, come)
        if d > 1:
            d_kv = d_blocks[d - 1] + come.astype(F32)
    d_kv = [d_blocks[0], come]
    out_head = out_sum[:, :head_width]
    for p in range(1, T):
        out_head = out_head + swap(out_low[:, p * head_width : (p + 1) * head_width], "tp", p).astype(F32)
    head_of = lambda p: d_query_late[:, p * head_width : (p + 1) * head_width]
    normed_late = after(normed, d_kv[1])
    (q_halves,) = weight_grad(
        f, own, [(normed_late, p) for p in range(T)], [(swap(head_of(p), "tp", p) if p else head_of(p), 0) for p in range(T)]
    )
    out_low = out_head.astype(LOW)
    d_kv[0] = after(d_kv[0], *q_halves, out_low)
    own_rows = lambda table: jnp.tile(table, (seqs, 1))
    grad_input, dg_input, dg_key, *kv_halves = pl.pallas_call(
        finish_kernel,
        in_specs=[SMEM] + [VMEM] * (11 + len(d_kv)),
        out_shape=[token, gain_row, struct((1, head_width), F32)] + [struct((half, 2 * head_width), LOW)] * 2,
        scratch_shapes=[pltpu.VMEM((2 * half, 2 * head_width), F32)],
        compiler_params=ROOM,
        name="finish",
    )(f.reshape(1), key_own, own_rows(cos_own), own_rows(sin_own), g_key, d_query, q_full, kv_full, d_hidden, x_own, g_input,
      normed_own, *[v.reshape(own, 2 * head_width) for v in d_kv])

    def pack(values, wide):
        top = lax.reduce_precision(values, 8, 7)
        flat = jnp.concatenate([top, values - top], axis=1).astype(LOW)
        rows = -(-flat.shape[1] // wide)
        return jnp.pad(flat, ((0, 0), (0, rows * wide - flat.shape[1]))).reshape(values.shape[0], rows, wide)

    def unpack(rows, n):
        flat = rows.reshape(-1)
        return flat[:n] + flat[n : 2 * n]

    sums = [dg_input, dg_post_attn, dg_pre_ffn, dg_post_ffn]
    small = [jnp.sum(dg_query, axis=(0, 1)), dg_key]
    extra = [v.reshape(F * C, piece) for v in sums] + [v.reshape(F * C, gain_piece) for v in small]
    extra = jnp.concatenate(extra + [jnp.broadcast_to(error[:, :1], (F * C, 1))], axis=1).reshape(F, C, -1)
    n = extra.shape[2]
    extra = lax.dynamic_index_in_dim(extra, f, 0, False) + swap(lax.dynamic_index_in_dim(extra, f ^ 1, 0, False), "fsdp", 1)
    q_low = collect_core(after(q_halves[0], dg_key), q_halves[1]).astype(LOW)
    grads = jnp.concatenate([q_low, out_low, collect_core(*kv_halves).astype(LOW)], axis=1)
    grads = jnp.concatenate([grads.reshape(C, piece, grads.shape[1]), pack(extra, grads.shape[1])], axis=1)
    grads = jnp.sum(exchange(grads, "ctx").astype(F32), axis=0)
    grad_query, grad_out = grads[:piece, :head_width], grads[:piece, head_width : 2 * head_width]
    kv_low = grads[:piece, 2 * head_width :]
    kv_low = jnp.concatenate([kv_low.astype(LOW), pack(unpack(grads[piece:], n)[None], kv_low.shape[1])[0]], axis=0)
    kv_low = lax.optimization_barrier(kv_low)
    totals = {p: (swap(kv_low, "tp", p) if p else kv_low).astype(F32) for p in range(T)}
    bit = 1
    while bit < T:
        totals = {p: totals[p] + totals[p ^ bit] for p in totals if not p & bit}
        bit *= 2
    grad_kv, total = totals[0][:piece], unpack(totals[0][piece:], n)
    loss = total[-1] / (2.0 * width_model * count)
    at = 4 * piece
    return (
        output.reshape(seqs, sub, width_model),
        loss,
        grad_input.reshape(seqs, sub, width_model),
        grad_query,
        grad_kv[:, :head_width],
        grad_kv[:, head_width:],
        grad_out.T,
        grad_gate,
        grad_up,
        grad_down.T,
        total[:piece],
        total[at : at + gain_piece],
        total[at + gain_piece : at + 2 * gain_piece],
        total[piece : 2 * piece],
        total[2 * piece : 3 * piece],
        total[3 * piece : 4 * piece],
    )


def solution(mesh):
    rows = P(("fsdp", "ctx"), "tp")
    cols = P("tp", ("fsdp", "ctx"))
    split = P(("fsdp", "ctx"), None)
    gain = P(("fsdp", "ctx"))
    token = P("fsdp", "ctx", None)
    own = P("fsdp", ("ctx", "tp"), None)
    weights = (rows, split, split, cols, rows, rows, cols)
    return jax.shard_map(
        shards,
        mesh=mesh,
        in_specs=(token, token, P("fsdp", "ctx")) + weights + (gain,) * 6,
        out_specs=(own, P(), own) + weights + (gain,) * 6,
        check_vma=False,
    )
```

```python
import functools
import math

import jax
import jax.numpy as jnp
from jax import lax
from jax.experimental import pallas as pl
from jax.experimental.pallas import tpu as pltpu
from jax.sharding import PartitionSpec as P

WIN = 512
EPS = 1e-06
MASKED = -1e30
LOW = jnp.bfloat16
F32 = jnp.float32


def swap(values, axis, bits):
    return lax.ppermute(values, axis, [(i, i ^ bits) for i in range(lax.axis_size(axis))])


def shifted(values, axis, by):
    size = lax.axis_size(axis)
    return lax.ppermute(values, axis, [(i, i + by) for i in range(size) if 0 <= i + by < size])


def exchange(values, axes):
    return lax.all_to_all(values, axes, 0, 0, tiled=True)


def after(value, *earlier):
    return lax.optimization_barrier((value,) + earlier)[0]


def dot(left, right, contract):
    return lax.dot_general(left, right, (contract, ((), ())), preferred_element_type=F32)


def mm(left, right):
    return dot(left, right, ((1,), (0,)))


def mm_t(left, right):
    return dot(left, right, ((1,), (1,)))


def t_mm(left, right):
    return dot(left, right, ((0,), (0,)))


def inverse_rms(values):
    return lax.rsqrt(jnp.mean(values * values, axis=-1, keepdims=True) + EPS)


def rms_back(grad, values, inverse, gain_row):
    n = values * inverse
    eg = grad * gain_row
    return inverse * (eg - n * jnp.mean(eg * n, axis=-1, keepdims=True)), grad * n


def turn(values):
    half = values.shape[-1] // 2
    return jnp.concatenate([-values[..., half:], values[..., :half]], axis=-1)


def turn_back(values):
    half = values.shape[-1] // 2
    return jnp.concatenate([values[..., half:], -values[..., :half]], axis=-1)


def rotary_tables(positions, head_width):
    frequency = 10000.0 ** (-2.0 * jnp.arange(head_width // 2, dtype=F32) / head_width)
    angles = positions.astype(F32)[:, None] * frequency[None, :]
    angles = jnp.concatenate([angles, angles], axis=-1)
    return jnp.cos(angles), jnp.sin(angles)


def heads_of(values, heads):
    width = values.shape[1] // heads
    return [values[:, h * width : (h + 1) * width] for h in range(heads)]


VMEM = pl.BlockSpec(memory_space=pltpu.VMEM)
SMEM = pl.BlockSpec(memory_space=pltpu.SMEM)
ROOM = pltpu.CompilerParams(vmem_limit_bytes=28 * 1024 * 1024)
ALL = pltpu.CompilerParams(vmem_limit_bytes=60 * 1024 * 1024)


def cost(multiply_adds, *arrays):
    moved = sum(math.prod(v.shape) * jnp.dtype(v.dtype).itemsize for v in arrays)
    return pl.CostEstimate(flops=2 * multiply_adds, bytes_accessed=moved, transcendentals=0)


def struct(shape, dtype):
    return jax.ShapeDtypeStruct(shape, dtype)


def column_sum(values):
    return jnp.sum(values, axis=0, keepdims=True)


def assemble_kernel(pieces, core_ref, *refs):
    width = refs[0].shape[1] // 2
    results = refs[2 * pieces :]
    for step in range(2):

        @pl.when(pl.program_id(0) == step)
        def _():
            for i, result in enumerate(results):
                for p in range(pieces):
                    result[0, :, p * width : (p + 1) * width] = refs[step * pieces + p][:, i * width : (i + 1) * width]


def assemble(core, mine, others):
    half, width = mine[0].shape
    pieces = len(mine)
    wide = pieces * width // 2
    out = pl.BlockSpec((1, half, wide), lambda i, core: (i ^ core[0], 0, 0))
    results = pl.pallas_call(
        functools.partial(assemble_kernel, pieces),
        grid_spec=pltpu.PrefetchScalarGridSpec(
            num_scalar_prefetch=1,
            grid=(2,),
            in_specs=[pl.BlockSpec((half, width), lambda i, core: (0, 0))] * (2 * pieces),
            out_specs=[out, out],
        ),
        out_shape=[struct((2, half, wide), LOW)] * 2,
        compiler_params=ROOM,
        cost_estimate=cost(0, *mine, *others, *mine, *others),
        name="assemble",
    )(core.reshape(1), *mine, *others)
    return [v.reshape(2 * half, wide) for v in results]


def norm_rows_kernel(chunks, place_ref, x_ref, gain_ref, out_ref):
    sub = x_ref.shape[1] // chunks
    for p in range(chunks):
        x = x_ref[0, pl.ds(pl.multiple_of((place_ref[0] ^ p) * sub, sub), sub), :].astype(F32)
        out_ref[p, 0] = (x * inverse_rms(x) * gain_ref[...]).astype(LOW)


def norm_rows(place, x, gain_row, chunks):
    seqs, rows, width = x.shape
    sub = rows // chunks
    return pl.pallas_call(
        functools.partial(norm_rows_kernel, chunks),
        grid=(seqs,),
        in_specs=[
            pl.BlockSpec(memory_space=pltpu.SMEM),
            pl.BlockSpec((1, rows, width), lambda s: (s, 0, 0)),
            pl.BlockSpec((1, width), lambda s: (0, 0)),
        ],
        out_specs=pl.BlockSpec((chunks, 1, sub, width), lambda s: (0, s, 0, 0)),
        out_shape=jax.ShapeDtypeStruct((chunks, seqs, sub, width), LOW),
        compiler_params=ROOM,
        cost_estimate=cost(0, x, x, x, x),
        name="norm_rows",
    )(place.reshape(1), x, gain_row).reshape(chunks * seqs * sub, width)


def keys_kernel(core_ref, x_ref, near_ref, far_ref, gain_ref, cos_ref, sin_ref, pair_ref, first_ref, raw_ref, full_ref):
    chunks, _, sub, width = x_ref.shape
    half = near_ref.shape[0]
    head = gain_ref.shape[1]

    @pl.when(pl.program_id(0) == 0)
    def _():
        for place, source in ((core_ref[0], near_ref), (1 - core_ref[0], far_ref)):
            full_ref[pl.ds(pl.multiple_of(place * half, half), half), :] = source[...]

    kv = mm(x_ref[...].reshape(chunks * sub, width), full_ref[...])
    key = kv[:, :head]
    n = key * inverse_rms(key) * gain_ref[...]
    rot = (n * cos_ref[...] + turn(n) * sin_ref[...]).astype(LOW)
    value = kv[:, head:].astype(LOW)
    raw_ref[...] = key[:sub]
    pair_ref[:, 0, :, :head] = rot.reshape(chunks, sub, head)
    pair_ref[:, 0, :, head:] = value.reshape(chunks, sub, head)
    first_ref[0, :, :head] = rot[:sub]
    first_ref[0, :, head:] = value[:sub]


def project_keys(core, normed, near, far, gain_row, cos, sin):
    chunks, seqs, sub, width = normed.shape
    half, both = near.shape
    head = both // 2
    whole = lambda *shape: pl.BlockSpec(shape, lambda s: (0,) * len(shape))
    return pl.pallas_call(
        keys_kernel,
        grid=(seqs,),
        in_specs=[
            SMEM,
            pl.BlockSpec((chunks, 1, sub, width), lambda s: (0, s, 0, 0)),
            whole(half, both),
            whole(half, both),
            whole(1, head),
            whole(chunks * sub, head),
            whole(chunks * sub, head),
        ],
        out_specs=[
            pl.BlockSpec((chunks, 1, sub, both), lambda s: (0, s, 0, 0)),
            pl.BlockSpec((1, sub, both), lambda s: (s, 0, 0)),
            pl.BlockSpec((sub, head), lambda s: (s, 0)),
            whole(2 * half, both),
        ],
        out_shape=[
            struct((chunks, seqs, sub, both), LOW),
            struct((seqs, sub, both), LOW),
            struct((seqs * sub, head), F32),
            struct((2 * half, both), LOW),
        ],
        compiler_params=ROOM,
        cost_estimate=cost(seqs * chunks * sub * width * both, normed, normed),
        name="project_keys",
    )(core.reshape(1), normed, near, far, gain_row, cos, sin)


def mask_of(qinfo_ref, kinfo_ref):
    qpos, qseg = qinfo_ref[0, :, 0:1], qinfo_ref[0, :, 1:2]
    kpos, kseg = kinfo_ref[0, 0:1, :], kinfo_ref[0, 1:2, :]
    return (kseg == qseg) & (kpos <= qpos) & (kpos > qpos - WIN)


def key_rows(kv_refs, width):
    own_ref, *far_refs = kv_refs
    sides = []
    for at in (0, width):
        own = own_ref[:, 0, :, at : at + width].reshape(own_ref.shape[0] * own_ref.shape[2], width)
        sides.append(jnp.concatenate([own] + [r[0, :, at : at + width] for r in far_refs], axis=0))
    return sides


def attend_kernel(heads, qinfo_ref, kinfo_ref, q_ref, gain_ref, cos_ref, sin_ref, *refs):
    kv_refs, (rot_ref, out_ref, lse_ref) = refs[:-3], refs[-3:]
    width = q_ref.shape[1] // heads
    scale = width ** (-0.5)
    rotated = []
    for h, q in enumerate(heads_of(q_ref[...], heads)):
        n = q * inverse_rms(q) * gain_ref[...]
        rot = ((n * cos_ref[...] + turn(n) * sin_ref[...]) * scale).astype(LOW)
        rot_ref[:, h * width : (h + 1) * width] = rot
        rotated.append(rot)
    rows = jnp.concatenate(rotated, axis=0)
    keys, vals = key_rows(kv_refs, width)
    bias = jnp.where(mask_of(qinfo_ref, kinfo_ref), 0.0, MASKED)
    allowed = jnp.concatenate([bias] * heads, axis=0) == 0.0
    scores = jnp.where(allowed, mm_t(rows, keys), MASKED)
    top = jnp.max(scores, axis=1, keepdims=True)
    expos = jnp.exp(scores - top)
    total = jnp.sum(expos, axis=1, keepdims=True)
    lse_ref[0] = top + jnp.log(total)
    probs = (expos / total).astype(LOW)
    attended = mm(probs, vals).astype(LOW)
    count = q_ref.shape[0]
    for h in range(heads):
        out_ref[:, h * width : (h + 1) * width] = attended[h * count : (h + 1) * count]


def attend_back_kernel(heads, chunks, blocks, place_ref, qinfo_ref, kinfo_ref, q_ref, gain_ref, cos_ref, sin_ref, rot_ref, lse_ref,
                       dout_ref, *refs):
    far_count = (blocks - 1) * chunks
    kv_refs, (dq_ref, dgain_ref), dkv_refs = refs[: far_count + 1], refs[far_count + 1 : far_count + 3], refs[far_count + 3 :]
    width = q_ref.shape[1] // heads
    scale = width ** (-0.5)
    count = q_ref.shape[0]
    rows = jnp.concatenate(heads_of(rot_ref[...], heads), axis=0)
    douts = jnp.concatenate(heads_of(dout_ref[...], heads), axis=0)
    keys, vals = key_rows(kv_refs, width)
    bias = jnp.where(mask_of(qinfo_ref, kinfo_ref), 0.0, MASKED)
    allowed = jnp.concatenate([bias] * heads, axis=0) == 0.0
    probs = jnp.where(allowed, jnp.exp(mm_t(rows, keys) - lse_ref[0]), 0.0)
    d_probs = mm_t(douts, vals)
    delta = jnp.sum(probs * d_probs, axis=1, keepdims=True)
    d_scores = (probs * (d_probs - delta)).astype(LOW)
    d_rows = mm(d_scores, keys)
    d_keys = t_mm(d_scores, rows)
    d_vals = t_mm(probs.astype(LOW), douts)
    per = kv_refs[0].shape[2]
    for part, at in ((d_keys, 0), (d_vals, width)):
        piece = lambda b, p: part[(b * chunks + p) * per : (b * chunks + p + 1) * per]
        for b in range(blocks):
            dkv_refs[0][b, 0, :, at : at + width] = piece(b, 0)
        for p in range(1, chunks):
            earlier = (place_ref[0] ^ p) < place_ref[0]
            for b in range(1, blocks - 1):
                dkv_refs[p][b - 1, 0, :, at : at + width] = piece(b, p).astype(LOW)
            dkv_refs[p][blocks - 2, 0, :, at : at + width] = jnp.where(earlier, piece(0, p), piece(blocks - 1, p)).astype(LOW)
    gain_sum = jnp.zeros((1, width), F32)
    for h, q in enumerate(heads_of(q_ref[...], heads)):
        e = d_rows[h * count : (h + 1) * count] * scale
        e = e * cos_ref[...] + turn_back(e * sin_ref[...])
        d_q, d_g = rms_back(e, q, inverse_rms(q), gain_ref[...])
        gain_sum = gain_sum + column_sum(d_g)
        dq_ref[:, h * width : (h + 1) * width] = d_q.astype(LOW)
    dgain_ref[0] = gain_sum


def pair_sum_kernel(*refs):
    out = refs[-1]
    for i in range(out.shape[0]):
        out[i] = (refs[2 * i][...].astype(F32) + refs[2 * i + 1][...].astype(F32)).astype(LOW)


def pair_sum(*pairs):
    rows, width = pairs[0][0].shape
    step = rows // 4 if rows % 64 == 0 else rows
    arrays = [v for pair in pairs for v in pair]
    return pl.pallas_call(
        pair_sum_kernel,
        grid=(rows // step,),
        in_specs=[pl.BlockSpec((step, width), lambda j: (j, 0))] * len(arrays),
        out_specs=pl.BlockSpec((len(pairs), step, width), lambda j: (0, j, 0)),
        out_shape=struct((len(pairs), rows, width), LOW),
        compiler_params=ROOM,
        name="pair_sum",
    )(*arrays)


def attention_specs(seqs, rows, spans, chunks, wide, width):
    whole = lambda *shape: pl.BlockSpec(shape, lambda s: (0,) * len(shape))
    return dict(
        qinfo=pl.BlockSpec((1, rows, 2), lambda s: (s, 0, 0)),
        kinfo=pl.BlockSpec((1, 2, spans), lambda s: (s, 0, 0)),
        q=pl.BlockSpec((rows, wide), lambda s: (s, 0)),
        gain=whole(1, width),
        table=whole(rows, width),
        own=pl.BlockSpec((chunks, 1, rows, 2 * width), lambda s: (0, s, 0, 0)),
        far=pl.BlockSpec((1, rows, 2 * width), lambda s: (s, 0, 0)),
        lse=pl.BlockSpec((1, rows * (wide // width), 1), lambda s: (s, 0, 0)),
        dgain=pl.BlockSpec((1, 1, width), lambda s: (s, 0, 0)),
    )


def mix_kernel(att_ref, out_ref, x_ref, gain_attn_ref, gain_ffn_ref, branch_ref, hidden_ref, ffn_ref):
    branch = mm_t(att_ref[...], out_ref[...])
    branch_ref[...] = branch
    hidden = x_ref[...].astype(F32) + branch * inverse_rms(branch) * gain_attn_ref[...]
    hidden_ref[...] = hidden
    ffn_ref[...] = (hidden * inverse_rms(hidden) * gain_ffn_ref[...]).astype(LOW)


def for_blocks(width, step, block):
    full, rest = divmod(width, step)

    @pl.when(pl.program_id(0) < full)
    def _():
        block(step)

    if rest:

        @pl.when(pl.program_id(0) == full)
        def _():
            block(rest)


def ffn_kernel(units, chunks, *refs):
    rows_refs, (gate_ref, up_ref, down_ref) = refs[:chunks], refs[chunks : chunks + 3]
    part_refs, (act_ref, slope_ref, curve_ref, sums) = refs[chunks + 3 : 2 * chunks + 3], refs[2 * chunks + 3 :]

    @pl.when(pl.program_id(0) == 0)
    def _():
        sums[...] = jnp.zeros_like(sums)

    def block(size):
        rows = jnp.concatenate([r[...] for r in rows_refs], axis=0)
        gate, up = mm(rows, gate_ref[0, :, :size]), mm(rows, up_ref[0, :, :size])
        root = (2.0 / math.pi) ** 0.5
        square = gate * gate
        bend = jnp.tanh(root * (gate + 0.044715 * (square * gate)))
        share = 0.5 * (1.0 + bend)
        curve = gate * share
        slope = share + 0.5 * gate * (1.0 - bend * bend) * (root * (1.0 + 3.0 * 0.044715 * square))
        act = (curve * up).astype(LOW)
        act_ref[:, :size] = act
        slope_ref[:, :size] = (slope * up).astype(LOW)
        curve_ref[:, :size] = curve.astype(LOW)
        sums[...] += mm_t(act, down_ref[0, :, :size])

    for_blocks(units, act_ref.shape[1], block)
    split_rows(sums, part_refs)


def split_rows(sums, part_refs):
    @pl.when(pl.program_id(0) == pl.num_programs(0) - 1)
    def _():
        count = part_refs[0].shape[0]
        for p, part in enumerate(part_refs):
            part[...] = sums[p * count : (p + 1) * count].astype(part.dtype)


def ffn_back_kernel(units, chunks, *refs):
    rows_refs, (gate_ref, up_ref, down_ref, slope_ref, curve_ref) = refs[:chunks], refs[chunks : chunks + 5]
    part_refs, (dgate_ref, dup_ref, sums) = refs[chunks + 5 : 2 * chunks + 5], refs[2 * chunks + 5 :]

    @pl.when(pl.program_id(0) == 0)
    def _():
        sums[...] = jnp.zeros_like(sums)

    def block(size):
        rows = jnp.concatenate([r[...] for r in rows_refs], axis=0)
        d_act = mm(rows, down_ref[0, :, :size])
        d_gate = (d_act * slope_ref[:, :size].astype(F32)).astype(LOW)
        d_up = (d_act * curve_ref[:, :size].astype(F32)).astype(LOW)
        dgate_ref[:, :size] = d_gate
        dup_ref[:, :size] = d_up
        sums[...] += mm_t(d_gate, gate_ref[0, :, :size]) + mm_t(d_up, up_ref[0, :, :size])

    for_blocks(units, dgate_ref.shape[1], block)
    split_rows(sums, part_refs)


def ffn_call(kernel, name, rows, weights, saved, results, dtype, step=640):
    chunks = len(rows)
    count, width = rows[0].shape
    units = weights.shape[2]
    whole = pl.BlockSpec((count, width), lambda j: (0, 0))
    strip = pl.BlockSpec((chunks * count, step), lambda j: (0, j))
    flat = pl.pallas_call(
        functools.partial(kernel, units, chunks),
        grid=(pl.cdiv(units, step),),
        in_specs=[whole] * chunks
        + [pl.BlockSpec((1, width, step), lambda j, i=i: (i, 0, j)) for i in range(3)]
        + [strip] * len(saved),
        out_specs=[whole] * chunks + [strip] * results,
        out_shape=[struct((count, width), dtype)] * chunks + [struct((chunks * count, units), LOW)] * results,
        scratch_shapes=[pltpu.VMEM((chunks * count, width), F32)],
        compiler_params=ALL,
        cost_estimate=cost(3 * chunks * count * width * units, *rows, weights, *saved),
        name=name,
    )(*rows, weights, weights, weights, *saved)
    return flat[:chunks], flat[chunks:]


def loss_kernel(factor_ref, hidden_ref, target_ref, valid_ref, gain_ref, *refs):
    parts, (out_ref, dres_ref, dffn_ref, dgain_ref, error_ref) = refs[:-5], refs[-5:]
    ffn = sum(r[...].astype(F32) for r in parts)
    inverse = inverse_rms(ffn)
    result = hidden_ref[...] + ffn * inverse * gain_ref[...]
    out_ref[...] = result.astype(LOW)
    mismatch = result - target_ref[...].astype(F32)
    marked = valid_ref[...] * mismatch
    error_ref[...] = jnp.broadcast_to(column_sum(jnp.sum(marked * mismatch, axis=1, keepdims=True)), error_ref.shape)
    d_result = factor_ref[0] * marked
    dres_ref[...] = d_result
    d_ffn, d_gain = rms_back(d_result, ffn, inverse, gain_ref[...])
    dffn_ref[...] = d_ffn.astype(LOW)
    dgain_ref[...] = column_sum(d_gain)


def middle_kernel(dres_ref, hidden_ref, branch_ref, out_ref, gain_ffn_ref, gain_attn_ref, *refs):
    parts, (dhid_ref, dbranch_ref, datt_ref, dgain_ffn_ref, dgain_attn_ref) = refs[:-5], refs[-5:]
    d_ffn_in = sum(r[...].astype(F32) for r in parts)
    hidden = hidden_ref[...]
    d_add, d_gain = rms_back(d_ffn_in, hidden, inverse_rms(hidden), gain_ffn_ref[...])
    dgain_ffn_ref[...] = column_sum(d_gain)
    d_hidden = dres_ref[...] + d_add
    dhid_ref[...] = d_hidden
    branch = branch_ref[...]
    d_branch, d_gain = rms_back(d_hidden, branch, inverse_rms(branch), gain_attn_ref[...])
    dgain_attn_ref[...] = column_sum(d_gain)
    low = d_branch.astype(LOW)
    dbranch_ref[...] = low
    datt_ref[...] = mm(low, out_ref[...]).astype(LOW)


def pull_kernel(left_ref, right_ref, out_ref):
    out_ref[...] = mm_t(left_ref[...], right_ref[...])


def finish_kernel(core_ref, raw_ref, cos_ref, sin_ref, gain_key_ref, pulled_ref, kv_ref, dhid_ref, x_ref, gain_ref, normed_ref, *refs):
    parts, (din_ref, dgain_ref, dgain_key_ref, send_ref, own_ref, sums) = refs[:-6], refs[-6:]
    head = raw_ref.shape[1]
    d_kv = sum(r[...].astype(F32) for r in parts)
    key = raw_ref[...]
    e = d_kv[:, :head]
    e = e * cos_ref[...] + turn_back(e * sin_ref[...])
    d_key, d_gain = rms_back(e, key, inverse_rms(key), gain_key_ref[...])
    dgain_key_ref[...] = column_sum(d_gain)
    low = jnp.concatenate([d_key.astype(LOW), d_kv[:, head:].astype(LOW)], axis=1)
    sums[...] = mm(normed_ref[...].T, low)
    half = own_ref.shape[0]
    core = core_ref[0]
    own_ref[...] = sums[pl.ds(pl.multiple_of(core * half, half), half), :].astype(LOW)
    send_ref[...] = sums[pl.ds(pl.multiple_of((1 - core) * half, half), half), :].astype(LOW)
    d_normed = pulled_ref[...] + mm_t(low, kv_ref[...])
    x = x_ref[...].astype(F32)
    d_x, d_gain = rms_back(d_normed, x, inverse_rms(x), gain_ref[...])
    dgain_ref[...] = column_sum(d_gain)
    din_ref[...] = dhid_ref[...] + d_x


def weight_grad_kernel(chunks, sets, core_ref, *refs):
    lefts, refs = refs[:chunks], refs[chunks:]
    rights, refs = refs[: chunks * sets], refs[chunks * sets :]
    outs, (turned, sums) = refs[: 2 * sets], refs[2 * sets :]
    rows = lefts[0].shape[0]
    half = outs[0].shape[0]

    @pl.when(pl.program_id(0) == 0)
    def _():
        for p in range(chunks):
            turned[:, p * rows : (p + 1) * rows] = lefts[p][...].T

    core = core_ref[0]
    for i in range(sets):
        right = jnp.concatenate([r[...] for r in rights[i * chunks : (i + 1) * chunks]], axis=0)
        sums[i] = mm(turned[...], right)
        for place, out in ((1 - core, outs[2 * i]), (core, outs[2 * i + 1])):
            out[...] = sums[i, pl.ds(pl.multiple_of(place * half, half), half), :].astype(LOW)


def weight_grad(core, rows, lefts, *rights, step=256):
    chunks, sets = len(lefts), len(rights)
    height = lefts[0][0].shape[1]
    width = rights[0][0][0].shape[1]
    rights = [pair for group in rights for pair in group]
    out = pl.BlockSpec((height // 2, step), lambda j: (0, j))
    flat = pl.pallas_call(
        functools.partial(weight_grad_kernel, chunks, sets),
        grid=(pl.cdiv(width, step),),
        in_specs=[SMEM]
        + [pl.BlockSpec((rows, height), lambda j, at=at: (at, 0)) for _, at in lefts]
        + [pl.BlockSpec((rows, step), lambda j, at=at: (at, j)) for _, at in rights],
        out_specs=[out] * (2 * sets),
        out_shape=[struct((height // 2, width), LOW)] * (2 * sets),
        scratch_shapes=[pltpu.VMEM((height, chunks * rows), LOW), pltpu.VMEM((sets, height, step), F32)],
        compiler_params=ALL if chunks > 1 else ROOM,
        cost_estimate=cost(sets * chunks * rows * height * width, *[v for v, _ in lefts], struct((height, sets * width), LOW)),
        name="weight_grad",
    )(core.reshape(1), *[v for v, _ in lefts], *[v for v, _ in rights])
    return [flat[2 * i : 2 * i + 2] for i in range(sets)]


def shards(inputs, target, segment_ids, w_query, w_key, w_value, w_out, w_gate, w_up, w_down,
           gain_input, gain_query, gain_key, gain_post_attn, gain_pre_ffn, gain_post_ffn):
    F, C, T = (lax.axis_size(a) for a in ("fsdp", "ctx", "tp"))
    f, z, t = (lax.axis_index(a) for a in ("fsdp", "ctx", "tp"))
    me = f * C + z
    seqs, block_rows, width_model = inputs.shape
    piece = w_query.shape[0]
    head_width = w_key.shape[1]
    gain_piece = gain_query.shape[0]
    sub = block_rows // T
    own = seqs * sub
    half = C * piece
    halo = -(-(WIN - 1) // block_rows)
    spans = (halo + 1) * block_rows

    both = 2 * head_width
    blocks = jnp.stack([jnp.concatenate([w_query, w_out.T], axis=1), jnp.concatenate([w_key, w_value], axis=1)])
    near = lax.all_gather(blocks, "ctx", axis=1, tiled=True)
    weights = lax.all_gather(jnp.stack([w_gate, w_up, w_down.T]), ("fsdp", "ctx"), axis=1, tiled=True)
    packed = jnp.concatenate(
        [gain_input, gain_post_attn, gain_pre_ffn, gain_post_ffn, gain_query, gain_key, segment_ids.astype(LOW).reshape(-1)]
    )
    packed = exchange(jnp.broadcast_to(packed[None], (F * C, packed.shape[0])), ("fsdp", "ctx")).astype(F32)
    at = 4 * piece
    g_input, g_post_attn, g_pre_ffn, g_post_ffn = [
        packed[:, i * piece : (i + 1) * piece].reshape(1, width_model) for i in range(4)
    ]
    g_query, g_key = [
        packed[:, at + i * gain_piece : at + (i + 1) * gain_piece].reshape(1, head_width) for i in range(2)
    ]
    seg_blocks = packed[:, at + 2 * gain_piece :].astype(jnp.int32)
    count = jnp.sum((seg_blocks != 0).astype(F32))
    normed = norm_rows(t, inputs, g_input, T)
    def sub_rows(values):
        return [lax.dynamic_slice_in_dim(values, (t ^ p) * sub, sub, 1) for p in range(T)]

    x_own = lax.dynamic_slice_in_dim(inputs, t * sub, sub, 1).reshape(own, width_model)
    target_own = lax.dynamic_slice_in_dim(target, t * sub, sub, 1).reshape(own, width_model)
    positions = jnp.concatenate([z * block_rows + (t ^ p) * sub + jnp.arange(sub, dtype=jnp.int32) for p in range(T)])
    segs = [segment_ids + 1]
    for d in range(1, halo + 1):
        far = lax.dynamic_index_in_dim(seg_blocks, jnp.maximum(me - d, 0), 0, False).reshape(seqs, block_rows)
        segs.append(jnp.where(z >= d, far + 1, 0))
    key_seg = jnp.concatenate([v for seg in segs for v in sub_rows(seg)], axis=1)
    key_pos = jnp.concatenate([positions - d * block_rows for d in range(halo + 1)])
    kinfo = jnp.stack([jnp.broadcast_to(key_pos, (seqs, spans)), key_seg], axis=1)
    qinfo = jnp.stack([jnp.broadcast_to(positions[:sub], (seqs, sub)), key_seg[:, :sub]], axis=2)
    valid_own = (key_seg[:, :sub] != 1).astype(F32).reshape(own, 1)
    cos_all, sin_all = rotary_tables(positions, head_width)
    cos_own, sin_own = cos_all[:sub], sin_all[:sub]

    ready = (normed, kinfo, qinfo, cos_all, sin_all, cos_own, sin_own, g_query, g_key, g_post_attn, g_pre_ffn, x_own)
    (near, *ready) = lax.optimization_barrier((near,) + ready)
    normed, kinfo, qinfo, cos_all, sin_all, cos_own, sin_own, g_query, g_key, g_post_attn, g_pre_ffn, x_own = ready
    near_qo, near_kv = near
    far_kv = swap(near_kv, "fsdp", 1)
    near_qo = [near_qo] + [swap(near_qo, "tp", p) for p in range(1, T)]
    pair, first, key_own, kv_full = project_keys(f, normed.reshape(T, seqs, sub, width_model), near_kv, far_kv, g_key, cos_all, sin_all)
    q_full, out_full = assemble(f, near_qo, [swap(after(v, first), "fsdp", 1) for v in near_qo])
    kv_rows, far = [pair], first
    for d in range(halo):
        far = shifted(far, "ctx", 1)
        kv_rows += [swap(far, "tp", p) if p else far for p in range(T)]
    normed_own = normed[:own]
    q_raw = mm(normed_own, q_full)
    wide = q_raw.shape[1]
    heads = wide // head_width
    specs = attention_specs(seqs, sub, spans, T, wide, head_width)
    kv_specs = [specs["own"]] + [specs["far"]] * (halo * T)
    q_rot, attended, lse = pl.pallas_call(
        functools.partial(attend_kernel, heads),
        grid=(seqs,),
        in_specs=[specs[k] for k in ("qinfo", "kinfo", "q", "gain", "table", "table")] + kv_specs,
        out_specs=[specs["q"], specs["q"], specs["lse"]],
        out_shape=[struct((own, wide), LOW), struct((own, wide), LOW), struct((seqs, sub * heads, 1), F32)],
        compiler_params=ROOM,
        cost_estimate=cost(4 * own * spans * wide // seqs, *kv_rows, q_raw),
        name="attend",
    )(qinfo, kinfo, q_raw, g_query, cos_own, sin_own, *kv_rows)
    token = struct((own, width_model), F32)
    token_low = struct((own, width_model), LOW)
    gain_row = struct((1, width_model), F32)
    branch, hidden, ffn_in = pl.pallas_call(
        mix_kernel, out_shape=[token, token, token_low], compiler_params=ROOM, cost_estimate=cost(own * wide * width_model, out_full, out_full), name="mix"
    )(attended, out_full, x_own, g_post_attn, g_pre_ffn)

    from_tp = lambda parts: parts[:1] + [swap(v, "tp", p) for p, v in enumerate(parts) if p]
    ffn_ins = from_tp([ffn_in] * T)
    groups = [[0], [1], list(range(2, T))]
    place = {p: (g, i) for g, group in enumerate(groups) for i, p in enumerate(group)}
    done = [ffn_call(ffn_kernel, "ffn", [ffn_ins[p] for p in group], weights, (), 3, LOW if g else F32) for g, group in enumerate(groups)]
    parts = [done[place[p][0]][0][place[p][1]] for p in range(T)]
    acts, slopes, curves = zip(*[results for _, results in done])
    acts = [(acts[place[p][0]], place[p][1]) for p in range(T)]
    all_tokens = seqs * block_rows * F * C
    output, d_result, d_ffn_low, dg_post_ffn, error = pl.pallas_call(
        loss_kernel,
        in_specs=[SMEM] + [VMEM] * (4 + T),
        out_shape=[token_low, token, token_low, gain_row, struct((1, 128), F32)],
        compiler_params=ROOM,
        cost_estimate=cost(own, *parts, *parts),
        name="loss",
    )((all_tokens / count).reshape(1), hidden, target_own, valid_own, g_post_ffn, *from_tp(parts))

    def collect_core(send, mine, *earlier):
        other = swap(send, "fsdp", 1)
        return mine.astype(F32) + (after(other, *earlier) if earlier else other).astype(F32)

    def scatter_ctx(sums):
        return lax.psum_scatter(sums, "ctx", scatter_dimension=1, tiled=True).astype(F32)

    d_outs = from_tp([d_ffn_low] * T)
    done = []
    for g, group in enumerate(groups):
        rows = [d_outs[p] for p in group]
        if g == 1:
            rows[0] = after(rows[0], done[0][0][0])
        if g == 2:
            rows[0] = after(rows[0], done[1][0][0])
        done.append(ffn_call(ffn_back_kernel, "ffn_back", rows, weights, (slopes[g], curves[g]), 2, LOW if g else F32))
    last = done[-1][0][-1]
    (down_halves,) = weight_grad(f, own, [(v if p else after(v, last), 0) for p, v in enumerate(d_outs)], acts)
    down_sum = pair_sum((down_halves[1], swap(down_halves[0], "fsdp", 1)))
    (grad_down,) = scatter_ctx(down_sum)
    parts = [done[place[p][0]][0][place[p][1]] for p in range(T)]
    d_gates, d_ups = [[(done[place[p][0]][1][i], place[p][1]) for p in range(T)] for i in range(2)]
    first_in = after(ffn_ins[0], down_sum)
    gate_halves, up_halves = weight_grad(f, own, [(v, 0) for v in [first_in] + ffn_ins[1:]], d_gates, d_ups)

    parts = [after(v, *gate_halves, *up_halves) if p == 0 else v for p, v in enumerate(from_tp(parts))]
    d_hidden, d_branch, d_attended, dg_pre_ffn, dg_post_attn = pl.pallas_call(
        middle_kernel,
        out_shape=[token, token_low, struct((own, wide), LOW), gain_row, gain_row],
        compiler_params=ROOM,
        cost_estimate=cost(300 * own * wide * width_model, out_full),
        name="middle",
    )(d_result, hidden, branch, out_full, g_pre_ffn, g_post_attn, *parts)
    assert halo * block_rows == WIN
    others = [after(swap(after(v[0], *parts[1:]), "fsdp", 1), d_branch) for v in (gate_halves, up_halves)]
    both_sums = pair_sum((gate_halves[1], others[0]), (up_halves[1], others[1]))
    grad_gate, grad_up = scatter_ctx(both_sums)
    d_attended = after(d_attended, both_sums)
    (out_halves,) = weight_grad(f, own, [(d_branch, 0)], [(attended, 0)])
    out_sum = collect_core(*out_halves)
    out_low = out_sum.astype(LOW)
    d_attended = after(d_attended, *out_halves)
    d_query, dg_query, *d_pairs = pl.pallas_call(
        functools.partial(attend_back_kernel, heads, T, halo + 1),
        grid=(seqs,),
        in_specs=[SMEM] + [specs[k] for k in ("qinfo", "kinfo", "q", "gain", "table", "table", "q", "lse", "q")] + kv_specs,
        out_specs=[specs["q"], specs["dgain"]]
        + [pl.BlockSpec((halo + (p == 0), 1, sub, 2 * head_width), lambda s: (0, s, 0, 0)) for p in range(T)],
        out_shape=[struct((own, wide), LOW), struct((seqs, 1, head_width), F32)]
        + [struct((halo + (p == 0), seqs, sub, 2 * head_width), F32 if p == 0 else LOW) for p in range(T)],
        compiler_params=ALL,
        name="attend_back",
    )(t.reshape(1), qinfo, kinfo, q_raw, g_query, cos_own, sin_own, q_rot, lse, d_attended, *kv_rows)
    d_own = after(d_pairs[0], out_low)
    d_blocks = [d_own[b] for b in range(halo + 1)]
    for p in range(1, T):
        got = swap(d_pairs[p], "tp", p).astype(F32)
        for b in range(1, halo):
            d_blocks[b] = d_blocks[b] + got[b - 1]
        later = (t ^ p) > t
        d_blocks[0] = d_blocks[0] + jnp.where(later, got[halo - 1], 0.0)
        d_blocks[halo] = d_blocks[halo] + jnp.where(later, 0.0, got[halo - 1])
    d_kv = d_blocks[halo]
    d_query_late, out_low = after(d_query, d_kv.astype(LOW)), after(out_low, d_kv.astype(LOW))
    for d in range(halo, 0, -1):
        come = shifted(d_kv.astype(LOW), "ctx", -1)
        if d > 1:
            d_kv = d_blocks[d - 1] + come.astype(F32)
    d_kv = [d_blocks[0], come]
    head = lambda v, p: v[:, p * head_width : (p + 1) * head_width]
    heads_sent = [jnp.concatenate([head(d_query_late, p), head(out_low, p)], axis=0) for p in range(1, T)]
    heads_here = [swap(v, "tp", p + 1) for p, v in enumerate(heads_sent)]
    out_head = head(out_sum, 0)
    for v in heads_here:
        out_head = out_head + v[own:].astype(F32)
    normed_late = after(normed, come)
    (q_halves,) = weight_grad(f, own, [(normed_late, p) for p in range(T)], [(head(d_query, 0), 0)] + [(v, 0) for v in heads_here])
    pulled = pl.pallas_call(
        pull_kernel, out_shape=token, compiler_params=ROOM, name="pull"
    )(d_query, q_full)

    def pack(values, wide):
        top = lax.reduce_precision(values, 8, 7)
        flat = jnp.concatenate([top, values - top], axis=1).astype(LOW)
        rows = -(-flat.shape[1] // wide)
        return jnp.pad(flat, ((0, 0), (0, rows * wide - flat.shape[1]))).reshape(values.shape[0], rows, wide)

    def unpack(rows, n):
        flat = rows.reshape(-1)
        return flat[:n] + flat[n : 2 * n]

    def core_rows(values):
        rows = jnp.concatenate([v.reshape(F * C, -1) for v in values], axis=1).reshape(F, C, -1)
        return lax.dynamic_index_in_dim(rows, f, 0, False) + swap(lax.dynamic_index_in_dim(rows, f ^ 1, 0, False), "fsdp", 1)

    def owner_sums(weight_sums, rows):
        wide = weight_sums.shape[1]
        sent = jnp.concatenate([weight_sums.reshape(C, piece, wide), pack(rows, wide)], axis=1)
        sums = jnp.sum(exchange(sent, "ctx").astype(F32), axis=0)
        return sums[:piece], unpack(sums[piece:], rows.shape[1])

    early = core_rows(
        [dg_post_attn, dg_pre_ffn, dg_post_ffn, jnp.sum(dg_query, axis=(0, 1)), jnp.broadcast_to(error[:, :1], (F * C, 1))]
    )
    both_heads = jnp.concatenate([collect_core(*q_halves).astype(LOW), out_head.astype(LOW)], axis=1)
    d_kv[0] = after(d_kv[0], both_heads, pulled)
    own_rows = lambda table: jnp.tile(table, (seqs, 1))
    grad_input, dg_input, dg_key, *kv_halves = pl.pallas_call(
        finish_kernel,
        in_specs=[SMEM] + [VMEM] * (10 + len(d_kv)),
        out_shape=[token, gain_row, struct((1, head_width), F32)] + [struct((half, 2 * head_width), LOW)] * 2,
        scratch_shapes=[pltpu.VMEM((2 * half, 2 * head_width), F32)],
        compiler_params=ROOM,
        name="finish",
    )(f.reshape(1), key_own, own_rows(cos_own), own_rows(sin_own), g_key, pulled, kv_full, d_hidden, x_own, g_input,
      normed_own, *[v.reshape(own, 2 * head_width) for v in d_kv])
    late = core_rows([dg_input, dg_key])
    sums = jnp.concatenate([both_heads, collect_core(*kv_halves).astype(LOW)], axis=1)
    sums, total = owner_sums(sums, jnp.concatenate([early, late], axis=1))
    grad_query, grad_out = sums[:, :head_width], sums[:, head_width : 2 * head_width]
    grad_kv = sums[:, 2 * head_width :]
    low = jnp.concatenate([grad_kv.astype(LOW), pack(total[None], 2 * head_width)[0]], axis=0)
    low = lax.optimization_barrier(low)
    totals = {p: (swap(low, "tp", p) if p else low).astype(F32) for p in range(T)}
    bit = 1
    while bit < T:
        totals = {p: totals[p] + totals[p ^ bit] for p in totals if not p & bit}
        bit *= 2
    grad_kv, total = totals[0][:piece], unpack(totals[0][piece:], total.shape[0])
    early, late = total[: early.shape[1]], total[early.shape[1] :]
    loss = early[-1] / (2.0 * width_model * count)
    at = 3 * piece
    return (
        output.reshape(seqs, sub, width_model),
        loss,
        grad_input.reshape(seqs, sub, width_model),
        grad_query,
        grad_kv[:, :head_width],
        grad_kv[:, head_width:],
        grad_out.T,
        grad_gate,
        grad_up,
        grad_down.T,
        late[:piece],
        early[at : at + gain_piece],
        late[piece:],
        early[:piece],
        early[piece : 2 * piece],
        early[2 * piece : at],
    )


def solution(mesh):
    rows = P(("fsdp", "ctx"), "tp")
    cols = P("tp", ("fsdp", "ctx"))
    split = P(("fsdp", "ctx"), None)
    gain = P(("fsdp", "ctx"))
    token = P("fsdp", "ctx", None)
    own = P("fsdp", ("ctx", "tp"), None)
    weights = (rows, split, split, cols, rows, rows, cols)
    return jax.shard_map(
        shards,
        mesh=mesh,
        in_specs=(token, token, P("fsdp", "ctx")) + weights + (gain,) * 6,
        out_specs=(own, P(), own) + weights + (gain,) * 6,
        check_vma=False,
    )
```

```python
import functools
import math

import jax
import jax.numpy as jnp
from jax import lax
from jax.experimental import pallas as pl
from jax.experimental.pallas import tpu as pltpu
from jax.sharding import PartitionSpec as P

WIN = 512
EPS = 1e-06
MASKED = -1e30
LOW = jnp.bfloat16
F32 = jnp.float32


def swap(values, axis, bits):
    return lax.ppermute(values, axis, [(i, i ^ bits) for i in range(lax.axis_size(axis))])


def shifted(values, axis, by):
    size = lax.axis_size(axis)
    return lax.ppermute(values, axis, [(i, i + by) for i in range(size) if 0 <= i + by < size])


def exchange(values, axes):
    return lax.all_to_all(values, axes, 0, 0, tiled=True)


def after(value, *earlier):
    return lax.optimization_barrier((value,) + earlier)[0]


def dot(left, right, contract):
    return lax.dot_general(left, right, (contract, ((), ())), preferred_element_type=F32)


def mm(left, right):
    return dot(left, right, ((1,), (0,)))


def mm_t(left, right):
    return dot(left, right, ((1,), (1,)))


def t_mm(left, right):
    return dot(left, right, ((0,), (0,)))


def inverse_rms(values):
    return lax.rsqrt(jnp.mean(values * values, axis=-1, keepdims=True) + EPS)


def rms_back(grad, values, inverse, gain_row):
    n = values * inverse
    eg = grad * gain_row
    return inverse * (eg - n * jnp.mean(eg * n, axis=-1, keepdims=True)), grad * n


def turn(values):
    half = values.shape[-1] // 2
    return jnp.concatenate([-values[..., half:], values[..., :half]], axis=-1)


def turn_back(values):
    half = values.shape[-1] // 2
    return jnp.concatenate([values[..., half:], -values[..., :half]], axis=-1)


def rotary_tables(positions, head_width):
    frequency = 10000.0 ** (-2.0 * jnp.arange(head_width // 2, dtype=F32) / head_width)
    angles = positions.astype(F32)[:, None] * frequency[None, :]
    angles = jnp.concatenate([angles, angles], axis=-1)
    return jnp.cos(angles), jnp.sin(angles)


def heads_of(values, heads):
    width = values.shape[1] // heads
    return [values[:, h * width : (h + 1) * width] for h in range(heads)]


VMEM = pl.BlockSpec(memory_space=pltpu.VMEM)
SMEM = pl.BlockSpec(memory_space=pltpu.SMEM)
ROOM = pltpu.CompilerParams(vmem_limit_bytes=28 * 1024 * 1024)
ALL = pltpu.CompilerParams(vmem_limit_bytes=60 * 1024 * 1024)


def cost(multiply_adds, *arrays):
    moved = sum(math.prod(v.shape) * jnp.dtype(v.dtype).itemsize for v in arrays)
    return pl.CostEstimate(flops=2 * multiply_adds, bytes_accessed=moved, transcendentals=0)


def struct(shape, dtype):
    return jax.ShapeDtypeStruct(shape, dtype)


def column_sum(values):
    return jnp.sum(values, axis=0, keepdims=True)


def assemble_kernel(pieces, core_ref, *refs):
    width = refs[0].shape[1] // 2
    results = refs[2 * pieces :]
    for step in range(2):

        @pl.when(pl.program_id(0) == step)
        def _():
            for i, result in enumerate(results):
                for p in range(pieces):
                    result[0, :, p * width : (p + 1) * width] = refs[step * pieces + p][:, i * width : (i + 1) * width]


def assemble(core, mine, others):
    half, width = mine[0].shape
    pieces = len(mine)
    wide = pieces * width // 2
    out = pl.BlockSpec((1, half, wide), lambda i, core: (i ^ core[0], 0, 0))
    results = pl.pallas_call(
        functools.partial(assemble_kernel, pieces),
        grid_spec=pltpu.PrefetchScalarGridSpec(
            num_scalar_prefetch=1,
            grid=(2,),
            in_specs=[pl.BlockSpec((half, width), lambda i, core: (0, 0))] * (2 * pieces),
            out_specs=[out, out],
        ),
        out_shape=[struct((2, half, wide), LOW)] * 2,
        compiler_params=ROOM,
        cost_estimate=cost(0, *mine, *others, *mine, *others),
        name="assemble",
    )(core.reshape(1), *mine, *others)
    return [v.reshape(2 * half, wide) for v in results]


def norm_rows_kernel(chunks, place_ref, x_ref, gain_ref, out_ref):
    sub = x_ref.shape[1] // chunks
    for p in range(chunks):
        x = x_ref[0, pl.ds(pl.multiple_of((place_ref[0] ^ p) * sub, sub), sub), :].astype(F32)
        out_ref[p, 0] = (x * inverse_rms(x) * gain_ref[...]).astype(LOW)


def norm_rows(place, x, gain_row, chunks):
    seqs, rows, width = x.shape
    sub = rows // chunks
    return pl.pallas_call(
        functools.partial(norm_rows_kernel, chunks),
        grid=(seqs,),
        in_specs=[
            pl.BlockSpec(memory_space=pltpu.SMEM),
            pl.BlockSpec((1, rows, width), lambda s: (s, 0, 0)),
            pl.BlockSpec((1, width), lambda s: (0, 0)),
        ],
        out_specs=pl.BlockSpec((chunks, 1, sub, width), lambda s: (0, s, 0, 0)),
        out_shape=jax.ShapeDtypeStruct((chunks, seqs, sub, width), LOW),
        compiler_params=ROOM,
        cost_estimate=cost(0, x, x, x, x),
        name="norm_rows",
    )(place.reshape(1), x, gain_row).reshape(chunks * seqs * sub, width)


def keys_kernel(core_ref, x_ref, near_ref, far_ref, gain_ref, cos_ref, sin_ref, pair_ref, first_ref, raw_ref, full_ref):
    chunks, _, sub, width = x_ref.shape
    half = near_ref.shape[0]
    head = gain_ref.shape[1]

    @pl.when(pl.program_id(0) == 0)
    def _():
        for place, source in ((core_ref[0], near_ref), (1 - core_ref[0], far_ref)):
            full_ref[pl.ds(pl.multiple_of(place * half, half), half), :] = source[...]

    kv = mm(x_ref[...].reshape(chunks * sub, width), full_ref[...])
    key = kv[:, :head]
    n = key * inverse_rms(key) * gain_ref[...]
    rot = (n * cos_ref[...] + turn(n) * sin_ref[...]).astype(LOW)
    value = kv[:, head:].astype(LOW)
    raw_ref[...] = key[:sub]
    pair_ref[:, 0, :, :head] = rot.reshape(chunks, sub, head)
    pair_ref[:, 0, :, head:] = value.reshape(chunks, sub, head)
    first_ref[0, :, :head] = rot[:sub]
    first_ref[0, :, head:] = value[:sub]


def project_keys(core, normed, near, far, gain_row, cos, sin):
    chunks, seqs, sub, width = normed.shape
    half, both = near.shape
    head = both // 2
    whole = lambda *shape: pl.BlockSpec(shape, lambda s: (0,) * len(shape))
    return pl.pallas_call(
        keys_kernel,
        grid=(seqs,),
        in_specs=[
            SMEM,
            pl.BlockSpec((chunks, 1, sub, width), lambda s: (0, s, 0, 0)),
            whole(half, both),
            whole(half, both),
            whole(1, head),
            whole(chunks * sub, head),
            whole(chunks * sub, head),
        ],
        out_specs=[
            pl.BlockSpec((chunks, 1, sub, both), lambda s: (0, s, 0, 0)),
            pl.BlockSpec((1, sub, both), lambda s: (s, 0, 0)),
            pl.BlockSpec((sub, head), lambda s: (s, 0)),
            whole(2 * half, both),
        ],
        out_shape=[
            struct((chunks, seqs, sub, both), LOW),
            struct((seqs, sub, both), LOW),
            struct((seqs * sub, head), F32),
            struct((2 * half, both), LOW),
        ],
        compiler_params=ROOM,
        cost_estimate=cost(seqs * chunks * sub * width * both, normed, normed),
        name="project_keys",
    )(core.reshape(1), normed, near, far, gain_row, cos, sin)


def mask_of(qinfo_ref, kinfo_ref):
    qpos, qseg = qinfo_ref[0, :, 0:1], qinfo_ref[0, :, 1:2]
    kpos, kseg = kinfo_ref[0, 0:1, :], kinfo_ref[0, 1:2, :]
    return (kseg == qseg) & (kpos <= qpos) & (kpos > qpos - WIN)


def key_rows(kv_refs, width):
    own_ref, *far_refs = kv_refs
    sides = []
    for at in (0, width):
        own = own_ref[:, 0, :, at : at + width].reshape(own_ref.shape[0] * own_ref.shape[2], width)
        sides.append(jnp.concatenate([own] + [r[0, :, at : at + width] for r in far_refs], axis=0))
    return sides


def attend_kernel(heads, qinfo_ref, kinfo_ref, q_ref, gain_ref, cos_ref, sin_ref, *refs):
    kv_refs, (rot_ref, out_ref, lse_ref) = refs[:-3], refs[-3:]
    width = q_ref.shape[1] // heads
    scale = width ** (-0.5)
    rotated = []
    for h, q in enumerate(heads_of(q_ref[...], heads)):
        n = q * inverse_rms(q) * gain_ref[...]
        rot = ((n * cos_ref[...] + turn(n) * sin_ref[...]) * scale).astype(LOW)
        rot_ref[:, h * width : (h + 1) * width] = rot
        rotated.append(rot)
    rows = jnp.concatenate(rotated, axis=0)
    keys, vals = key_rows(kv_refs, width)
    bias = jnp.where(mask_of(qinfo_ref, kinfo_ref), 0.0, MASKED)
    allowed = jnp.concatenate([bias] * heads, axis=0) == 0.0
    scores = jnp.where(allowed, mm_t(rows, keys), MASKED)
    top = jnp.max(scores, axis=1, keepdims=True)
    expos = jnp.exp(scores - top)
    total = jnp.sum(expos, axis=1, keepdims=True)
    lse_ref[0] = top + jnp.log(total)
    probs = (expos / total).astype(LOW)
    attended = mm(probs, vals).astype(LOW)
    count = q_ref.shape[0]
    for h in range(heads):
        out_ref[:, h * width : (h + 1) * width] = attended[h * count : (h + 1) * count]


def attend_back_kernel(heads, chunks, blocks, place_ref, qinfo_ref, kinfo_ref, q_ref, gain_ref, cos_ref, sin_ref, rot_ref, lse_ref,
                       dout_ref, *refs):
    far_count = (blocks - 1) * chunks
    kv_refs, (dq_ref, dgain_ref), dkv_refs = refs[: far_count + 1], refs[far_count + 1 : far_count + 3], refs[far_count + 3 :]
    width = q_ref.shape[1] // heads
    scale = width ** (-0.5)
    count = q_ref.shape[0]
    rows = jnp.concatenate(heads_of(rot_ref[...], heads), axis=0)
    douts = jnp.concatenate(heads_of(dout_ref[...], heads), axis=0)
    keys, vals = key_rows(kv_refs, width)
    bias = jnp.where(mask_of(qinfo_ref, kinfo_ref), 0.0, MASKED)
    allowed = jnp.concatenate([bias] * heads, axis=0) == 0.0
    probs = jnp.where(allowed, jnp.exp(mm_t(rows, keys) - lse_ref[0]), 0.0)
    d_probs = mm_t(douts, vals)
    delta = jnp.sum(probs * d_probs, axis=1, keepdims=True)
    d_scores = (probs * (d_probs - delta)).astype(LOW)
    d_rows = mm(d_scores, keys)
    d_keys = t_mm(d_scores, rows)
    d_vals = t_mm(probs.astype(LOW), douts)
    per = kv_refs[0].shape[2]
    own_ref, side_refs, middle_refs = dkv_refs[0], dkv_refs[1:chunks], dkv_refs[chunks:]
    for part, at in ((d_keys, 0), (d_vals, width)):
        piece = lambda b, p: part[(b * chunks + p) * per : (b * chunks + p + 1) * per]
        for b in range(blocks):
            own_ref[b, 0, :, at : at + width] = piece(b, 0)
        for p in range(1, chunks):
            earlier = (place_ref[0] ^ p) < place_ref[0]
            for b in range(1, blocks - 1):
                middle_refs[p - 1][b - 1, 0, :, at : at + width] = piece(b, p).astype(LOW)
            side_refs[p - 1][0, :, at : at + width] = jnp.where(earlier, piece(0, p), piece(blocks - 1, p)).astype(LOW)
    gain_sum = jnp.zeros((1, width), F32)
    for h, q in enumerate(heads_of(q_ref[...], heads)):
        e = d_rows[h * count : (h + 1) * count] * scale
        e = e * cos_ref[...] + turn_back(e * sin_ref[...])
        d_q, d_g = rms_back(e, q, inverse_rms(q), gain_ref[...])
        gain_sum = gain_sum + column_sum(d_g)
        dq_ref[:, h * width : (h + 1) * width] = d_q.astype(LOW)
    dgain_ref[0] = gain_sum


def pair_sum_kernel(*refs):
    out = refs[-1]
    for i in range(out.shape[0]):
        out[i] = (refs[2 * i][...].astype(F32) + refs[2 * i + 1][...].astype(F32)).astype(LOW)


def pair_sum(*pairs):
    rows, width = pairs[0][0].shape
    step = rows // 4 if rows % 64 == 0 else rows
    arrays = [v for pair in pairs for v in pair]
    return pl.pallas_call(
        pair_sum_kernel,
        grid=(rows // step,),
        in_specs=[pl.BlockSpec((step, width), lambda j: (j, 0))] * len(arrays),
        out_specs=pl.BlockSpec((len(pairs), step, width), lambda j: (0, j, 0)),
        out_shape=struct((len(pairs), rows, width), LOW),
        compiler_params=ALL,
        name="pair_sum",
    )(*arrays)


def attention_specs(seqs, rows, spans, chunks, wide, width):
    whole = lambda *shape: pl.BlockSpec(shape, lambda s: (0,) * len(shape))
    return dict(
        qinfo=pl.BlockSpec((1, rows, 2), lambda s: (s, 0, 0)),
        kinfo=pl.BlockSpec((1, 2, spans), lambda s: (s, 0, 0)),
        q=pl.BlockSpec((rows, wide), lambda s: (s, 0)),
        gain=whole(1, width),
        table=whole(rows, width),
        own=pl.BlockSpec((chunks, 1, rows, 2 * width), lambda s: (0, s, 0, 0)),
        far=pl.BlockSpec((1, rows, 2 * width), lambda s: (s, 0, 0)),
        lse=pl.BlockSpec((1, rows * (wide // width), 1), lambda s: (s, 0, 0)),
        dgain=pl.BlockSpec((1, 1, width), lambda s: (s, 0, 0)),
    )


def mix_kernel(att_ref, out_ref, x_ref, gain_attn_ref, gain_ffn_ref, branch_ref, hidden_ref, ffn_ref):
    branch = mm_t(att_ref[...], out_ref[...])
    branch_ref[...] = branch
    hidden = x_ref[...].astype(F32) + branch * inverse_rms(branch) * gain_attn_ref[...]
    hidden_ref[...] = hidden
    ffn_ref[...] = (hidden * inverse_rms(hidden) * gain_ffn_ref[...]).astype(LOW)


def for_blocks(width, step, block):
    full, rest = divmod(width, step)

    @pl.when(pl.program_id(0) < full)
    def _():
        block(step)

    if rest:

        @pl.when(pl.program_id(0) == full)
        def _():
            block(rest)


def ffn_kernel(units, chunks, *refs):
    rows_refs, (gate_ref, up_ref, down_ref) = refs[:chunks], refs[chunks : chunks + 3]
    part_refs, (act_ref, slope_ref, curve_ref, sums) = refs[chunks + 3 : 2 * chunks + 3], refs[2 * chunks + 3 :]

    @pl.when(pl.program_id(0) == 0)
    def _():
        sums[...] = jnp.zeros_like(sums)

    def block(size):
        rows = jnp.concatenate([r[...] for r in rows_refs], axis=0)
        gate, up = mm(rows, gate_ref[0, :, :size]), mm(rows, up_ref[0, :, :size])
        root = (2.0 / math.pi) ** 0.5
        square = gate * gate
        bend = jnp.tanh(root * (gate + 0.044715 * (square * gate)))
        share = 0.5 * (1.0 + bend)
        curve = gate * share
        slope = share + 0.5 * gate * (1.0 - bend * bend) * (root * (1.0 + 3.0 * 0.044715 * square))
        act = (curve * up).astype(LOW)
        act_ref[:, :size] = act
        slope_ref[:, :size] = (slope * up).astype(LOW)
        curve_ref[:, :size] = curve.astype(LOW)
        sums[...] += mm_t(act, down_ref[0, :, :size])

    for_blocks(units, act_ref.shape[1], block)
    split_rows(sums, part_refs)


def split_rows(sums, part_refs):
    @pl.when(pl.program_id(0) == pl.num_programs(0) - 1)
    def _():
        count = part_refs[0].shape[0]
        for p, part in enumerate(part_refs):
            part[...] = sums[p * count : (p + 1) * count].astype(part.dtype)


def ffn_back_kernel(units, chunks, *refs):
    rows_refs, (gate_ref, up_ref, down_ref, slope_ref, curve_ref) = refs[:chunks], refs[chunks : chunks + 5]
    part_refs, (dgate_ref, dup_ref, sums) = refs[chunks + 5 : 2 * chunks + 5], refs[2 * chunks + 5 :]

    @pl.when(pl.program_id(0) == 0)
    def _():
        sums[...] = jnp.zeros_like(sums)

    def block(size):
        rows = jnp.concatenate([r[...] for r in rows_refs], axis=0)
        d_act = mm(rows, down_ref[0, :, :size])
        d_gate = (d_act * slope_ref[:, :size].astype(F32)).astype(LOW)
        d_up = (d_act * curve_ref[:, :size].astype(F32)).astype(LOW)
        dgate_ref[:, :size] = d_gate
        dup_ref[:, :size] = d_up
        sums[...] += mm_t(d_gate, gate_ref[0, :, :size]) + mm_t(d_up, up_ref[0, :, :size])

    for_blocks(units, dgate_ref.shape[1], block)
    split_rows(sums, part_refs)


def ffn_call(kernel, name, rows, weights, saved, results, dtype, step=640):
    chunks = len(rows)
    count, width = rows[0].shape
    units = weights.shape[2]
    whole = pl.BlockSpec((count, width), lambda j: (0, 0))
    strip = pl.BlockSpec((chunks * count, step), lambda j: (0, j))
    flat = pl.pallas_call(
        functools.partial(kernel, units, chunks),
        grid=(pl.cdiv(units, step),),
        in_specs=[whole] * chunks
        + [pl.BlockSpec((1, width, step), lambda j, i=i: (i, 0, j)) for i in range(3)]
        + [strip] * len(saved),
        out_specs=[whole] * chunks + [strip] * results,
        out_shape=[struct((count, width), dtype)] * chunks + [struct((chunks * count, units), LOW)] * results,
        scratch_shapes=[pltpu.VMEM((chunks * count, width), F32)],
        compiler_params=ALL,
        cost_estimate=cost(3 * chunks * count * width * units, *rows, weights, *saved),
        name=name,
    )(*rows, weights, weights, weights, *saved)
    return flat[:chunks], flat[chunks:]


def loss_kernel(factor_ref, hidden_ref, target_ref, valid_ref, gain_ref, *refs):
    parts, (out_ref, dres_ref, dffn_ref, dgain_ref, error_ref) = refs[:-5], refs[-5:]
    ffn = sum(r[...].astype(F32) for r in parts)
    inverse = inverse_rms(ffn)
    result = hidden_ref[...] + ffn * inverse * gain_ref[...]
    out_ref[...] = result.astype(LOW)
    mismatch = result - target_ref[...].astype(F32)
    marked = valid_ref[...] * mismatch
    error_ref[...] = jnp.broadcast_to(column_sum(jnp.sum(marked * mismatch, axis=1, keepdims=True)), error_ref.shape)
    d_result = factor_ref[0] * marked
    dres_ref[...] = d_result
    d_ffn, d_gain = rms_back(d_result, ffn, inverse, gain_ref[...])
    dffn_ref[...] = d_ffn.astype(LOW)
    dgain_ref[...] = column_sum(d_gain)


def middle_kernel(dres_ref, hidden_ref, branch_ref, out_ref, gain_ffn_ref, gain_attn_ref, *refs):
    parts, (dhid_ref, dbranch_ref, datt_ref, dgain_ffn_ref, dgain_attn_ref) = refs[:-5], refs[-5:]
    d_ffn_in = sum(r[...].astype(F32) for r in parts)
    hidden = hidden_ref[...]
    d_add, d_gain = rms_back(d_ffn_in, hidden, inverse_rms(hidden), gain_ffn_ref[...])
    dgain_ffn_ref[...] = column_sum(d_gain)
    d_hidden = dres_ref[...] + d_add
    dhid_ref[...] = d_hidden
    branch = branch_ref[...]
    d_branch, d_gain = rms_back(d_hidden, branch, inverse_rms(branch), gain_attn_ref[...])
    dgain_attn_ref[...] = column_sum(d_gain)
    low = d_branch.astype(LOW)
    dbranch_ref[...] = low
    datt_ref[...] = mm(low, out_ref[...]).astype(LOW)


def pull_kernel(left_ref, right_ref, out_ref):
    out_ref[...] = mm_t(left_ref[...], right_ref[...])


def finish_kernel(core_ref, raw_ref, cos_ref, sin_ref, gain_key_ref, pulled_ref, kv_ref, dhid_ref, x_ref, gain_ref, normed_ref, *refs):
    parts, (din_ref, dgain_ref, dgain_key_ref, send_ref, own_ref, sums) = refs[:-6], refs[-6:]
    head = raw_ref.shape[1]
    d_kv = sum(r[...].astype(F32) for r in parts)
    key = raw_ref[...]
    e = d_kv[:, :head]
    e = e * cos_ref[...] + turn_back(e * sin_ref[...])
    d_key, d_gain = rms_back(e, key, inverse_rms(key), gain_key_ref[...])
    dgain_key_ref[...] = column_sum(d_gain)
    low = jnp.concatenate([d_key.astype(LOW), d_kv[:, head:].astype(LOW)], axis=1)
    sums[...] = mm(normed_ref[...].T, low)
    half = own_ref.shape[0]
    core = core_ref[0]
    own_ref[...] = sums[pl.ds(pl.multiple_of(core * half, half), half), :].astype(LOW)
    send_ref[...] = sums[pl.ds(pl.multiple_of((1 - core) * half, half), half), :].astype(LOW)
    d_normed = pulled_ref[...] + mm_t(low, kv_ref[...])
    x = x_ref[...].astype(F32)
    d_x, d_gain = rms_back(d_normed, x, inverse_rms(x), gain_ref[...])
    dgain_ref[...] = column_sum(d_gain)
    din_ref[...] = dhid_ref[...] + d_x


def weight_grad_kernel(chunks, sets, core_ref, *refs):
    lefts, refs = refs[:chunks], refs[chunks:]
    rights, refs = refs[: chunks * sets], refs[chunks * sets :]
    outs, turned = refs[: 2 * sets], refs[2 * sets]
    rows = lefts[0].shape[0]
    half = outs[0].shape[0]

    @pl.when(pl.program_id(0) == 0)
    def _():
        for p in range(chunks):
            turned[:, p * rows : (p + 1) * rows] = lefts[p][...].T

    core = core_ref[0]
    for i in range(sets):
        right = jnp.concatenate([r[...] for r in rights[i * chunks : (i + 1) * chunks]], axis=0)
        for place, out in ((1 - core, outs[2 * i]), (core, outs[2 * i + 1])):
            out[...] = mm(turned[pl.ds(pl.multiple_of(place * half, half), half), :], right).astype(LOW)


def weight_grad(core, rows, lefts, *rights):
    chunks, sets = len(lefts), len(rights)
    step = 896 if sets == 1 and rights[0][0][0].shape[1] > 1024 else 256
    height = lefts[0][0].shape[1]
    width = rights[0][0][0].shape[1]
    rights = [pair for group in rights for pair in group]
    out = pl.BlockSpec((height // 2, step), lambda j: (0, j))
    flat = pl.pallas_call(
        functools.partial(weight_grad_kernel, chunks, sets),
        grid=(pl.cdiv(width, step),),
        in_specs=[SMEM]
        + [pl.BlockSpec((rows, height), lambda j, at=at: (at, 0)) for _, at in lefts]
        + [pl.BlockSpec((rows, step), lambda j, at=at: (at, j)) for _, at in rights],
        out_specs=[out] * (2 * sets),
        out_shape=[struct((height // 2, width), LOW)] * (2 * sets),
        scratch_shapes=[pltpu.VMEM((height, chunks * rows), LOW)],
        compiler_params=ALL,
        cost_estimate=None if width < height else cost(sets * chunks * rows * height * width, *[v for v, _ in lefts], struct((height, sets * width), LOW)),
        name="weight_grad",
    )(core.reshape(1), *[v for v, _ in lefts], *[v for v, _ in rights])
    return [flat[2 * i : 2 * i + 2] for i in range(sets)]


def shards(inputs, target, segment_ids, w_query, w_key, w_value, w_out, w_gate, w_up, w_down,
           gain_input, gain_query, gain_key, gain_post_attn, gain_pre_ffn, gain_post_ffn):
    F, C, T = (lax.axis_size(a) for a in ("fsdp", "ctx", "tp"))
    f, z, t = (lax.axis_index(a) for a in ("fsdp", "ctx", "tp"))
    me = f * C + z
    seqs, block_rows, width_model = inputs.shape
    piece = w_query.shape[0]
    head_width = w_key.shape[1]
    gain_piece = gain_query.shape[0]
    sub = block_rows // T
    own = seqs * sub
    half = C * piece
    halo = -(-(WIN - 1) // block_rows)
    spans = (halo + 1) * block_rows

    both = 2 * head_width
    blocks = jnp.stack([jnp.concatenate([w_query, w_out.T], axis=1), jnp.concatenate([w_key, w_value], axis=1)])
    near = lax.all_gather(blocks, "ctx", axis=1, tiled=True)
    weights = lax.all_gather(jnp.stack([w_gate, w_up, w_down.T]), ("fsdp", "ctx"), axis=1, tiled=True)
    packed = jnp.concatenate(
        [gain_input, gain_post_attn, gain_pre_ffn, gain_post_ffn, gain_query, gain_key, segment_ids.astype(LOW).reshape(-1)]
    )
    packed = exchange(jnp.broadcast_to(packed[None], (F * C, packed.shape[0])), ("fsdp", "ctx")).astype(F32)
    at = 4 * piece
    g_input, g_post_attn, g_pre_ffn, g_post_ffn = [
        packed[:, i * piece : (i + 1) * piece].reshape(1, width_model) for i in range(4)
    ]
    g_query, g_key = [
        packed[:, at + i * gain_piece : at + (i + 1) * gain_piece].reshape(1, head_width) for i in range(2)
    ]
    seg_blocks = packed[:, at + 2 * gain_piece :].astype(jnp.int32)
    count = jnp.sum((seg_blocks != 0).astype(F32))
    normed = norm_rows(t, inputs, g_input, T)
    def sub_rows(values):
        return [lax.dynamic_slice_in_dim(values, (t ^ p) * sub, sub, 1) for p in range(T)]

    x_own = lax.dynamic_slice_in_dim(inputs, t * sub, sub, 1).reshape(own, width_model)
    target_own = lax.dynamic_slice_in_dim(target, t * sub, sub, 1).reshape(own, width_model)
    positions = jnp.concatenate([z * block_rows + (t ^ p) * sub + jnp.arange(sub, dtype=jnp.int32) for p in range(T)])
    segs = [segment_ids + 1]
    for d in range(1, halo + 1):
        far = lax.dynamic_index_in_dim(seg_blocks, jnp.maximum(me - d, 0), 0, False).reshape(seqs, block_rows)
        segs.append(jnp.where(z >= d, far + 1, 0))
    key_seg = jnp.concatenate([v for seg in segs for v in sub_rows(seg)], axis=1)
    key_pos = jnp.concatenate([positions - d * block_rows for d in range(halo + 1)])
    kinfo = jnp.stack([jnp.broadcast_to(key_pos, (seqs, spans)), key_seg], axis=1)
    qinfo = jnp.stack([jnp.broadcast_to(positions[:sub], (seqs, sub)), key_seg[:, :sub]], axis=2)
    valid_own = (key_seg[:, :sub] != 1).astype(F32).reshape(own, 1)
    cos_all, sin_all = rotary_tables(positions, head_width)
    cos_own, sin_own = cos_all[:sub], sin_all[:sub]

    ready = (normed, kinfo, qinfo, cos_all, sin_all, cos_own, sin_own, g_query, g_key, g_post_attn, g_pre_ffn, x_own)
    (near, *ready) = lax.optimization_barrier((near,) + ready)
    normed, kinfo, qinfo, cos_all, sin_all, cos_own, sin_own, g_query, g_key, g_post_attn, g_pre_ffn, x_own = ready
    near_qo, near_kv = near
    far_kv = swap(near_kv, "fsdp", 1)
    near_qo = [near_qo] + [swap(near_qo, "tp", p) for p in range(1, T)]
    pair, first, key_own, kv_full = project_keys(f, normed.reshape(T, seqs, sub, width_model), near_kv, far_kv, g_key, cos_all, sin_all)
    q_full, out_full = assemble(f, near_qo, [swap(after(v, first), "fsdp", 1) for v in near_qo])
    kv_rows, far = [pair], first
    for d in range(halo):
        far = shifted(far, "ctx", 1)
        kv_rows += [swap(far, "tp", p) if p else far for p in range(T)]
    normed_own = normed[:own]
    q_raw = mm(normed_own, q_full)
    wide = q_raw.shape[1]
    heads = wide // head_width
    specs = attention_specs(seqs, sub, spans, T, wide, head_width)
    kv_specs = [specs["own"]] + [specs["far"]] * (halo * T)
    q_rot, attended, lse = pl.pallas_call(
        functools.partial(attend_kernel, heads),
        grid=(seqs,),
        in_specs=[specs[k] for k in ("qinfo", "kinfo", "q", "gain", "table", "table")] + kv_specs,
        out_specs=[specs["q"], specs["q"], specs["lse"]],
        out_shape=[struct((own, wide), LOW), struct((own, wide), LOW), struct((seqs, sub * heads, 1), F32)],
        compiler_params=ROOM,
        cost_estimate=cost(4 * own * spans * wide // seqs, *kv_rows, q_raw),
        name="attend",
    )(qinfo, kinfo, q_raw, g_query, cos_own, sin_own, *kv_rows)
    token = struct((own, width_model), F32)
    token_low = struct((own, width_model), LOW)
    gain_row = struct((1, width_model), F32)
    branch, hidden, ffn_in = pl.pallas_call(
        mix_kernel, out_shape=[token, token, token_low], compiler_params=ROOM, cost_estimate=cost(own * wide * width_model, out_full, out_full), name="mix"
    )(attended, out_full, x_own, g_post_attn, g_pre_ffn)

    from_tp = lambda parts: parts[:1] + [swap(v, "tp", p) for p, v in enumerate(parts) if p]
    ffn_ins = from_tp([ffn_in] * T)
    groups = [[0], [1], list(range(2, T))]
    place = {p: (g, i) for g, group in enumerate(groups) for i, p in enumerate(group)}
    done = [ffn_call(ffn_kernel, "ffn", [ffn_ins[p] for p in group], weights, (), 3, LOW if g else F32) for g, group in enumerate(groups)]
    parts = [done[place[p][0]][0][place[p][1]] for p in range(T)]
    acts, slopes, curves = zip(*[results for _, results in done])
    acts = [(acts[place[p][0]], place[p][1]) for p in range(T)]
    all_tokens = seqs * block_rows * F * C
    output, d_result, d_ffn_low, dg_post_ffn, error = pl.pallas_call(
        loss_kernel,
        in_specs=[SMEM] + [VMEM] * (4 + T),
        out_shape=[token_low, token, token_low, gain_row, struct((1, 128), F32)],
        compiler_params=ALL,
        cost_estimate=cost(own, *parts, *parts),
        name="loss",
    )((all_tokens / count).reshape(1), hidden, target_own, valid_own, g_post_ffn, *from_tp(parts))

    def collect_core(send, mine, *earlier):
        other = swap(send, "fsdp", 1)
        return mine.astype(F32) + (after(other, *earlier) if earlier else other).astype(F32)

    def scatter_ctx(sums):
        return lax.psum_scatter(sums, "ctx", scatter_dimension=1, tiled=True).astype(F32)

    d_outs = from_tp([d_ffn_low] * T)
    done = []
    for g, group in enumerate(groups):
        rows = [d_outs[p] for p in group]
        if g == 1:
            rows[0] = after(rows[0], done[0][0][0])
        if g == 2:
            rows[0] = after(rows[0], done[1][0][0])
        done.append(ffn_call(ffn_back_kernel, "ffn_back", rows, weights, (slopes[g], curves[g]), 2, LOW if g else F32))
    last = done[-1][0][-1]
    (down_halves,) = weight_grad(f, own, [(v if p else after(v, last), 0) for p, v in enumerate(d_outs)], acts)
    down_sum = pair_sum((down_halves[1], swap(down_halves[0], "fsdp", 1)))
    (grad_down,) = scatter_ctx(down_sum)
    parts = [done[place[p][0]][0][place[p][1]] for p in range(T)]
    d_gates, d_ups = [[(done[place[p][0]][1][i], place[p][1]) for p in range(T)] for i in range(2)]
    first_in = after(ffn_ins[0], down_sum)
    gate_halves, up_halves = weight_grad(f, own, [(v, 0) for v in [first_in] + ffn_ins[1:]], d_gates, d_ups)

    parts = [after(v, *gate_halves, *up_halves) if p == 0 else v for p, v in enumerate(from_tp(parts))]
    d_hidden, d_branch, d_attended, dg_pre_ffn, dg_post_attn = pl.pallas_call(
        middle_kernel,
        out_shape=[token, token_low, struct((own, wide), LOW), gain_row, gain_row],
        compiler_params=ALL,
        cost_estimate=cost(300 * own * wide * width_model, out_full),
        name="middle",
    )(d_result, hidden, branch, out_full, g_pre_ffn, g_post_attn, *parts)
    assert halo * block_rows == WIN
    others = [after(swap(after(v[0], *parts[1:]), "fsdp", 1), d_branch) for v in (gate_halves, up_halves)]
    both_sums = pair_sum((gate_halves[1], others[0]), (up_halves[1], others[1]))
    grad_gate, grad_up = scatter_ctx(both_sums)
    d_attended = after(d_attended, both_sums)
    (out_halves,) = weight_grad(f, own, [(d_branch, 0)], [(attended, 0)])
    out_sum = collect_core(*out_halves)
    out_low = out_sum.astype(LOW)
    d_attended = after(d_attended, *out_halves)
    d_query, dg_query, *d_pairs = pl.pallas_call(
        functools.partial(attend_back_kernel, heads, T, halo + 1),
        grid=(seqs,),
        in_specs=[SMEM] + [specs[k] for k in ("qinfo", "kinfo", "q", "gain", "table", "table", "q", "lse", "q")] + kv_specs,
        out_specs=[specs["q"], specs["dgain"]]
        + [pl.BlockSpec((halo + 1, 1, sub, 2 * head_width), lambda s: (0, s, 0, 0))]
        + [specs["far"]] * (T - 1)
        + [pl.BlockSpec((halo - 1, 1, sub, 2 * head_width), lambda s: (0, s, 0, 0))] * (T - 1),
        out_shape=[struct((own, wide), LOW), struct((seqs, 1, head_width), F32), struct((halo + 1, seqs, sub, 2 * head_width), F32)]
        + [struct((seqs, sub, 2 * head_width), LOW)] * (T - 1)
        + [struct((halo - 1, seqs, sub, 2 * head_width), LOW)] * (T - 1),
        compiler_params=ALL,
        name="attend_back",
    )(t.reshape(1), qinfo, kinfo, q_raw, g_query, cos_own, sin_own, q_rot, lse, d_attended, *kv_rows)
    d_own = after(d_pairs[0], out_low)
    d_blocks = [d_own[b] for b in range(halo + 1)]
    for p in range(1, T):
        got = swap(d_pairs[p], "tp", p).astype(F32)
        later = (t ^ p) > t
        d_blocks[0] = d_blocks[0] + jnp.where(later, got, 0.0)
        d_blocks[halo] = d_blocks[halo] + jnp.where(later, 0.0, got)
    d_kv = d_blocks[halo].astype(LOW)
    for p in range(1, T):
        middle = swap(after(d_pairs[T - 1 + p], d_kv), "tp", p)
        for b in range(1, halo):
            d_blocks[b] = d_blocks[b] + middle[b - 1].astype(F32)
    d_query_late, out_low = after(d_query, middle), after(out_low, middle)
    for d in range(halo, 0, -1):
        come = shifted(d_kv, "ctx", -1)
        if d > 1:
            d_kv = (d_blocks[d - 1] + come.astype(F32)).astype(LOW)
    d_kv = [d_blocks[0], come]
    head = lambda v, p: v[:, p * head_width : (p + 1) * head_width]
    heads_sent = [jnp.concatenate([head(d_query_late, p), head(out_low, p)], axis=0) for p in range(1, T)]
    heads_here = [swap(v, "tp", p + 1) for p, v in enumerate(heads_sent)]
    out_head = head(out_sum, 0)
    for v in heads_here:
        out_head = out_head + v[own:].astype(F32)
    normed_late = after(normed, come)
    (q_halves,) = weight_grad(f, own, [(normed_late, p) for p in range(T)], [(head(d_query, 0), 0)] + [(v, 0) for v in heads_here])
    pulled = pl.pallas_call(
        pull_kernel, out_shape=token, compiler_params=ROOM, name="pull"
    )(d_query, q_full)

    def pack(values, wide):
        top = lax.reduce_precision(values, 8, 7)
        flat = jnp.concatenate([top, values - top], axis=1).astype(LOW)
        rows = -(-flat.shape[1] // wide)
        return jnp.pad(flat, ((0, 0), (0, rows * wide - flat.shape[1]))).reshape(values.shape[0], rows, wide)

    def unpack(rows, n):
        flat = rows.reshape(-1)
        return flat[:n] + flat[n : 2 * n]

    def core_rows(values):
        rows = jnp.concatenate([v.reshape(F * C, -1) for v in values], axis=1).reshape(F, C, -1)
        return lax.dynamic_index_in_dim(rows, f, 0, False) + swap(lax.dynamic_index_in_dim(rows, f ^ 1, 0, False), "fsdp", 1)

    def owner_sums(weight_sums, rows):
        wide = weight_sums.shape[1]
        sent = jnp.concatenate([weight_sums.reshape(C, piece, wide), pack(rows, wide)], axis=1)
        sums = jnp.sum(exchange(sent, "ctx").astype(F32), axis=0)
        return sums[:piece], unpack(sums[piece:], rows.shape[1])

    early = core_rows(
        [dg_post_attn, dg_pre_ffn, dg_post_ffn, jnp.sum(dg_query, axis=(0, 1)), jnp.broadcast_to(error[:, :1], (F * C, 1))]
    )
    both_heads = jnp.concatenate([collect_core(*q_halves).astype(LOW), out_head.astype(LOW)], axis=1)
    d_kv[0] = after(d_kv[0], both_heads, pulled)
    own_rows = lambda table: jnp.tile(table, (seqs, 1))
    grad_input, dg_input, dg_key, *kv_halves = pl.pallas_call(
        finish_kernel,
        in_specs=[SMEM] + [VMEM] * (10 + len(d_kv)),
        out_shape=[token, gain_row, struct((1, head_width), F32)] + [struct((half, 2 * head_width), LOW)] * 2,
        scratch_shapes=[pltpu.VMEM((2 * half, 2 * head_width), F32)],
        compiler_params=ROOM,
        name="finish",
    )(f.reshape(1), key_own, own_rows(cos_own), own_rows(sin_own), g_key, pulled, kv_full, d_hidden, x_own, g_input,
      normed_own, *[v.reshape(own, 2 * head_width) for v in d_kv])
    late = core_rows([dg_input, dg_key])
    sums = jnp.concatenate([both_heads, collect_core(*kv_halves).astype(LOW)], axis=1)
    sums, total = owner_sums(sums, jnp.concatenate([early, late], axis=1))
    grad_query, grad_out = sums[:, :head_width], sums[:, head_width : 2 * head_width]
    grad_kv = sums[:, 2 * head_width :]
    low = jnp.concatenate([grad_kv.astype(LOW), pack(total[None], 2 * head_width)[0]], axis=0)
    low, grad_gate, grad_up, grad_down = lax.optimization_barrier((low, grad_gate, grad_up, grad_down))
    totals = {p: (swap(low, "tp", p) if p else low).astype(F32) for p in range(T)}
    bit = 1
    while bit < T:
        totals = {p: totals[p] + totals[p ^ bit] for p in totals if not p & bit}
        bit *= 2
    grad_kv, total = totals[0][:piece], unpack(totals[0][piece:], total.shape[0])
    early, late = total[: early.shape[1]], total[early.shape[1] :]
    loss = early[-1] / (2.0 * width_model * count)
    at = 3 * piece
    return (
        output.reshape(seqs, sub, width_model),
        loss,
        grad_input.reshape(seqs, sub, width_model),
        grad_query,
        grad_kv[:, :head_width],
        grad_kv[:, head_width:],
        grad_out.T,
        grad_gate,
        grad_up,
        grad_down.T,
        late[:piece],
        early[at : at + gain_piece],
        late[piece:],
        early[:piece],
        early[piece : 2 * piece],
        early[2 * piece : at],
    )


def solution(mesh):
    rows = P(("fsdp", "ctx"), "tp")
    cols = P("tp", ("fsdp", "ctx"))
    split = P(("fsdp", "ctx"), None)
    gain = P(("fsdp", "ctx"))
    token = P("fsdp", "ctx", None)
    own = P("fsdp", ("ctx", "tp"), None)
    weights = (rows, split, split, cols, rows, rows, cols)
    return jax.shard_map(
        shards,
        mesh=mesh,
        in_specs=(token, token, P("fsdp", "ctx")) + weights + (gain,) * 6,
        out_specs=(own, P(), own) + weights + (gain,) * 6,
        check_vma=False,
    )
```

```python
import functools
import math

import jax
import jax.numpy as jnp
from jax import lax
from jax.experimental import pallas as pl
from jax.experimental.pallas import tpu as pltpu
from jax.sharding import PartitionSpec as P

WIN = 512
EPS = 1e-06
MASKED = -1e30
LOW = jnp.bfloat16
F32 = jnp.float32


def swap(values, axis, bits):
    return lax.ppermute(values, axis, [(i, i ^ bits) for i in range(lax.axis_size(axis))])


def shifted(values, axis, by):
    size = lax.axis_size(axis)
    return lax.ppermute(values, axis, [(i, i + by) for i in range(size) if 0 <= i + by < size])


def exchange(values, axes):
    return lax.all_to_all(values, axes, 0, 0, tiled=True)


def after(value, *earlier):
    return lax.optimization_barrier((value,) + earlier)[0]


def dot(left, right, contract):
    return lax.dot_general(left, right, (contract, ((), ())), preferred_element_type=F32)


def mm(left, right):
    return dot(left, right, ((1,), (0,)))


def mm_t(left, right):
    return dot(left, right, ((1,), (1,)))


def t_mm(left, right):
    return dot(left, right, ((0,), (0,)))


def inverse_rms(values):
    return lax.rsqrt(jnp.mean(values * values, axis=-1, keepdims=True) + EPS)


def rms_back(grad, values, inverse, gain_row):
    n = values * inverse
    eg = grad * gain_row
    return inverse * (eg - n * jnp.mean(eg * n, axis=-1, keepdims=True)), grad * n


def turn(values):
    half = values.shape[-1] // 2
    return jnp.concatenate([-values[..., half:], values[..., :half]], axis=-1)


def turn_back(values):
    half = values.shape[-1] // 2
    return jnp.concatenate([values[..., half:], -values[..., :half]], axis=-1)


def rotary_tables(positions, head_width):
    frequency = 10000.0 ** (-2.0 * jnp.arange(head_width // 2, dtype=F32) / head_width)
    angles = positions.astype(F32)[:, None] * frequency[None, :]
    angles = jnp.concatenate([angles, angles], axis=-1)
    return jnp.cos(angles), jnp.sin(angles)


def heads_of(values, heads):
    width = values.shape[1] // heads
    return [values[:, h * width : (h + 1) * width] for h in range(heads)]


VMEM = pl.BlockSpec(memory_space=pltpu.VMEM)
SMEM = pl.BlockSpec(memory_space=pltpu.SMEM)
ROOM = pltpu.CompilerParams(vmem_limit_bytes=28 * 1024 * 1024)
ALL = pltpu.CompilerParams(vmem_limit_bytes=60 * 1024 * 1024)


def cost(multiply_adds, *arrays):
    moved = sum(math.prod(v.shape) * jnp.dtype(v.dtype).itemsize for v in arrays)
    return pl.CostEstimate(flops=2 * multiply_adds, bytes_accessed=moved, transcendentals=0)


def struct(shape, dtype):
    return jax.ShapeDtypeStruct(shape, dtype)


def column_sum(values):
    return jnp.sum(values, axis=0, keepdims=True)


def assemble_kernel(pieces, core_ref, *refs):
    width = refs[0].shape[1] // 2
    results = refs[2 * pieces :]
    for step in range(2):

        @pl.when(pl.program_id(0) == step)
        def _():
            for i, result in enumerate(results):
                for p in range(pieces):
                    result[0, :, p * width : (p + 1) * width] = refs[step * pieces + p][:, i * width : (i + 1) * width]


def assemble(core, mine, others):
    half, width = mine[0].shape
    pieces = len(mine)
    wide = pieces * width // 2
    out = pl.BlockSpec((1, half, wide), lambda i, core: (i ^ core[0], 0, 0))
    results = pl.pallas_call(
        functools.partial(assemble_kernel, pieces),
        grid_spec=pltpu.PrefetchScalarGridSpec(
            num_scalar_prefetch=1,
            grid=(2,),
            in_specs=[pl.BlockSpec((half, width), lambda i, core: (0, 0))] * (2 * pieces),
            out_specs=[out, out],
        ),
        out_shape=[struct((2, half, wide), LOW)] * 2,
        compiler_params=ROOM,
        cost_estimate=cost(0, *mine, *others, *mine, *others),
        name="assemble",
    )(core.reshape(1), *mine, *others)
    return [v.reshape(2 * half, wide) for v in results]


def norm_rows_kernel(chunks, place_ref, x_ref, gain_ref, out_ref):
    sub = x_ref.shape[1] // chunks
    for p in range(chunks):
        x = x_ref[0, pl.ds(pl.multiple_of((place_ref[0] ^ p) * sub, sub), sub), :].astype(F32)
        out_ref[p, 0] = (x * inverse_rms(x) * gain_ref[...]).astype(LOW)


def norm_rows(place, x, gain_row, chunks):
    seqs, rows, width = x.shape
    sub = rows // chunks
    return pl.pallas_call(
        functools.partial(norm_rows_kernel, chunks),
        grid=(seqs,),
        in_specs=[
            pl.BlockSpec(memory_space=pltpu.SMEM),
            pl.BlockSpec((1, rows, width), lambda s: (s, 0, 0)),
            pl.BlockSpec((1, width), lambda s: (0, 0)),
        ],
        out_specs=pl.BlockSpec((chunks, 1, sub, width), lambda s: (0, s, 0, 0)),
        out_shape=jax.ShapeDtypeStruct((chunks, seqs, sub, width), LOW),
        compiler_params=ROOM,
        cost_estimate=cost(0, x, x, x, x),
        name="norm_rows",
    )(place.reshape(1), x, gain_row).reshape(chunks * seqs * sub, width)


def keys_kernel(core_ref, x_ref, near_ref, far_ref, gain_ref, cos_ref, sin_ref, pair_ref, first_ref, raw_ref, full_ref):
    chunks, _, sub, width = x_ref.shape
    half = near_ref.shape[0]
    head = gain_ref.shape[1]

    @pl.when(pl.program_id(0) == 0)
    def _():
        for place, source in ((core_ref[0], near_ref), (1 - core_ref[0], far_ref)):
            full_ref[pl.ds(pl.multiple_of(place * half, half), half), :] = source[...]

    kv = mm(x_ref[...].reshape(chunks * sub, width), full_ref[...])
    key = kv[:, :head]
    n = key * inverse_rms(key) * gain_ref[...]
    rot = (n * cos_ref[...] + turn(n) * sin_ref[...]).astype(LOW)
    value = kv[:, head:].astype(LOW)
    raw_ref[...] = key[:sub]
    pair_ref[:, 0, :, :head] = rot.reshape(chunks, sub, head)
    pair_ref[:, 0, :, head:] = value.reshape(chunks, sub, head)
    first_ref[0, :, :head] = rot[:sub]
    first_ref[0, :, head:] = value[:sub]


def project_keys(core, normed, near, far, gain_row, cos, sin):
    chunks, seqs, sub, width = normed.shape
    half, both = near.shape
    head = both // 2
    whole = lambda *shape: pl.BlockSpec(shape, lambda s: (0,) * len(shape))
    return pl.pallas_call(
        keys_kernel,
        grid=(seqs,),
        in_specs=[
            SMEM,
            pl.BlockSpec((chunks, 1, sub, width), lambda s: (0, s, 0, 0)),
            whole(half, both),
            whole(half, both),
            whole(1, head),
            whole(chunks * sub, head),
            whole(chunks * sub, head),
        ],
        out_specs=[
            pl.BlockSpec((chunks, 1, sub, both), lambda s: (0, s, 0, 0)),
            pl.BlockSpec((1, sub, both), lambda s: (s, 0, 0)),
            pl.BlockSpec((sub, head), lambda s: (s, 0)),
            whole(2 * half, both),
        ],
        out_shape=[
            struct((chunks, seqs, sub, both), LOW),
            struct((seqs, sub, both), LOW),
            struct((seqs * sub, head), F32),
            struct((2 * half, both), LOW),
        ],
        compiler_params=ROOM,
        cost_estimate=cost(seqs * chunks * sub * width * both, normed, normed),
        name="project_keys",
    )(core.reshape(1), normed, near, far, gain_row, cos, sin)


def mask_of(qinfo_ref, kinfo_ref):
    qpos, qseg = qinfo_ref[0, :, 0:1], qinfo_ref[0, :, 1:2]
    kpos, kseg = kinfo_ref[0, 0:1, :], kinfo_ref[0, 1:2, :]
    return (kseg == qseg) & (kpos <= qpos) & (kpos > qpos - WIN)


def key_rows(kv_refs, width):
    own_ref, *far_refs = kv_refs
    sides = []
    for at in (0, width):
        own = own_ref[:, 0, :, at : at + width].reshape(own_ref.shape[0] * own_ref.shape[2], width)
        sides.append(jnp.concatenate([own] + [r[0, :, at : at + width] for r in far_refs], axis=0))
    return sides


def attend_kernel(heads, qinfo_ref, kinfo_ref, q_ref, gain_ref, cos_ref, sin_ref, *refs):
    kv_refs, (rot_ref, out_ref, lse_ref) = refs[:-3], refs[-3:]
    width = q_ref.shape[1] // heads
    scale = width ** (-0.5)
    rotated = []
    for h, q in enumerate(heads_of(q_ref[...], heads)):
        n = q * inverse_rms(q) * gain_ref[...]
        rot = ((n * cos_ref[...] + turn(n) * sin_ref[...]) * scale).astype(LOW)
        rot_ref[:, h * width : (h + 1) * width] = rot
        rotated.append(rot)
    rows = jnp.concatenate(rotated, axis=0)
    keys, vals = key_rows(kv_refs, width)
    bias = jnp.where(mask_of(qinfo_ref, kinfo_ref), 0.0, MASKED)
    allowed = jnp.concatenate([bias] * heads, axis=0) == 0.0
    scores = jnp.where(allowed, mm_t(rows, keys), MASKED)
    top = jnp.max(scores, axis=1, keepdims=True)
    expos = jnp.exp(scores - top)
    total = jnp.sum(expos, axis=1, keepdims=True)
    lse_ref[0] = top + jnp.log(total)
    probs = (expos / total).astype(LOW)
    attended = mm(probs, vals).astype(LOW)
    count = q_ref.shape[0]
    for h in range(heads):
        out_ref[:, h * width : (h + 1) * width] = attended[h * count : (h + 1) * count]


def attend_back_kernel(heads, chunks, blocks, place_ref, qinfo_ref, kinfo_ref, q_ref, gain_ref, cos_ref, sin_ref, rot_ref, lse_ref,
                       dout_ref, *refs):
    far_count = (blocks - 1) * chunks
    kv_refs, (dq_ref, dgain_ref), dkv_refs = refs[: far_count + 1], refs[far_count + 1 : far_count + 3], refs[far_count + 3 :]
    width = q_ref.shape[1] // heads
    scale = width ** (-0.5)
    count = q_ref.shape[0]
    rows = jnp.concatenate(heads_of(rot_ref[...], heads), axis=0)
    douts = jnp.concatenate(heads_of(dout_ref[...], heads), axis=0)
    keys, vals = key_rows(kv_refs, width)
    bias = jnp.where(mask_of(qinfo_ref, kinfo_ref), 0.0, MASKED)
    allowed = jnp.concatenate([bias] * heads, axis=0) == 0.0
    probs = jnp.where(allowed, jnp.exp(mm_t(rows, keys) - lse_ref[0]), 0.0)
    d_probs = mm_t(douts, vals)
    delta = jnp.sum(probs * d_probs, axis=1, keepdims=True)
    d_scores = (probs * (d_probs - delta)).astype(LOW)
    d_rows = mm(d_scores, keys)
    d_keys = t_mm(d_scores, rows)
    d_vals = t_mm(probs.astype(LOW), douts)
    per = kv_refs[0].shape[2]
    own_ref, side_refs, middle_refs = dkv_refs[0], dkv_refs[1:chunks], dkv_refs[chunks:]
    for part, at in ((d_keys, 0), (d_vals, width)):
        piece = lambda b, p: part[(b * chunks + p) * per : (b * chunks + p + 1) * per]
        for b in range(blocks):
            own_ref[b, 0, :, at : at + width] = piece(b, 0)
        for p in range(1, chunks):
            earlier = (place_ref[0] ^ p) < place_ref[0]
            for b in range(1, blocks - 1):
                middle_refs[p - 1][b - 1, 0, :, at : at + width] = piece(b, p).astype(LOW)
            side_refs[p - 1][0, :, at : at + width] = jnp.where(earlier, piece(0, p), piece(blocks - 1, p)).astype(LOW)
    gain_sum = jnp.zeros((1, width), F32)
    for h, q in enumerate(heads_of(q_ref[...], heads)):
        e = d_rows[h * count : (h + 1) * count] * scale
        e = e * cos_ref[...] + turn_back(e * sin_ref[...])
        d_q, d_g = rms_back(e, q, inverse_rms(q), gain_ref[...])
        gain_sum = gain_sum + column_sum(d_g)
        dq_ref[:, h * width : (h + 1) * width] = d_q.astype(LOW)
    dgain_ref[0] = gain_sum


def pair_sum_kernel(*refs):
    out = refs[-1]
    for i in range(out.shape[0]):
        out[i] = (refs[2 * i][...].astype(F32) + refs[2 * i + 1][...].astype(F32)).astype(LOW)


def pair_sum(*pairs):
    rows, width = pairs[0][0].shape
    step = rows // 4 if rows % 64 == 0 else rows
    arrays = [v for pair in pairs for v in pair]
    return pl.pallas_call(
        pair_sum_kernel,
        grid=(rows // step,),
        in_specs=[pl.BlockSpec((step, width), lambda j: (j, 0))] * len(arrays),
        out_specs=pl.BlockSpec((len(pairs), step, width), lambda j: (0, j, 0)),
        out_shape=struct((len(pairs), rows, width), LOW),
        compiler_params=ALL,
        name="pair_sum",
    )(*arrays)


def attention_specs(seqs, rows, spans, chunks, wide, width):
    whole = lambda *shape: pl.BlockSpec(shape, lambda s: (0,) * len(shape))
    return dict(
        qinfo=pl.BlockSpec((1, rows, 2), lambda s: (s, 0, 0)),
        kinfo=pl.BlockSpec((1, 2, spans), lambda s: (s, 0, 0)),
        q=pl.BlockSpec((rows, wide), lambda s: (s, 0)),
        gain=whole(1, width),
        table=whole(rows, width),
        own=pl.BlockSpec((chunks, 1, rows, 2 * width), lambda s: (0, s, 0, 0)),
        far=pl.BlockSpec((1, rows, 2 * width), lambda s: (s, 0, 0)),
        lse=pl.BlockSpec((1, rows * (wide // width), 1), lambda s: (s, 0, 0)),
        dgain=pl.BlockSpec((1, 1, width), lambda s: (s, 0, 0)),
    )


def mix_kernel(att_ref, out_ref, x_ref, gain_attn_ref, gain_ffn_ref, branch_ref, hidden_ref, ffn_ref):
    branch = mm_t(att_ref[...], out_ref[...])
    branch_ref[...] = branch
    hidden = x_ref[...].astype(F32) + branch * inverse_rms(branch) * gain_attn_ref[...]
    hidden_ref[...] = hidden
    ffn_ref[...] = (hidden * inverse_rms(hidden) * gain_ffn_ref[...]).astype(LOW)


def for_blocks(width, step, block):
    full, rest = divmod(width, step)

    @pl.when(pl.program_id(0) < full)
    def _():
        block(step)

    if rest:

        @pl.when(pl.program_id(0) == full)
        def _():
            block(rest)


def ffn_kernel(units, chunks, *refs):
    rows_refs, (gate_ref, up_ref, down_ref) = refs[:chunks], refs[chunks : chunks + 3]
    part_refs, (act_ref, slope_ref, curve_ref, sums) = refs[chunks + 3 : 2 * chunks + 3], refs[2 * chunks + 3 :]

    @pl.when(pl.program_id(0) == 0)
    def _():
        sums[...] = jnp.zeros_like(sums)

    def block(size):
        rows = jnp.concatenate([r[...] for r in rows_refs], axis=0)
        gate, up = mm(rows, gate_ref[0, :, :size]), mm(rows, up_ref[0, :, :size])
        root = (2.0 / math.pi) ** 0.5
        square = gate * gate
        bend = jnp.tanh(root * (gate + 0.044715 * (square * gate)))
        share = 0.5 * (1.0 + bend)
        curve = gate * share
        slope = share + 0.5 * gate * (1.0 - bend * bend) * (root * (1.0 + 3.0 * 0.044715 * square))
        act = (curve * up).astype(LOW)
        act_ref[:, :size] = act
        slope_ref[:, :size] = (slope * up).astype(LOW)
        curve_ref[:, :size] = curve.astype(LOW)
        sums[...] += mm_t(act, down_ref[0, :, :size])

    for_blocks(units, act_ref.shape[1], block)
    split_rows(sums, part_refs)


def split_rows(sums, part_refs):
    @pl.when(pl.program_id(0) == pl.num_programs(0) - 1)
    def _():
        count = part_refs[0].shape[0]
        for p, part in enumerate(part_refs):
            part[...] = sums[p * count : (p + 1) * count].astype(part.dtype)


def ffn_back_kernel(units, chunks, *refs):
    rows_refs, (gate_ref, up_ref, down_ref, slope_ref, curve_ref) = refs[:chunks], refs[chunks : chunks + 5]
    part_refs, (dgate_ref, dup_ref, sums) = refs[chunks + 5 : 2 * chunks + 5], refs[2 * chunks + 5 :]

    @pl.when(pl.program_id(0) == 0)
    def _():
        sums[...] = jnp.zeros_like(sums)

    def block(size):
        rows = jnp.concatenate([r[...] for r in rows_refs], axis=0)
        d_act = mm(rows, down_ref[0, :, :size])
        d_gate = (d_act * slope_ref[:, :size].astype(F32)).astype(LOW)
        d_up = (d_act * curve_ref[:, :size].astype(F32)).astype(LOW)
        dgate_ref[:, :size] = d_gate
        dup_ref[:, :size] = d_up
        sums[...] += mm_t(d_gate, gate_ref[0, :, :size]) + mm_t(d_up, up_ref[0, :, :size])

    for_blocks(units, dgate_ref.shape[1], block)
    split_rows(sums, part_refs)


def ffn_call(kernel, name, rows, weights, saved, results, dtype, step=640):
    chunks = len(rows)
    count, width = rows[0].shape
    units = weights.shape[2]
    whole = pl.BlockSpec((count, width), lambda j: (0, 0))
    strip = pl.BlockSpec((chunks * count, step), lambda j: (0, j))
    flat = pl.pallas_call(
        functools.partial(kernel, units, chunks),
        grid=(pl.cdiv(units, step),),
        in_specs=[whole] * chunks
        + [pl.BlockSpec((1, width, step), lambda j, i=i: (i, 0, j)) for i in range(3)]
        + [strip] * len(saved),
        out_specs=[whole] * chunks + [strip] * results,
        out_shape=[struct((count, width), dtype)] * chunks + [struct((chunks * count, units), LOW)] * results,
        scratch_shapes=[pltpu.VMEM((chunks * count, width), F32)],
        compiler_params=ALL,
        cost_estimate=cost(3 * chunks * count * width * units, *rows, weights, *saved),
        name=name,
    )(*rows, weights, weights, weights, *saved)
    return flat[:chunks], flat[chunks:]


def loss_kernel(factor_ref, hidden_ref, target_ref, valid_ref, gain_ref, *refs):
    parts, (out_ref, dres_ref, dffn_ref, dgain_ref, error_ref) = refs[:-5], refs[-5:]
    ffn = sum(r[...].astype(F32) for r in parts)
    inverse = inverse_rms(ffn)
    result = hidden_ref[...] + ffn * inverse * gain_ref[...]
    out_ref[...] = result.astype(LOW)
    mismatch = result - target_ref[...].astype(F32)
    marked = valid_ref[...] * mismatch
    error_ref[...] = jnp.broadcast_to(column_sum(jnp.sum(marked * mismatch, axis=1, keepdims=True)), error_ref.shape)
    d_result = factor_ref[0] * marked
    dres_ref[...] = d_result
    d_ffn, d_gain = rms_back(d_result, ffn, inverse, gain_ref[...])
    dffn_ref[...] = d_ffn.astype(LOW)
    dgain_ref[...] = column_sum(d_gain)


def middle_kernel(dres_ref, hidden_ref, branch_ref, out_ref, gain_ffn_ref, gain_attn_ref, *refs):
    parts, (dhid_ref, dbranch_ref, datt_ref, dgain_ffn_ref, dgain_attn_ref) = refs[:-5], refs[-5:]
    d_ffn_in = sum(r[...].astype(F32) for r in parts)
    hidden = hidden_ref[...]
    d_add, d_gain = rms_back(d_ffn_in, hidden, inverse_rms(hidden), gain_ffn_ref[...])
    dgain_ffn_ref[...] = column_sum(d_gain)
    d_hidden = dres_ref[...] + d_add
    dhid_ref[...] = d_hidden
    branch = branch_ref[...]
    d_branch, d_gain = rms_back(d_hidden, branch, inverse_rms(branch), gain_attn_ref[...])
    dgain_attn_ref[...] = column_sum(d_gain)
    low = d_branch.astype(LOW)
    dbranch_ref[...] = low
    datt_ref[...] = mm(low, out_ref[...]).astype(LOW)


def pull_kernel(left_ref, right_ref, out_ref):
    out_ref[...] = mm_t(left_ref[...], right_ref[...])


def finish_kernel(chunks, place_ref, raw_ref, cos_ref, sin_ref, gain_key_ref, pulled_ref, kv_ref, dhid_ref, x_ref, gain_ref, normed_ref, *refs):
    parts, (din_ref, dgain_ref, dgain_key_ref, send_ref, own_ref, sums, turned) = refs[:-7], refs[-7:]
    head = raw_ref.shape[1]
    d_kv = sum(r[...].astype(F32) for r in parts)
    key = raw_ref[...]
    e = d_kv[:, :head]
    e = e * cos_ref[...] + turn_back(e * sin_ref[...])
    d_key, d_gain = rms_back(e, key, inverse_rms(key), gain_key_ref[...])
    dgain_key_ref[...] = column_sum(d_gain)
    low = jnp.concatenate([d_key.astype(LOW), d_kv[:, head:].astype(LOW)], axis=1)
    turned[...] = low
    part = low.shape[1] // chunks
    ordered = [turned[:, pl.ds(pl.multiple_of((place_ref[1] ^ p) * part, part), part)] for p in range(chunks)]
    sums[...] = mm(normed_ref[...].T, jnp.concatenate(ordered, axis=1))
    half = own_ref.shape[0]
    core = place_ref[0]
    own_ref[...] = sums[pl.ds(pl.multiple_of(core * half, half), half), :].astype(LOW)
    send_ref[...] = sums[pl.ds(pl.multiple_of((1 - core) * half, half), half), :].astype(LOW)
    d_normed = pulled_ref[...] + mm_t(low, kv_ref[...])
    x = x_ref[...].astype(F32)
    d_x, d_gain = rms_back(d_normed, x, inverse_rms(x), gain_ref[...])
    dgain_ref[...] = column_sum(d_gain)
    din_ref[...] = dhid_ref[...] + d_x


def weight_grad_kernel(chunks, sets, core_ref, *refs):
    lefts, refs = refs[:chunks], refs[chunks:]
    rights, refs = refs[: chunks * sets], refs[chunks * sets :]
    outs, turned = refs[: 2 * sets], refs[2 * sets]
    rows = lefts[0].shape[0]
    half = outs[0].shape[0]

    @pl.when(pl.program_id(0) == 0)
    def _():
        for p in range(chunks):
            turned[:, p * rows : (p + 1) * rows] = lefts[p][...].T

    core = core_ref[0]
    for i in range(sets):
        right = jnp.concatenate([r[...] for r in rights[i * chunks : (i + 1) * chunks]], axis=0)
        for place, out in ((1 - core, outs[2 * i]), (core, outs[2 * i + 1])):
            out[...] = mm(turned[pl.ds(pl.multiple_of(place * half, half), half), :], right).astype(LOW)


def weight_grad(core, rows, lefts, *rights):
    chunks, sets = len(lefts), len(rights)
    step = 896 if sets == 1 and rights[0][0][0].shape[1] > 1024 else 256
    height = lefts[0][0].shape[1]
    width = rights[0][0][0].shape[1]
    rights = [pair for group in rights for pair in group]
    out = pl.BlockSpec((height // 2, step), lambda j: (0, j))
    flat = pl.pallas_call(
        functools.partial(weight_grad_kernel, chunks, sets),
        grid=(pl.cdiv(width, step),),
        in_specs=[SMEM]
        + [pl.BlockSpec((rows, height), lambda j, at=at: (at, 0)) for _, at in lefts]
        + [pl.BlockSpec((rows, step), lambda j, at=at: (at, j)) for _, at in rights],
        out_specs=[out] * (2 * sets),
        out_shape=[struct((height // 2, width), LOW)] * (2 * sets),
        scratch_shapes=[pltpu.VMEM((height, chunks * rows), LOW)],
        compiler_params=ALL,
        cost_estimate=None if width < height else cost(sets * chunks * rows * height * width, *[v for v, _ in lefts], struct((height, sets * width), LOW)),
        name="weight_grad",
    )(core.reshape(1), *[v for v, _ in lefts], *[v for v, _ in rights])
    return [flat[2 * i : 2 * i + 2] for i in range(sets)]


def shards(inputs, target, segment_ids, w_query, w_key, w_value, w_out, w_gate, w_up, w_down,
           gain_input, gain_query, gain_key, gain_post_attn, gain_pre_ffn, gain_post_ffn):
    F, C, T = (lax.axis_size(a) for a in ("fsdp", "ctx", "tp"))
    f, z, t = (lax.axis_index(a) for a in ("fsdp", "ctx", "tp"))
    me = f * C + z
    seqs, block_rows, width_model = inputs.shape
    piece = w_query.shape[0]
    head_width = w_key.shape[1]
    gain_piece = gain_query.shape[0]
    sub = block_rows // T
    own = seqs * sub
    half = C * piece
    halo = -(-(WIN - 1) // block_rows)
    spans = (halo + 1) * block_rows

    both = 2 * head_width
    blocks = jnp.stack([jnp.concatenate([w_query, w_out.T], axis=1), jnp.concatenate([w_key, w_value], axis=1)])
    near = lax.all_gather(blocks, "ctx", axis=1, tiled=True)
    weights = lax.all_gather(jnp.stack([w_gate, w_up, w_down.T]), ("fsdp", "ctx"), axis=1, tiled=True)
    packed = jnp.concatenate(
        [gain_input, gain_post_attn, gain_pre_ffn, gain_post_ffn, gain_query, gain_key, segment_ids.astype(LOW).reshape(-1)]
    )
    packed = exchange(jnp.broadcast_to(packed[None], (F * C, packed.shape[0])), ("fsdp", "ctx")).astype(F32)
    at = 4 * piece
    g_input, g_post_attn, g_pre_ffn, g_post_ffn = [
        packed[:, i * piece : (i + 1) * piece].reshape(1, width_model) for i in range(4)
    ]
    g_query, g_key = [
        packed[:, at + i * gain_piece : at + (i + 1) * gain_piece].reshape(1, head_width) for i in range(2)
    ]
    seg_blocks = packed[:, at + 2 * gain_piece :].astype(jnp.int32)
    count = jnp.sum((seg_blocks != 0).astype(F32))
    normed = norm_rows(t, inputs, g_input, T)
    def sub_rows(values):
        return [lax.dynamic_slice_in_dim(values, (t ^ p) * sub, sub, 1) for p in range(T)]

    x_own = lax.dynamic_slice_in_dim(inputs, t * sub, sub, 1).reshape(own, width_model)
    target_own = lax.dynamic_slice_in_dim(target, t * sub, sub, 1).reshape(own, width_model)
    positions = jnp.concatenate([z * block_rows + (t ^ p) * sub + jnp.arange(sub, dtype=jnp.int32) for p in range(T)])
    segs = [segment_ids + 1]
    for d in range(1, halo + 1):
        far = lax.dynamic_index_in_dim(seg_blocks, jnp.maximum(me - d, 0), 0, False).reshape(seqs, block_rows)
        segs.append(jnp.where(z >= d, far + 1, 0))
    key_seg = jnp.concatenate([v for seg in segs for v in sub_rows(seg)], axis=1)
    key_pos = jnp.concatenate([positions - d * block_rows for d in range(halo + 1)])
    kinfo = jnp.stack([jnp.broadcast_to(key_pos, (seqs, spans)), key_seg], axis=1)
    qinfo = jnp.stack([jnp.broadcast_to(positions[:sub], (seqs, sub)), key_seg[:, :sub]], axis=2)
    valid_own = (key_seg[:, :sub] != 1).astype(F32).reshape(own, 1)
    cos_all, sin_all = rotary_tables(positions, head_width)
    cos_own, sin_own = cos_all[:sub], sin_all[:sub]

    ready = (normed, kinfo, qinfo, cos_all, sin_all, cos_own, sin_own, g_query, g_key, g_post_attn, g_pre_ffn, x_own)
    (near, *ready) = lax.optimization_barrier((near,) + ready)
    normed, kinfo, qinfo, cos_all, sin_all, cos_own, sin_own, g_query, g_key, g_post_attn, g_pre_ffn, x_own = ready
    near_qo, near_kv = near
    far_kv = swap(near_kv, "fsdp", 1)
    near_qo = [near_qo] + [swap(near_qo, "tp", p) for p in range(1, T)]
    pair, first, key_own, kv_full = project_keys(f, normed.reshape(T, seqs, sub, width_model), near_kv, far_kv, g_key, cos_all, sin_all)
    q_full, out_full = assemble(f, near_qo, [swap(after(v, first), "fsdp", 1) for v in near_qo])
    kv_rows, far = [pair], first
    for d in range(halo):
        far = shifted(far, "ctx", 1)
        kv_rows += [swap(far, "tp", p) if p else far for p in range(T)]
    normed_own = normed[:own]
    q_raw = mm(normed_own, q_full)
    wide = q_raw.shape[1]
    heads = wide // head_width
    specs = attention_specs(seqs, sub, spans, T, wide, head_width)
    kv_specs = [specs["own"]] + [specs["far"]] * (halo * T)
    q_rot, attended, lse = pl.pallas_call(
        functools.partial(attend_kernel, heads),
        grid=(seqs,),
        in_specs=[specs[k] for k in ("qinfo", "kinfo", "q", "gain", "table", "table")] + kv_specs,
        out_specs=[specs["q"], specs["q"], specs["lse"]],
        out_shape=[struct((own, wide), LOW), struct((own, wide), LOW), struct((seqs, sub * heads, 1), F32)],
        compiler_params=ROOM,
        cost_estimate=cost(4 * own * spans * wide // seqs, *kv_rows, q_raw),
        name="attend",
    )(qinfo, kinfo, q_raw, g_query, cos_own, sin_own, *kv_rows)
    token = struct((own, width_model), F32)
    token_low = struct((own, width_model), LOW)
    gain_row = struct((1, width_model), F32)
    branch, hidden, ffn_in = pl.pallas_call(
        mix_kernel, out_shape=[token, token, token_low], compiler_params=ROOM, cost_estimate=cost(own * wide * width_model, out_full, out_full), name="mix"
    )(attended, out_full, x_own, g_post_attn, g_pre_ffn)

    from_tp = lambda parts: parts[:1] + [swap(v, "tp", p) for p, v in enumerate(parts) if p]
    ffn_ins = from_tp([ffn_in] * T)
    groups = [[0], [1], list(range(2, T))]
    place = {p: (g, i) for g, group in enumerate(groups) for i, p in enumerate(group)}
    done = [ffn_call(ffn_kernel, "ffn", [ffn_ins[p] for p in group], weights, (), 3, LOW if g else F32) for g, group in enumerate(groups)]
    parts = [done[place[p][0]][0][place[p][1]] for p in range(T)]
    acts, slopes, curves = zip(*[results for _, results in done])
    acts = [(acts[place[p][0]], place[p][1]) for p in range(T)]
    all_tokens = seqs * block_rows * F * C
    output, d_result, d_ffn_low, dg_post_ffn, error = pl.pallas_call(
        loss_kernel,
        in_specs=[SMEM] + [VMEM] * (4 + T),
        out_shape=[token_low, token, token_low, gain_row, struct((1, 128), F32)],
        compiler_params=ALL,
        cost_estimate=cost(own, *parts, *parts),
        name="loss",
    )((all_tokens / count).reshape(1), hidden, target_own, valid_own, g_post_ffn, *from_tp(parts))

    def collect_core(send, mine, *earlier):
        other = swap(send, "fsdp", 1)
        return mine.astype(F32) + (after(other, *earlier) if earlier else other).astype(F32)

    def scatter_ctx(sums):
        return lax.psum_scatter(sums, "ctx", scatter_dimension=1, tiled=True).astype(F32)

    d_outs = from_tp([d_ffn_low] * T)
    done = []
    for g, group in enumerate(groups):
        rows = [d_outs[p] for p in group]
        if g == 1:
            rows[0] = after(rows[0], done[0][0][0])
        if g == 2:
            rows[0] = after(rows[0], done[1][0][0])
        done.append(ffn_call(ffn_back_kernel, "ffn_back", rows, weights, (slopes[g], curves[g]), 2, LOW if g else F32))
    last = done[-1][0][-1]
    (down_halves,) = weight_grad(f, own, [(v if p else after(v, last), 0) for p, v in enumerate(d_outs)], acts)
    down_sum = pair_sum((down_halves[1], swap(down_halves[0], "fsdp", 1)))
    (grad_down,) = scatter_ctx(down_sum)
    parts = [done[place[p][0]][0][place[p][1]] for p in range(T)]
    d_gates, d_ups = [[(done[place[p][0]][1][i], place[p][1]) for p in range(T)] for i in range(2)]
    first_in = after(ffn_ins[0], down_sum)
    gate_halves, up_halves = weight_grad(f, own, [(v, 0) for v in [first_in] + ffn_ins[1:]], d_gates, d_ups)

    parts = [after(v, *gate_halves, *up_halves) if p == 0 else v for p, v in enumerate(from_tp(parts))]
    d_hidden, d_branch, d_attended, dg_pre_ffn, dg_post_attn = pl.pallas_call(
        middle_kernel,
        out_shape=[token, token_low, struct((own, wide), LOW), gain_row, gain_row],
        compiler_params=ALL,
        cost_estimate=cost(300 * own * wide * width_model, out_full),
        name="middle",
    )(d_result, hidden, branch, out_full, g_pre_ffn, g_post_attn, *parts)
    assert halo * block_rows == WIN
    others = [after(swap(after(v[0], *parts[1:]), "fsdp", 1), d_branch) for v in (gate_halves, up_halves)]
    both_sums = pair_sum((gate_halves[1], others[0]), (up_halves[1], others[1]))
    grad_gate, grad_up = scatter_ctx(both_sums)
    d_attended = after(d_attended, both_sums)
    (out_halves,) = weight_grad(f, own, [(d_branch, 0)], [(attended, 0)])
    out_sum = collect_core(*out_halves)
    out_low = out_sum.astype(LOW)
    d_attended = after(d_attended, *out_halves)
    d_query, dg_query, *d_pairs = pl.pallas_call(
        functools.partial(attend_back_kernel, heads, T, halo + 1),
        grid=(seqs,),
        in_specs=[SMEM] + [specs[k] for k in ("qinfo", "kinfo", "q", "gain", "table", "table", "q", "lse", "q")] + kv_specs,
        out_specs=[specs["q"], specs["dgain"]]
        + [pl.BlockSpec((halo + 1, 1, sub, 2 * head_width), lambda s: (0, s, 0, 0))]
        + [specs["far"]] * (T - 1)
        + [pl.BlockSpec((halo - 1, 1, sub, 2 * head_width), lambda s: (0, s, 0, 0))] * (T - 1),
        out_shape=[struct((own, wide), LOW), struct((seqs, 1, head_width), F32), struct((halo + 1, seqs, sub, 2 * head_width), F32)]
        + [struct((seqs, sub, 2 * head_width), LOW)] * (T - 1)
        + [struct((halo - 1, seqs, sub, 2 * head_width), LOW)] * (T - 1),
        compiler_params=ALL,
        name="attend_back",
    )(t.reshape(1), qinfo, kinfo, q_raw, g_query, cos_own, sin_own, q_rot, lse, d_attended, *kv_rows)
    d_own = after(d_pairs[0], out_low)
    d_blocks = [d_own[b] for b in range(halo + 1)]
    for p in range(1, T):
        got = swap(d_pairs[p], "tp", p).astype(F32)
        later = (t ^ p) > t
        d_blocks[0] = d_blocks[0] + jnp.where(later, got, 0.0)
        d_blocks[halo] = d_blocks[halo] + jnp.where(later, 0.0, got)
    d_kv = d_blocks[halo].astype(LOW)
    for p in range(1, T):
        middle = swap(after(d_pairs[T - 1 + p], d_kv), "tp", p)
        for b in range(1, halo):
            d_blocks[b] = d_blocks[b] + middle[b - 1].astype(F32)
    d_query_late, out_low = after(d_query, d_kv), after(out_low, d_kv)
    for d in range(halo, 0, -1):
        come = shifted(d_kv, "ctx", -1)
        if d > 1:
            d_kv = (d_blocks[d - 1] + come.astype(F32)).astype(LOW)
    d_kv = [d_blocks[0], come]
    head = lambda v, p: v[:, p * head_width : (p + 1) * head_width]
    heads_sent = [jnp.concatenate([head(d_query_late, p), head(out_low, p)], axis=0) for p in range(1, T)]
    heads_here = [swap(v, "tp", p + 1) for p, v in enumerate(heads_sent)]
    out_head = head(out_sum, 0)
    for v in heads_here:
        out_head = out_head + v[own:].astype(F32)
    normed_late = after(normed, come)
    (q_halves,) = weight_grad(f, own, [(normed_late, p) for p in range(T)], [(head(d_query, 0), 0)] + [(v, 0) for v in heads_here])
    pulled = pl.pallas_call(
        pull_kernel, out_shape=token, compiler_params=ROOM, name="pull"
    )(d_query, q_full)

    def pack(values, wide):
        top = lax.reduce_precision(values, 8, 7)
        flat = jnp.concatenate([top, values - top], axis=1).astype(LOW)
        rows = -(-flat.shape[1] // wide)
        return jnp.pad(flat, ((0, 0), (0, rows * wide - flat.shape[1]))).reshape(values.shape[0], rows, wide)

    def unpack(rows, n):
        flat = rows.reshape(-1)
        return flat[:n] + flat[n : 2 * n]

    def core_rows(values):
        rows = jnp.concatenate([v.reshape(F * C, -1) for v in values], axis=1).reshape(F, C, -1)
        return lax.dynamic_index_in_dim(rows, f, 0, False) + swap(lax.dynamic_index_in_dim(rows, f ^ 1, 0, False), "fsdp", 1)

    def owner_sums(weight_sums, rows, *earlier):
        wide = weight_sums.shape[1]
        sent = jnp.concatenate([weight_sums.reshape(C, piece, wide), pack(rows, wide)], axis=1)
        sums = jnp.sum(after(exchange(sent, "ctx"), *earlier).astype(F32), axis=0)
        return sums[:piece], unpack(sums[piece:], rows.shape[1])

    early = core_rows(
        [dg_post_attn, dg_pre_ffn, dg_post_ffn, jnp.sum(dg_query, axis=(0, 1)), jnp.broadcast_to(error[:, :1], (F * C, 1))]
    )
    both_heads = jnp.concatenate([collect_core(*q_halves).astype(LOW), out_head.astype(LOW)], axis=1)
    d_kv[0] = after(d_kv[0], both_heads, pulled)
    own_rows = lambda table: jnp.tile(table, (seqs, 1))
    grad_input, dg_input, dg_key, *kv_halves = pl.pallas_call(
        functools.partial(finish_kernel, T),
        in_specs=[SMEM] + [VMEM] * (10 + len(d_kv)),
        out_shape=[token, gain_row, struct((1, head_width), F32)] + [struct((half, 2 * head_width), LOW)] * 2,
        scratch_shapes=[pltpu.VMEM((2 * half, 2 * head_width), F32), pltpu.VMEM((own, 2 * head_width), LOW)],
        compiler_params=ROOM,
        name="finish",
    )(jnp.stack([f, t]), key_own, own_rows(cos_own), own_rows(sin_own), g_key, pulled, kv_full, d_hidden, x_own, g_input,
      normed_own, *[v.reshape(own, 2 * head_width) for v in d_kv])
    late = core_rows([dg_input, dg_key])
    part = 2 * head_width // T
    kv_sum = collect_core(*kv_halves)
    kv_low = kv_sum.astype(LOW)
    kv_part = kv_sum[:, :part]
    for p in range(1, T):
        kv_part = kv_part + swap(kv_low[:, p * part : (p + 1) * part], "tp", p).astype(F32)
    sums = jnp.concatenate([both_heads, kv_part.astype(LOW)], axis=1)
    sums, total = owner_sums(sums, jnp.concatenate([early, late], axis=1), grad_gate, grad_up)
    grad_query, grad_out = sums[:, :head_width], sums[:, head_width : 2 * head_width]
    n = total.shape[0]
    rows = -(-n // part)
    mine = jnp.concatenate([sums[:, 2 * head_width :], jnp.pad(total, (0, rows * part - n)).reshape(rows, part)], axis=0)
    pieces = [swap(mine, "tp", p) if p else mine for p in range(T)]
    whole = jnp.stack(pieces)
    grad_kv = jnp.concatenate([lax.dynamic_index_in_dim(whole, t ^ p, 0, False)[:piece] for p in range(T)], axis=1)
    totals = {p: v[piece:] for p, v in enumerate(pieces)}
    bit = 1
    while bit < T:
        totals = {p: totals[p] + totals[p ^ bit] for p in totals if not p & bit}
        bit *= 2
    total = totals[0].reshape(-1)[:n]
    early, late = total[: early.shape[1]], total[early.shape[1] :]
    loss = early[-1] / (2.0 * width_model * count)
    at = 3 * piece
    return (
        output.reshape(seqs, sub, width_model),
        loss,
        grad_input.reshape(seqs, sub, width_model),
        grad_query,
        grad_kv[:, :head_width],
        grad_kv[:, head_width:],
        grad_out.T,
        grad_gate,
        grad_up,
        grad_down.T,
        late[:piece],
        early[at : at + gain_piece],
        late[piece:],
        early[:piece],
        early[piece : 2 * piece],
        early[2 * piece : at],
    )


def solution(mesh):
    rows = P(("fsdp", "ctx"), "tp")
    cols = P("tp", ("fsdp", "ctx"))
    split = P(("fsdp", "ctx"), None)
    gain = P(("fsdp", "ctx"))
    token = P("fsdp", "ctx", None)
    own = P("fsdp", ("ctx", "tp"), None)
    weights = (rows, split, split, cols, rows, rows, cols)
    return jax.shard_map(
        shards,
        mesh=mesh,
        in_specs=(token, token, P("fsdp", "ctx")) + weights + (gain,) * 6,
        out_specs=(own, P(), own) + weights + (gain,) * 6,
        check_vma=False,
    )
```

```python
import functools
import math

import jax
import jax.numpy as jnp
from jax import lax
from jax.experimental import pallas as pl
from jax.experimental.pallas import tpu as pltpu
from jax.sharding import PartitionSpec as P

WIN = 512
EPS = 1e-06
MASKED = -1e30
LOW = jnp.bfloat16
F32 = jnp.float32


def swap(values, axis, bits):
    return lax.ppermute(values, axis, [(i, i ^ bits) for i in range(lax.axis_size(axis))])


def shifted(values, axis, by):
    size = lax.axis_size(axis)
    return lax.ppermute(values, axis, [(i, i + by) for i in range(size) if 0 <= i + by < size])


def exchange(values, axes):
    return lax.all_to_all(values, axes, 0, 0, tiled=True)


def after(value, *earlier):
    return lax.optimization_barrier((value,) + earlier)[0]


def dot(left, right, contract):
    return lax.dot_general(left, right, (contract, ((), ())), preferred_element_type=F32)


def mm(left, right):
    return dot(left, right, ((1,), (0,)))


def mm_t(left, right):
    return dot(left, right, ((1,), (1,)))


def t_mm(left, right):
    return dot(left, right, ((0,), (0,)))


def inverse_rms(values):
    return lax.rsqrt(jnp.mean(values * values, axis=-1, keepdims=True) + EPS)


def rms_back(grad, values, inverse, gain_row):
    n = values * inverse
    eg = grad * gain_row
    return inverse * (eg - n * jnp.mean(eg * n, axis=-1, keepdims=True)), grad * n


def turn(values):
    half = values.shape[-1] // 2
    return jnp.concatenate([-values[..., half:], values[..., :half]], axis=-1)


def turn_back(values):
    half = values.shape[-1] // 2
    return jnp.concatenate([values[..., half:], -values[..., :half]], axis=-1)


def rotary_tables(positions, head_width):
    frequency = 10000.0 ** (-2.0 * jnp.arange(head_width // 2, dtype=F32) / head_width)
    angles = positions.astype(F32)[:, None] * frequency[None, :]
    angles = jnp.concatenate([angles, angles], axis=-1)
    return jnp.cos(angles), jnp.sin(angles)


def heads_of(values, heads):
    width = values.shape[1] // heads
    return [values[:, h * width : (h + 1) * width] for h in range(heads)]


VMEM = pl.BlockSpec(memory_space=pltpu.VMEM)
SMEM = pl.BlockSpec(memory_space=pltpu.SMEM)
ROOM = pltpu.CompilerParams(vmem_limit_bytes=28 * 1024 * 1024)
ALL = pltpu.CompilerParams(vmem_limit_bytes=60 * 1024 * 1024)


def cost(multiply_adds, *arrays):
    moved = sum(math.prod(v.shape) * jnp.dtype(v.dtype).itemsize for v in arrays)
    return pl.CostEstimate(flops=2 * multiply_adds, bytes_accessed=moved, transcendentals=0)


def struct(shape, dtype):
    return jax.ShapeDtypeStruct(shape, dtype)


def column_sum(values):
    return jnp.sum(values, axis=0, keepdims=True)


def assemble_kernel(pieces, core_ref, *refs):
    width = refs[0].shape[1] // 2
    results = refs[2 * pieces :]
    for step in range(2):

        @pl.when(pl.program_id(0) == step)
        def _():
            for i, result in enumerate(results):
                for p in range(pieces):
                    result[0, :, p * width : (p + 1) * width] = refs[step * pieces + p][:, i * width : (i + 1) * width]


def assemble(core, mine, others):
    half, width = mine[0].shape
    pieces = len(mine)
    wide = pieces * width // 2
    out = pl.BlockSpec((1, half, wide), lambda i, core: (i ^ core[0], 0, 0))
    results = pl.pallas_call(
        functools.partial(assemble_kernel, pieces),
        grid_spec=pltpu.PrefetchScalarGridSpec(
            num_scalar_prefetch=1,
            grid=(2,),
            in_specs=[pl.BlockSpec((half, width), lambda i, core: (0, 0))] * (2 * pieces),
            out_specs=[out, out],
        ),
        out_shape=[struct((2, half, wide), LOW)] * 2,
        compiler_params=ROOM,
        cost_estimate=cost(0, *mine, *others, *mine, *others),
        name="assemble",
    )(core.reshape(1), *mine, *others)
    return [v.reshape(2 * half, wide) for v in results]


def norm_rows_kernel(chunks, place_ref, x_ref, gain_ref, out_ref):
    sub = x_ref.shape[1] // chunks
    for p in range(chunks):
        x = x_ref[0, pl.ds(pl.multiple_of((place_ref[0] ^ p) * sub, sub), sub), :].astype(F32)
        out_ref[p, 0] = (x * inverse_rms(x) * gain_ref[...]).astype(LOW)


def norm_rows(place, x, gain_row, chunks):
    seqs, rows, width = x.shape
    sub = rows // chunks
    return pl.pallas_call(
        functools.partial(norm_rows_kernel, chunks),
        grid=(seqs,),
        in_specs=[
            pl.BlockSpec(memory_space=pltpu.SMEM),
            pl.BlockSpec((1, rows, width), lambda s: (s, 0, 0)),
            pl.BlockSpec((1, width), lambda s: (0, 0)),
        ],
        out_specs=pl.BlockSpec((chunks, 1, sub, width), lambda s: (0, s, 0, 0)),
        out_shape=jax.ShapeDtypeStruct((chunks, seqs, sub, width), LOW),
        compiler_params=ROOM,
        cost_estimate=cost(0, x, x, x, x),
        name="norm_rows",
    )(place.reshape(1), x, gain_row).reshape(chunks * seqs * sub, width)


def keys_kernel(core_ref, x_ref, near_ref, far_ref, gain_ref, cos_ref, sin_ref, pair_ref, first_ref, raw_ref, full_ref):
    chunks, _, sub, width = x_ref.shape
    half = near_ref.shape[0]
    head = gain_ref.shape[1]

    @pl.when(pl.program_id(0) == 0)
    def _():
        for place, source in ((core_ref[0], near_ref), (1 - core_ref[0], far_ref)):
            full_ref[pl.ds(pl.multiple_of(place * half, half), half), :] = source[...]

    kv = mm(x_ref[...].reshape(chunks * sub, width), full_ref[...])
    key = kv[:, :head]
    n = key * inverse_rms(key) * gain_ref[...]
    rot = (n * cos_ref[...] + turn(n) * sin_ref[...]).astype(LOW)
    value = kv[:, head:].astype(LOW)
    raw_ref[...] = key[:sub]
    pair_ref[:, 0, :, :head] = rot.reshape(chunks, sub, head)
    pair_ref[:, 0, :, head:] = value.reshape(chunks, sub, head)
    first_ref[0, :, :head] = rot[:sub]
    first_ref[0, :, head:] = value[:sub]


def project_keys(core, normed, near, far, gain_row, cos, sin):
    chunks, seqs, sub, width = normed.shape
    half, both = near.shape
    head = both // 2
    whole = lambda *shape: pl.BlockSpec(shape, lambda s: (0,) * len(shape))
    return pl.pallas_call(
        keys_kernel,
        grid=(seqs,),
        in_specs=[
            SMEM,
            pl.BlockSpec((chunks, 1, sub, width), lambda s: (0, s, 0, 0)),
            whole(half, both),
            whole(half, both),
            whole(1, head),
            whole(chunks * sub, head),
            whole(chunks * sub, head),
        ],
        out_specs=[
            pl.BlockSpec((chunks, 1, sub, both), lambda s: (0, s, 0, 0)),
            pl.BlockSpec((1, sub, both), lambda s: (s, 0, 0)),
            pl.BlockSpec((sub, head), lambda s: (s, 0)),
            whole(2 * half, both),
        ],
        out_shape=[
            struct((chunks, seqs, sub, both), LOW),
            struct((seqs, sub, both), LOW),
            struct((seqs * sub, head), F32),
            struct((2 * half, both), LOW),
        ],
        compiler_params=ROOM,
        cost_estimate=cost(seqs * chunks * sub * width * both, normed, normed),
        name="project_keys",
    )(core.reshape(1), normed, near, far, gain_row, cos, sin)


def mask_of(qinfo_ref, kinfo_ref):
    qpos, qseg = qinfo_ref[0, :, 0:1], qinfo_ref[0, :, 1:2]
    kpos, kseg = kinfo_ref[0, 0:1, :], kinfo_ref[0, 1:2, :]
    return (kseg == qseg) & (kpos <= qpos) & (kpos > qpos - WIN)


def key_rows(kv_refs, width):
    own_ref, *far_refs = kv_refs
    sides = []
    for at in (0, width):
        own = own_ref[:, 0, :, at : at + width].reshape(own_ref.shape[0] * own_ref.shape[2], width)
        sides.append(jnp.concatenate([own] + [r[0, :, at : at + width] for r in far_refs], axis=0))
    return sides


def attend_kernel(heads, qinfo_ref, kinfo_ref, q_ref, gain_ref, cos_ref, sin_ref, *refs):
    kv_refs, (rot_ref, out_ref, lse_ref) = refs[:-3], refs[-3:]
    width = q_ref.shape[1] // heads
    scale = width ** (-0.5)
    rotated = []
    for h, q in enumerate(heads_of(q_ref[...], heads)):
        n = q * inverse_rms(q) * gain_ref[...]
        rot = ((n * cos_ref[...] + turn(n) * sin_ref[...]) * scale).astype(LOW)
        rot_ref[:, h * width : (h + 1) * width] = rot
        rotated.append(rot)
    rows = jnp.concatenate(rotated, axis=0)
    keys, vals = key_rows(kv_refs, width)
    bias = jnp.where(mask_of(qinfo_ref, kinfo_ref), 0.0, MASKED)
    allowed = jnp.concatenate([bias] * heads, axis=0) == 0.0
    scores = jnp.where(allowed, mm_t(rows, keys), MASKED)
    top = jnp.max(scores, axis=1, keepdims=True)
    expos = jnp.exp(scores - top)
    total = jnp.sum(expos, axis=1, keepdims=True)
    lse_ref[0] = top + jnp.log(total)
    probs = (expos / total).astype(LOW)
    attended = mm(probs, vals).astype(LOW)
    count = q_ref.shape[0]
    for h in range(heads):
        out_ref[:, h * width : (h + 1) * width] = attended[h * count : (h + 1) * count]


def attend_back_kernel(heads, chunks, blocks, place_ref, qinfo_ref, kinfo_ref, q_ref, gain_ref, cos_ref, sin_ref, rot_ref, lse_ref,
                       dout_ref, *refs):
    far_count = (blocks - 1) * chunks
    kv_refs, (dq_ref, dgain_ref), dkv_refs = refs[: far_count + 1], refs[far_count + 1 : far_count + 3], refs[far_count + 3 :]
    width = q_ref.shape[1] // heads
    scale = width ** (-0.5)
    count = q_ref.shape[0]
    rows = jnp.concatenate(heads_of(rot_ref[...], heads), axis=0)
    douts = jnp.concatenate(heads_of(dout_ref[...], heads), axis=0)
    keys, vals = key_rows(kv_refs, width)
    bias = jnp.where(mask_of(qinfo_ref, kinfo_ref), 0.0, MASKED)
    allowed = jnp.concatenate([bias] * heads, axis=0) == 0.0
    probs = jnp.where(allowed, jnp.exp(mm_t(rows, keys) - lse_ref[0]), 0.0)
    d_probs = mm_t(douts, vals)
    delta = jnp.sum(probs * d_probs, axis=1, keepdims=True)
    d_scores = (probs * (d_probs - delta)).astype(LOW)
    d_rows = mm(d_scores, keys)
    d_keys = t_mm(d_scores, rows)
    d_vals = t_mm(probs.astype(LOW), douts)
    per = kv_refs[0].shape[2]
    own_ref, side_refs, middle_refs = dkv_refs[0], dkv_refs[1:chunks], dkv_refs[chunks:]
    for part, at in ((d_keys, 0), (d_vals, width)):
        piece = lambda b, p: part[(b * chunks + p) * per : (b * chunks + p + 1) * per]
        for b in range(blocks):
            own_ref[b, 0, :, at : at + width] = piece(b, 0)
        for p in range(1, chunks):
            earlier = (place_ref[0] ^ p) < place_ref[0]
            for b in range(1, blocks - 1):
                middle_refs[p - 1][b - 1, 0, :, at : at + width] = piece(b, p).astype(LOW)
            side_refs[p - 1][0, :, at : at + width] = jnp.where(earlier, piece(0, p), piece(blocks - 1, p)).astype(LOW)
    gain_sum = jnp.zeros((1, width), F32)
    for h, q in enumerate(heads_of(q_ref[...], heads)):
        e = d_rows[h * count : (h + 1) * count] * scale
        e = e * cos_ref[...] + turn_back(e * sin_ref[...])
        d_q, d_g = rms_back(e, q, inverse_rms(q), gain_ref[...])
        gain_sum = gain_sum + column_sum(d_g)
        dq_ref[:, h * width : (h + 1) * width] = d_q.astype(LOW)
    dgain_ref[0] = gain_sum


def pair_sum_kernel(*refs):
    out = refs[-1]
    for i in range(out.shape[0]):
        out[i] = (refs[2 * i][...].astype(F32) + refs[2 * i + 1][...].astype(F32)).astype(LOW)


def pair_sum(*pairs):
    rows, width = pairs[0][0].shape
    step = rows // 4 if rows % 64 == 0 else rows
    arrays = [v for pair in pairs for v in pair]
    return pl.pallas_call(
        pair_sum_kernel,
        grid=(rows // step,),
        in_specs=[pl.BlockSpec((step, width), lambda j: (j, 0))] * len(arrays),
        out_specs=pl.BlockSpec((len(pairs), step, width), lambda j: (0, j, 0)),
        out_shape=struct((len(pairs), rows, width), LOW),
        compiler_params=ALL,
        name="pair_sum",
    )(*arrays)


def attention_specs(seqs, rows, spans, chunks, wide, width):
    whole = lambda *shape: pl.BlockSpec(shape, lambda s: (0,) * len(shape))
    return dict(
        qinfo=pl.BlockSpec((1, rows, 2), lambda s: (s, 0, 0)),
        kinfo=pl.BlockSpec((1, 2, spans), lambda s: (s, 0, 0)),
        q=pl.BlockSpec((rows, wide), lambda s: (s, 0)),
        gain=whole(1, width),
        table=whole(rows, width),
        own=pl.BlockSpec((chunks, 1, rows, 2 * width), lambda s: (0, s, 0, 0)),
        far=pl.BlockSpec((1, rows, 2 * width), lambda s: (s, 0, 0)),
        lse=pl.BlockSpec((1, rows * (wide // width), 1), lambda s: (s, 0, 0)),
        dgain=pl.BlockSpec((1, 1, width), lambda s: (s, 0, 0)),
    )


def mix_kernel(att_ref, out_ref, x_ref, gain_attn_ref, gain_ffn_ref, branch_ref, hidden_ref, ffn_ref):
    branch = mm_t(att_ref[...], out_ref[...])
    branch_ref[...] = branch
    hidden = x_ref[...].astype(F32) + branch * inverse_rms(branch) * gain_attn_ref[...]
    hidden_ref[...] = hidden
    ffn_ref[...] = (hidden * inverse_rms(hidden) * gain_ffn_ref[...]).astype(LOW)


def for_blocks(width, step, block):
    full, rest = divmod(width, step)

    @pl.when(pl.program_id(0) < full)
    def _():
        block(step)

    if rest:

        @pl.when(pl.program_id(0) == full)
        def _():
            block(rest)


def ffn_kernel(units, chunks, *refs):
    rows_refs, (gate_ref, up_ref, down_ref) = refs[:chunks], refs[chunks : chunks + 3]
    part_refs, (act_ref, slope_ref, curve_ref, sums) = refs[chunks + 3 : 2 * chunks + 3], refs[2 * chunks + 3 :]

    @pl.when(pl.program_id(0) == 0)
    def _():
        sums[...] = jnp.zeros_like(sums)

    def block(size):
        rows = jnp.concatenate([r[...] for r in rows_refs], axis=0)
        gate, up = mm(rows, gate_ref[0, :, :size]), mm(rows, up_ref[0, :, :size])
        root = (2.0 / math.pi) ** 0.5
        square = gate * gate
        bend = jnp.tanh(root * (gate + 0.044715 * (square * gate)))
        share = 0.5 * (1.0 + bend)
        curve = gate * share
        slope = share + 0.5 * gate * (1.0 - bend * bend) * (root * (1.0 + 3.0 * 0.044715 * square))
        act = (curve * up).astype(LOW)
        act_ref[:, :size] = act
        slope_ref[:, :size] = (slope * up).astype(LOW)
        curve_ref[:, :size] = curve.astype(LOW)
        sums[...] += mm_t(act, down_ref[0, :, :size])

    for_blocks(units, act_ref.shape[1], block)
    split_rows(sums, part_refs)


def split_rows(sums, part_refs):
    @pl.when(pl.program_id(0) == pl.num_programs(0) - 1)
    def _():
        count = part_refs[0].shape[0]
        for p, part in enumerate(part_refs):
            part[...] = sums[p * count : (p + 1) * count].astype(part.dtype)


def ffn_back_kernel(units, chunks, *refs):
    rows_refs, (gate_ref, up_ref, down_ref, slope_ref, curve_ref) = refs[:chunks], refs[chunks : chunks + 5]
    part_refs, (dgate_ref, dup_ref, sums) = refs[chunks + 5 : 2 * chunks + 5], refs[2 * chunks + 5 :]

    @pl.when(pl.program_id(0) == 0)
    def _():
        sums[...] = jnp.zeros_like(sums)

    def block(size):
        rows = jnp.concatenate([r[...] for r in rows_refs], axis=0)
        d_act = mm(rows, down_ref[0, :, :size])
        d_gate = (d_act * slope_ref[:, :size].astype(F32)).astype(LOW)
        d_up = (d_act * curve_ref[:, :size].astype(F32)).astype(LOW)
        dgate_ref[:, :size] = d_gate
        dup_ref[:, :size] = d_up
        sums[...] += mm_t(d_gate, gate_ref[0, :, :size]) + mm_t(d_up, up_ref[0, :, :size])

    for_blocks(units, dgate_ref.shape[1], block)
    split_rows(sums, part_refs)


def ffn_call(kernel, name, rows, weights, saved, results, dtype, step=640):
    chunks = len(rows)
    count, width = rows[0].shape
    units = weights.shape[2]
    whole = pl.BlockSpec((count, width), lambda j: (0, 0))
    strip = pl.BlockSpec((chunks * count, step), lambda j: (0, j))
    flat = pl.pallas_call(
        functools.partial(kernel, units, chunks),
        grid=(pl.cdiv(units, step),),
        in_specs=[whole] * chunks
        + [pl.BlockSpec((1, width, step), lambda j, i=i: (i, 0, j)) for i in range(3)]
        + [strip] * len(saved),
        out_specs=[whole] * chunks + [strip] * results,
        out_shape=[struct((count, width), dtype)] * chunks + [struct((chunks * count, units), LOW)] * results,
        scratch_shapes=[pltpu.VMEM((chunks * count, width), F32)],
        compiler_params=ALL,
        cost_estimate=cost(3 * chunks * count * width * units, *rows, weights, *saved),
        name=name,
    )(*rows, weights, weights, weights, *saved)
    return flat[:chunks], flat[chunks:]


def loss_kernel(factor_ref, hidden_ref, target_ref, valid_ref, gain_ref, *refs):
    parts, (out_ref, dres_ref, dffn_ref, dgain_ref, error_ref) = refs[:-5], refs[-5:]
    ffn = sum(r[...].astype(F32) for r in parts)
    inverse = inverse_rms(ffn)
    result = hidden_ref[...] + ffn * inverse * gain_ref[...]
    out_ref[...] = result.astype(LOW)
    mismatch = result - target_ref[...].astype(F32)
    marked = valid_ref[...] * mismatch
    error_ref[...] = jnp.broadcast_to(column_sum(jnp.sum(marked * mismatch, axis=1, keepdims=True)), error_ref.shape)
    d_result = factor_ref[0] * marked
    dres_ref[...] = d_result
    d_ffn, d_gain = rms_back(d_result, ffn, inverse, gain_ref[...])
    dffn_ref[...] = d_ffn.astype(LOW)
    dgain_ref[...] = column_sum(d_gain)


def middle_kernel(dres_ref, hidden_ref, branch_ref, out_ref, gain_ffn_ref, gain_attn_ref, *refs):
    parts, (dhid_ref, dbranch_ref, datt_ref, dgain_ffn_ref, dgain_attn_ref) = refs[:-5], refs[-5:]
    d_ffn_in = sum(r[...].astype(F32) for r in parts)
    hidden = hidden_ref[...]
    d_add, d_gain = rms_back(d_ffn_in, hidden, inverse_rms(hidden), gain_ffn_ref[...])
    dgain_ffn_ref[...] = column_sum(d_gain)
    d_hidden = dres_ref[...] + d_add
    dhid_ref[...] = d_hidden
    branch = branch_ref[...]
    d_branch, d_gain = rms_back(d_hidden, branch, inverse_rms(branch), gain_attn_ref[...])
    dgain_attn_ref[...] = column_sum(d_gain)
    low = d_branch.astype(LOW)
    dbranch_ref[...] = low
    datt_ref[...] = mm(low, out_ref[...]).astype(LOW)


def pull_kernel(left_ref, right_ref, out_ref):
    out_ref[...] = mm_t(left_ref[...], right_ref[...])


def finish_kernel(chunks, place_ref, raw_ref, cos_ref, sin_ref, gain_key_ref, pulled_ref, kv_ref, dhid_ref, x_ref, gain_ref, normed_ref, *refs):
    parts, (din_ref, dgain_ref, dgain_key_ref, send_ref, own_ref, sums, turned) = refs[:-7], refs[-7:]
    head = raw_ref.shape[1]
    d_kv = sum(r[...].astype(F32) for r in parts)
    key = raw_ref[...]
    e = d_kv[:, :head]
    e = e * cos_ref[...] + turn_back(e * sin_ref[...])
    d_key, d_gain = rms_back(e, key, inverse_rms(key), gain_key_ref[...])
    dgain_key_ref[...] = column_sum(d_gain)
    low = jnp.concatenate([d_key.astype(LOW), d_kv[:, head:].astype(LOW)], axis=1)
    turned[...] = low
    part = low.shape[1] // chunks
    ordered = [turned[:, pl.ds(pl.multiple_of((place_ref[1] ^ p) * part, part), part)] for p in range(chunks)]
    sums[...] = mm(normed_ref[...].T, jnp.concatenate(ordered, axis=1))
    half = own_ref.shape[0]
    core = place_ref[0]
    own_ref[...] = sums[pl.ds(pl.multiple_of(core * half, half), half), :].astype(LOW)
    send_ref[...] = sums[pl.ds(pl.multiple_of((1 - core) * half, half), half), :].astype(LOW)
    d_normed = pulled_ref[...] + mm_t(low, kv_ref[...])
    x = x_ref[...].astype(F32)
    d_x, d_gain = rms_back(d_normed, x, inverse_rms(x), gain_ref[...])
    dgain_ref[...] = column_sum(d_gain)
    din_ref[...] = dhid_ref[...] + d_x


def weight_grad_kernel(chunks, sets, core_ref, *refs):
    lefts, refs = refs[:chunks], refs[chunks:]
    rights, refs = refs[: chunks * sets], refs[chunks * sets :]
    outs, turned = refs[: 2 * sets], refs[2 * sets]
    rows = lefts[0].shape[0]
    half = outs[0].shape[0]

    @pl.when(pl.program_id(0) == 0)
    def _():
        for p in range(chunks):
            turned[:, p * rows : (p + 1) * rows] = lefts[p][...].T

    core = core_ref[0]
    for i in range(sets):
        right = jnp.concatenate([r[...] for r in rights[i * chunks : (i + 1) * chunks]], axis=0)
        for place, out in ((1 - core, outs[2 * i]), (core, outs[2 * i + 1])):
            out[...] = mm(turned[pl.ds(pl.multiple_of(place * half, half), half), :], right).astype(LOW)


def weight_grad(core, rows, lefts, *rights):
    chunks, sets = len(lefts), len(rights)
    widest = rights[0][0][0].shape[1]
    step = 256 if sets > 1 or widest < 1024 else 512 if widest == 1024 else 896
    height = lefts[0][0].shape[1]
    width = rights[0][0][0].shape[1]
    rights = [pair for group in rights for pair in group]
    out = pl.BlockSpec((height // 2, step), lambda j: (0, j))
    flat = pl.pallas_call(
        functools.partial(weight_grad_kernel, chunks, sets),
        grid=(pl.cdiv(width, step),),
        in_specs=[SMEM]
        + [pl.BlockSpec((rows, height), lambda j, at=at: (at, 0)) for _, at in lefts]
        + [pl.BlockSpec((rows, step), lambda j, at=at: (at, j)) for _, at in rights],
        out_specs=[out] * (2 * sets),
        out_shape=[struct((height // 2, width), LOW)] * (2 * sets),
        scratch_shapes=[pltpu.VMEM((height, chunks * rows), LOW)],
        compiler_params=ALL,
        cost_estimate=None if width < height else cost(sets * chunks * rows * height * width, *[v for v, _ in lefts], struct((height, sets * width), LOW)),
        name="weight_grad",
    )(core.reshape(1), *[v for v, _ in lefts], *[v for v, _ in rights])
    return [flat[2 * i : 2 * i + 2] for i in range(sets)]


def shards(inputs, target, segment_ids, w_query, w_key, w_value, w_out, w_gate, w_up, w_down,
           gain_input, gain_query, gain_key, gain_post_attn, gain_pre_ffn, gain_post_ffn):
    F, C, T = (lax.axis_size(a) for a in ("fsdp", "ctx", "tp"))
    f, z, t = (lax.axis_index(a) for a in ("fsdp", "ctx", "tp"))
    me = f * C + z
    seqs, block_rows, width_model = inputs.shape
    piece = w_query.shape[0]
    head_width = w_key.shape[1]
    gain_piece = gain_query.shape[0]
    sub = block_rows // T
    own = seqs * sub
    half = C * piece
    halo = -(-(WIN - 1) // block_rows)
    spans = (halo + 1) * block_rows

    both = 2 * head_width
    blocks = jnp.stack([jnp.concatenate([w_query, w_out.T], axis=1), jnp.concatenate([w_key, w_value], axis=1)])
    near = lax.all_gather(blocks, "ctx", axis=1, tiled=True)
    weights = lax.all_gather(jnp.stack([w_gate, w_up, w_down.T]), ("fsdp", "ctx"), axis=1, tiled=True)
    packed = jnp.concatenate(
        [gain_input, gain_post_attn, gain_pre_ffn, gain_post_ffn, gain_query, gain_key, segment_ids.astype(LOW).reshape(-1)]
    )
    packed = exchange(jnp.broadcast_to(packed[None], (F * C, packed.shape[0])), ("fsdp", "ctx")).astype(F32)
    at = 4 * piece
    g_input, g_post_attn, g_pre_ffn, g_post_ffn = [
        packed[:, i * piece : (i + 1) * piece].reshape(1, width_model) for i in range(4)
    ]
    g_query, g_key = [
        packed[:, at + i * gain_piece : at + (i + 1) * gain_piece].reshape(1, head_width) for i in range(2)
    ]
    seg_blocks = packed[:, at + 2 * gain_piece :].astype(jnp.int32)
    count = jnp.sum((seg_blocks != 0).astype(F32))
    normed = norm_rows(t, inputs, g_input, T)
    def sub_rows(values):
        return [lax.dynamic_slice_in_dim(values, (t ^ p) * sub, sub, 1) for p in range(T)]

    x_own = lax.dynamic_slice_in_dim(inputs, t * sub, sub, 1).reshape(own, width_model)
    target_own = lax.dynamic_slice_in_dim(target, t * sub, sub, 1).reshape(own, width_model)
    positions = jnp.concatenate([z * block_rows + (t ^ p) * sub + jnp.arange(sub, dtype=jnp.int32) for p in range(T)])
    segs = [segment_ids + 1]
    for d in range(1, halo + 1):
        far = lax.dynamic_index_in_dim(seg_blocks, jnp.maximum(me - d, 0), 0, False).reshape(seqs, block_rows)
        segs.append(jnp.where(z >= d, far + 1, 0))
    key_seg = jnp.concatenate([v for seg in segs for v in sub_rows(seg)], axis=1)
    key_pos = jnp.concatenate([positions - d * block_rows for d in range(halo + 1)])
    kinfo = jnp.stack([jnp.broadcast_to(key_pos, (seqs, spans)), key_seg], axis=1)
    qinfo = jnp.stack([jnp.broadcast_to(positions[:sub], (seqs, sub)), key_seg[:, :sub]], axis=2)
    valid_own = (key_seg[:, :sub] != 1).astype(F32).reshape(own, 1)
    cos_all, sin_all = rotary_tables(positions, head_width)
    cos_own, sin_own = cos_all[:sub], sin_all[:sub]

    ready = (normed, kinfo, qinfo, cos_all, sin_all, cos_own, sin_own, g_query, g_key, g_post_attn, g_pre_ffn, x_own)
    (near, *ready) = lax.optimization_barrier((near,) + ready)
    normed, kinfo, qinfo, cos_all, sin_all, cos_own, sin_own, g_query, g_key, g_post_attn, g_pre_ffn, x_own = ready
    near_qo, near_kv = near
    far_kv = swap(near_kv, "fsdp", 1)
    near_qo = [near_qo] + [swap(near_qo, "tp", p) for p in range(1, T)]
    pair, first, key_own, kv_full = project_keys(f, normed.reshape(T, seqs, sub, width_model), near_kv, far_kv, g_key, cos_all, sin_all)
    q_full, out_full = assemble(f, near_qo, [swap(after(v, first), "fsdp", 1) for v in near_qo])
    kv_rows, far = [pair], first
    for d in range(halo):
        far = shifted(far, "ctx", 1)
        kv_rows += [swap(far, "tp", p) if p else far for p in range(T)]
    normed_own = normed[:own]
    q_raw = mm(normed_own, q_full)
    wide = q_raw.shape[1]
    heads = wide // head_width
    specs = attention_specs(seqs, sub, spans, T, wide, head_width)
    kv_specs = [specs["own"]] + [specs["far"]] * (halo * T)
    q_rot, attended, lse = pl.pallas_call(
        functools.partial(attend_kernel, heads),
        grid=(seqs,),
        in_specs=[specs[k] for k in ("qinfo", "kinfo", "q", "gain", "table", "table")] + kv_specs,
        out_specs=[specs["q"], specs["q"], specs["lse"]],
        out_shape=[struct((own, wide), LOW), struct((own, wide), LOW), struct((seqs, sub * heads, 1), F32)],
        compiler_params=ROOM,
        cost_estimate=cost(4 * own * spans * wide // seqs, *kv_rows, q_raw),
        name="attend",
    )(qinfo, kinfo, q_raw, g_query, cos_own, sin_own, *kv_rows)
    token = struct((own, width_model), F32)
    token_low = struct((own, width_model), LOW)
    gain_row = struct((1, width_model), F32)
    branch, hidden, ffn_in = pl.pallas_call(
        mix_kernel, out_shape=[token, token, token_low], compiler_params=ROOM, cost_estimate=cost(own * wide * width_model, out_full, out_full), name="mix"
    )(attended, out_full, x_own, g_post_attn, g_pre_ffn)

    from_tp = lambda parts: parts[:1] + [swap(v, "tp", p) for p, v in enumerate(parts) if p]
    ffn_ins = from_tp([ffn_in] * T)
    groups = [[0], [1], list(range(2, T))]
    place = {p: (g, i) for g, group in enumerate(groups) for i, p in enumerate(group)}
    done = [ffn_call(ffn_kernel, "ffn", [ffn_ins[p] for p in group], weights, (), 3, LOW if g else F32) for g, group in enumerate(groups)]
    parts = [done[place[p][0]][0][place[p][1]] for p in range(T)]
    acts, slopes, curves = zip(*[results for _, results in done])
    acts = [(acts[place[p][0]], place[p][1]) for p in range(T)]
    all_tokens = seqs * block_rows * F * C
    output, d_result, d_ffn_low, dg_post_ffn, error = pl.pallas_call(
        loss_kernel,
        in_specs=[SMEM] + [VMEM] * (4 + T),
        out_shape=[token_low, token, token_low, gain_row, struct((1, 128), F32)],
        compiler_params=ALL,
        cost_estimate=cost(own, *parts, *parts),
        name="loss",
    )((all_tokens / count).reshape(1), hidden, target_own, valid_own, g_post_ffn, *from_tp(parts))

    def collect_core(send, mine, *earlier):
        other = swap(send, "fsdp", 1)
        return mine.astype(F32) + (after(other, *earlier) if earlier else other).astype(F32)

    def scatter_ctx(sums):
        return lax.psum_scatter(sums, "ctx", scatter_dimension=1, tiled=True).astype(F32)

    d_outs = from_tp([d_ffn_low] * T)
    done = []
    for g, group in enumerate(groups):
        rows = [d_outs[p] for p in group]
        if g == 1:
            rows[0] = after(rows[0], done[0][0][0])
        if g == 2:
            rows[0] = after(rows[0], done[1][0][0])
        done.append(ffn_call(ffn_back_kernel, "ffn_back", rows, weights, (slopes[g], curves[g]), 2, LOW if g else F32))
    last = done[-1][0][-1]
    (down_halves,) = weight_grad(f, own, [(v if p else after(v, last), 0) for p, v in enumerate(d_outs)], acts)
    down_sum = pair_sum((down_halves[1], swap(down_halves[0], "fsdp", 1)))
    (grad_down,) = scatter_ctx(down_sum)
    parts = [done[place[p][0]][0][place[p][1]] for p in range(T)]
    d_gates, d_ups = [[(done[place[p][0]][1][i], place[p][1]) for p in range(T)] for i in range(2)]
    first_in = after(ffn_ins[0], down_sum)
    gate_halves, up_halves = weight_grad(f, own, [(v, 0) for v in [first_in] + ffn_ins[1:]], d_gates, d_ups)

    parts = [after(v, *gate_halves, *up_halves) if p == 0 else v for p, v in enumerate(from_tp(parts))]
    d_hidden, d_branch, d_attended, dg_pre_ffn, dg_post_attn = pl.pallas_call(
        middle_kernel,
        out_shape=[token, token_low, struct((own, wide), LOW), gain_row, gain_row],
        compiler_params=ALL,
        cost_estimate=cost(300 * own * wide * width_model, out_full),
        name="middle",
    )(d_result, hidden, branch, out_full, g_pre_ffn, g_post_attn, *parts)
    assert halo * block_rows == WIN
    others = [after(swap(after(v[0], *parts[1:]), "fsdp", 1), d_branch) for v in (gate_halves, up_halves)]
    both_sums = pair_sum((gate_halves[1], others[0]), (up_halves[1], others[1]))
    grad_gate, grad_up = scatter_ctx(both_sums)
    d_attended = after(d_attended, both_sums)
    (out_halves,) = weight_grad(f, own, [(d_branch, 0)], [(attended, 0)])
    out_sum = collect_core(*out_halves)
    out_low = out_sum.astype(LOW)
    d_attended = after(d_attended, *out_halves)
    d_query, dg_query, *d_pairs = pl.pallas_call(
        functools.partial(attend_back_kernel, heads, T, halo + 1),
        grid=(seqs,),
        in_specs=[SMEM] + [specs[k] for k in ("qinfo", "kinfo", "q", "gain", "table", "table", "q", "lse", "q")] + kv_specs,
        out_specs=[specs["q"], specs["dgain"]]
        + [pl.BlockSpec((halo + 1, 1, sub, 2 * head_width), lambda s: (0, s, 0, 0))]
        + [specs["far"]] * (T - 1)
        + [pl.BlockSpec((halo - 1, 1, sub, 2 * head_width), lambda s: (0, s, 0, 0))] * (T - 1),
        out_shape=[struct((own, wide), LOW), struct((seqs, 1, head_width), F32), struct((halo + 1, seqs, sub, 2 * head_width), F32)]
        + [struct((seqs, sub, 2 * head_width), LOW)] * (T - 1)
        + [struct((halo - 1, seqs, sub, 2 * head_width), LOW)] * (T - 1),
        compiler_params=ALL,
        name="attend_back",
    )(t.reshape(1), qinfo, kinfo, q_raw, g_query, cos_own, sin_own, q_rot, lse, d_attended, *kv_rows)
    d_own = after(d_pairs[0], out_low)
    d_blocks = [d_own[b] for b in range(halo + 1)]
    for p in range(1, T):
        got = swap(d_pairs[p], "tp", p).astype(F32)
        later = (t ^ p) > t
        d_blocks[0] = d_blocks[0] + jnp.where(later, got, 0.0)
        d_blocks[halo] = d_blocks[halo] + jnp.where(later, 0.0, got)
    d_kv = d_blocks[halo].astype(LOW)
    for p in range(1, T):
        middle = swap(after(d_pairs[T - 1 + p], d_kv), "tp", p)
        for b in range(1, halo):
            d_blocks[b] = d_blocks[b] + middle[b - 1].astype(F32)
    d_query_late, out_low = after(d_query, d_kv), after(out_low, d_kv)
    for d in range(halo, 0, -1):
        come = shifted(d_kv, "ctx", -1)
        if d > 1:
            d_kv = (d_blocks[d - 1] + come.astype(F32)).astype(LOW)
    d_kv = [d_blocks[0], come]
    head = lambda v, p: v[:, p * head_width : (p + 1) * head_width]
    heads_sent = [jnp.concatenate([head(d_query_late, p), head(out_low, p)], axis=0) for p in range(1, T)]
    heads_here = [swap(v, "tp", p + 1) for p, v in enumerate(heads_sent)]
    out_head = head(out_sum, 0)
    for v in heads_here:
        out_head = out_head + v[own:].astype(F32)
    normed_late = after(normed, come)
    (q_halves,) = weight_grad(f, own, [(normed_late, p) for p in range(T)], [(head(d_query, 0), 0)] + [(v, 0) for v in heads_here])
    pulled = pl.pallas_call(
        pull_kernel, out_shape=token, compiler_params=ROOM, name="pull"
    )(d_query, q_full)

    def pack(values, wide):
        top = lax.reduce_precision(values, 8, 7)
        flat = jnp.concatenate([top, values - top], axis=1).astype(LOW)
        rows = -(-flat.shape[1] // wide)
        return jnp.pad(flat, ((0, 0), (0, rows * wide - flat.shape[1]))).reshape(values.shape[0], rows, wide)

    def unpack(rows, n):
        flat = rows.reshape(-1)
        return flat[:n] + flat[n : 2 * n]

    def core_rows(values):
        rows = jnp.concatenate([v.reshape(F * C, -1) for v in values], axis=1).reshape(F, C, -1)
        return lax.dynamic_index_in_dim(rows, f, 0, False) + swap(lax.dynamic_index_in_dim(rows, f ^ 1, 0, False), "fsdp", 1)

    def owner_sums(weight_sums, rows, *earlier):
        wide = weight_sums.shape[1]
        sent = jnp.concatenate([weight_sums.reshape(C, piece, wide), pack(rows, wide)], axis=1)
        sums = jnp.sum(after(exchange(sent, "ctx"), *earlier).astype(F32), axis=0)
        return sums[:piece], unpack(sums[piece:], rows.shape[1])

    early = core_rows(
        [dg_post_attn, dg_pre_ffn, dg_post_ffn, jnp.sum(dg_query, axis=(0, 1)), jnp.broadcast_to(error[:, :1], (F * C, 1))]
    )
    both_heads = jnp.concatenate([collect_core(*q_halves).astype(LOW), out_head.astype(LOW)], axis=1)
    d_kv[0] = after(d_kv[0], both_heads, pulled)
    own_rows = lambda table: jnp.tile(table, (seqs, 1))
    grad_input, dg_input, dg_key, *kv_halves = pl.pallas_call(
        functools.partial(finish_kernel, T),
        in_specs=[SMEM] + [VMEM] * (10 + len(d_kv)),
        out_shape=[token, gain_row, struct((1, head_width), F32)] + [struct((half, 2 * head_width), LOW)] * 2,
        scratch_shapes=[pltpu.VMEM((2 * half, 2 * head_width), F32), pltpu.VMEM((own, 2 * head_width), LOW)],
        compiler_params=ROOM,
        name="finish",
    )(jnp.stack([f, t]), key_own, own_rows(cos_own), own_rows(sin_own), g_key, pulled, kv_full, d_hidden, x_own, g_input,
      normed_own, *[v.reshape(own, 2 * head_width) for v in d_kv])
    late = core_rows([dg_input, dg_key])
    part = 2 * head_width // T
    kv_sum = collect_core(*kv_halves)
    kv_low = kv_sum.astype(LOW)
    kv_part = kv_sum[:, :part]
    for p in range(1, T):
        kv_part = kv_part + swap(kv_low[:, p * part : (p + 1) * part], "tp", p).astype(F32)
    sums = jnp.concatenate([both_heads, kv_part.astype(LOW)], axis=1)
    sums, total = owner_sums(sums, jnp.concatenate([early, late], axis=1), grad_gate, grad_up)
    grad_query, grad_out = sums[:, :head_width], sums[:, head_width : 2 * head_width]
    n = total.shape[0]
    rows = -(-n // part)
    mine = jnp.concatenate([sums[:, 2 * head_width :], jnp.pad(total, (0, rows * part - n)).reshape(rows, part)], axis=0)
    pieces = [swap(mine, "tp", p) if p else mine for p in range(T)]
    whole = jnp.stack(pieces)
    grad_kv = jnp.concatenate([lax.dynamic_index_in_dim(whole, t ^ p, 0, False)[:piece] for p in range(T)], axis=1)
    totals = {p: v[piece:] for p, v in enumerate(pieces)}
    bit = 1
    while bit < T:
        totals = {p: totals[p] + totals[p ^ bit] for p in totals if not p & bit}
        bit *= 2
    total = totals[0].reshape(-1)[:n]
    early, late = total[: early.shape[1]], total[early.shape[1] :]
    loss = early[-1] / (2.0 * width_model * count)
    at = 3 * piece
    return (
        output.reshape(seqs, sub, width_model),
        loss,
        grad_input.reshape(seqs, sub, width_model),
        grad_query,
        grad_kv[:, :head_width],
        grad_kv[:, head_width:],
        grad_out.T,
        grad_gate,
        grad_up,
        grad_down.T,
        late[:piece],
        early[at : at + gain_piece],
        late[piece:],
        early[:piece],
        early[piece : 2 * piece],
        early[2 * piece : at],
    )


def solution(mesh):
    rows = P(("fsdp", "ctx"), "tp")
    cols = P("tp", ("fsdp", "ctx"))
    split = P(("fsdp", "ctx"), None)
    gain = P(("fsdp", "ctx"))
    token = P("fsdp", "ctx", None)
    own = P("fsdp", ("ctx", "tp"), None)
    weights = (rows, split, split, cols, rows, rows, cols)
    return jax.shard_map(
        shards,
        mesh=mesh,
        in_specs=(token, token, P("fsdp", "ctx")) + weights + (gain,) * 6,
        out_specs=(own, P(), own) + weights + (gain,) * 6,
        check_vma=False,
    )
```

```python
import functools
import math

import jax
import jax.numpy as jnp
from jax import lax
from jax.experimental import pallas as pl
from jax.experimental.pallas import tpu as pltpu
from jax.sharding import PartitionSpec as P

WIN = 512
EPS = 1e-06
MASKED = -1e30
LOW = jnp.bfloat16
F32 = jnp.float32


def swap(values, axis, bits):
    return lax.ppermute(values, axis, [(i, i ^ bits) for i in range(lax.axis_size(axis))])


def shifted(values, axis, by):
    size = lax.axis_size(axis)
    return lax.ppermute(values, axis, [(i, i + by) for i in range(size) if 0 <= i + by < size])


def exchange(values, axes):
    return lax.all_to_all(values, axes, 0, 0, tiled=True)


def after(value, *earlier):
    return lax.optimization_barrier((value,) + earlier)[0]


def dot(left, right, contract):
    return lax.dot_general(left, right, (contract, ((), ())), preferred_element_type=F32)


def mm(left, right):
    return dot(left, right, ((1,), (0,)))


def mm_t(left, right):
    return dot(left, right, ((1,), (1,)))


def t_mm(left, right):
    return dot(left, right, ((0,), (0,)))


def inverse_rms(values):
    return lax.rsqrt(jnp.mean(values * values, axis=-1, keepdims=True) + EPS)


def rms_back(grad, values, inverse, gain_row):
    n = values * inverse
    eg = grad * gain_row
    return inverse * (eg - n * jnp.mean(eg * n, axis=-1, keepdims=True)), grad * n


def turn(values):
    half = values.shape[-1] // 2
    return jnp.concatenate([-values[..., half:], values[..., :half]], axis=-1)


def turn_back(values):
    half = values.shape[-1] // 2
    return jnp.concatenate([values[..., half:], -values[..., :half]], axis=-1)


def rotary_tables(positions, head_width):
    frequency = 10000.0 ** (-2.0 * jnp.arange(head_width // 2, dtype=F32) / head_width)
    angles = positions.astype(F32)[:, None] * frequency[None, :]
    angles = jnp.concatenate([angles, angles], axis=-1)
    return jnp.cos(angles), jnp.sin(angles)


def heads_of(values, heads):
    width = values.shape[1] // heads
    return [values[:, h * width : (h + 1) * width] for h in range(heads)]


VMEM = pl.BlockSpec(memory_space=pltpu.VMEM)
SMEM = pl.BlockSpec(memory_space=pltpu.SMEM)
ROOM = pltpu.CompilerParams(vmem_limit_bytes=28 * 1024 * 1024)
ALL = pltpu.CompilerParams(vmem_limit_bytes=60 * 1024 * 1024)


def cost(multiply_adds, *arrays):
    moved = sum(math.prod(v.shape) * jnp.dtype(v.dtype).itemsize for v in arrays)
    return pl.CostEstimate(flops=2 * multiply_adds, bytes_accessed=moved, transcendentals=0)


def struct(shape, dtype):
    return jax.ShapeDtypeStruct(shape, dtype)


def column_sum(values):
    return jnp.sum(values, axis=0, keepdims=True)


def assemble_kernel(pieces, core_ref, *refs):
    width = refs[0].shape[1] // 2
    results = refs[2 * pieces :]
    for step in range(2):

        @pl.when(pl.program_id(0) == step)
        def _():
            for i, result in enumerate(results):
                for p in range(pieces):
                    result[0, :, p * width : (p + 1) * width] = refs[step * pieces + p][:, i * width : (i + 1) * width]


def assemble(core, mine, others):
    half, width = mine[0].shape
    pieces = len(mine)
    wide = pieces * width // 2
    out = pl.BlockSpec((1, half, wide), lambda i, core: (i ^ core[0], 0, 0))
    results = pl.pallas_call(
        functools.partial(assemble_kernel, pieces),
        grid_spec=pltpu.PrefetchScalarGridSpec(
            num_scalar_prefetch=1,
            grid=(2,),
            in_specs=[pl.BlockSpec((half, width), lambda i, core: (0, 0))] * (2 * pieces),
            out_specs=[out, out],
        ),
        out_shape=[struct((2, half, wide), LOW)] * 2,
        compiler_params=ROOM,
        cost_estimate=cost(0, *mine, *others, *mine, *others),
        name="assemble",
    )(core.reshape(1), *mine, *others)
    return [v.reshape(2 * half, wide) for v in results]


def norm_rows_kernel(chunks, place_ref, x_ref, gain_ref, out_ref):
    sub = x_ref.shape[1] // chunks
    for p in range(chunks):
        x = x_ref[0, pl.ds(pl.multiple_of((place_ref[0] ^ p) * sub, sub), sub), :].astype(F32)
        out_ref[p, 0] = (x * inverse_rms(x) * gain_ref[...]).astype(LOW)


def norm_rows(place, x, gain_row, chunks):
    seqs, rows, width = x.shape
    sub = rows // chunks
    return pl.pallas_call(
        functools.partial(norm_rows_kernel, chunks),
        grid=(seqs,),
        in_specs=[
            pl.BlockSpec(memory_space=pltpu.SMEM),
            pl.BlockSpec((1, rows, width), lambda s: (s, 0, 0)),
            pl.BlockSpec((1, width), lambda s: (0, 0)),
        ],
        out_specs=pl.BlockSpec((chunks, 1, sub, width), lambda s: (0, s, 0, 0)),
        out_shape=jax.ShapeDtypeStruct((chunks, seqs, sub, width), LOW),
        compiler_params=ROOM,
        cost_estimate=cost(0, x, x, x, x),
        name="norm_rows",
    )(place.reshape(1), x, gain_row).reshape(chunks * seqs * sub, width)


def keys_kernel(core_ref, x_ref, near_ref, far_ref, gain_ref, cos_ref, sin_ref, pair_ref, first_ref, raw_ref, full_ref):
    chunks, _, sub, width = x_ref.shape
    half = near_ref.shape[0]
    head = gain_ref.shape[1]

    @pl.when(pl.program_id(0) == 0)
    def _():
        for place, source in ((core_ref[0], near_ref), (1 - core_ref[0], far_ref)):
            full_ref[pl.ds(pl.multiple_of(place * half, half), half), :] = source[...]

    kv = mm(x_ref[...].reshape(chunks * sub, width), full_ref[...])
    key = kv[:, :head]
    n = key * inverse_rms(key) * gain_ref[...]
    rot = (n * cos_ref[...] + turn(n) * sin_ref[...]).astype(LOW)
    value = kv[:, head:].astype(LOW)
    raw_ref[...] = key[:sub]
    pair_ref[:, 0, :, :head] = rot.reshape(chunks, sub, head)
    pair_ref[:, 0, :, head:] = value.reshape(chunks, sub, head)
    first_ref[0, :, :head] = rot[:sub]
    first_ref[0, :, head:] = value[:sub]


def project_keys(core, normed, near, far, gain_row, cos, sin):
    chunks, seqs, sub, width = normed.shape
    half, both = near.shape
    head = both // 2
    whole = lambda *shape: pl.BlockSpec(shape, lambda s: (0,) * len(shape))
    return pl.pallas_call(
        keys_kernel,
        grid=(seqs,),
        in_specs=[
            SMEM,
            pl.BlockSpec((chunks, 1, sub, width), lambda s: (0, s, 0, 0)),
            whole(half, both),
            whole(half, both),
            whole(1, head),
            whole(chunks * sub, head),
            whole(chunks * sub, head),
        ],
        out_specs=[
            pl.BlockSpec((chunks, 1, sub, both), lambda s: (0, s, 0, 0)),
            pl.BlockSpec((1, sub, both), lambda s: (s, 0, 0)),
            pl.BlockSpec((sub, head), lambda s: (s, 0)),
            whole(2 * half, both),
        ],
        out_shape=[
            struct((chunks, seqs, sub, both), LOW),
            struct((seqs, sub, both), LOW),
            struct((seqs * sub, head), F32),
            struct((2 * half, both), LOW),
        ],
        compiler_params=ROOM,
        cost_estimate=cost(seqs * chunks * sub * width * both, normed, normed),
        name="project_keys",
    )(core.reshape(1), normed, near, far, gain_row, cos, sin)


def mask_of(qinfo_ref, kinfo_ref):
    qpos, qseg = qinfo_ref[0, :, 0:1], qinfo_ref[0, :, 1:2]
    kpos, kseg = kinfo_ref[0, 0:1, :], kinfo_ref[0, 1:2, :]
    return (kseg == qseg) & (kpos <= qpos) & (kpos > qpos - WIN)


def key_rows(kv_refs, width):
    own_ref, *far_refs = kv_refs
    sides = []
    for at in (0, width):
        own = own_ref[:, 0, :, at : at + width].reshape(own_ref.shape[0] * own_ref.shape[2], width)
        sides.append(jnp.concatenate([own] + [r[0, :, at : at + width] for r in far_refs], axis=0))
    return sides


def attend_kernel(heads, qinfo_ref, kinfo_ref, q_ref, gain_ref, cos_ref, sin_ref, *refs):
    kv_refs, (rot_ref, out_ref, lse_ref) = refs[:-3], refs[-3:]
    width = q_ref.shape[1] // heads
    scale = width ** (-0.5)
    rotated = []
    for h, q in enumerate(heads_of(q_ref[...], heads)):
        n = q * inverse_rms(q) * gain_ref[...]
        rot = ((n * cos_ref[...] + turn(n) * sin_ref[...]) * scale).astype(LOW)
        rot_ref[:, h * width : (h + 1) * width] = rot
        rotated.append(rot)
    rows = jnp.concatenate(rotated, axis=0)
    keys, vals = key_rows(kv_refs, width)
    bias = jnp.where(mask_of(qinfo_ref, kinfo_ref), 0.0, MASKED)
    allowed = jnp.concatenate([bias] * heads, axis=0) == 0.0
    scores = jnp.where(allowed, mm_t(rows, keys), MASKED)
    top = jnp.max(scores, axis=1, keepdims=True)
    expos = jnp.exp(scores - top)
    total = jnp.sum(expos, axis=1, keepdims=True)
    lse_ref[0] = top + jnp.log(total)
    probs = (expos / total).astype(LOW)
    attended = mm(probs, vals).astype(LOW)
    count = q_ref.shape[0]
    for h in range(heads):
        out_ref[:, h * width : (h + 1) * width] = attended[h * count : (h + 1) * count]


def attend_back_kernel(heads, chunks, blocks, place_ref, qinfo_ref, kinfo_ref, q_ref, gain_ref, cos_ref, sin_ref, rot_ref, lse_ref,
                       dout_ref, *refs):
    far_count = (blocks - 1) * chunks
    kv_refs, (dq_ref, dgain_ref), dkv_refs = refs[: far_count + 1], refs[far_count + 1 : far_count + 3], refs[far_count + 3 :]
    width = q_ref.shape[1] // heads
    scale = width ** (-0.5)
    count = q_ref.shape[0]
    rows = jnp.concatenate(heads_of(rot_ref[...], heads), axis=0)
    douts = jnp.concatenate(heads_of(dout_ref[...], heads), axis=0)
    keys, vals = key_rows(kv_refs, width)
    bias = jnp.where(mask_of(qinfo_ref, kinfo_ref), 0.0, MASKED)
    allowed = jnp.concatenate([bias] * heads, axis=0) == 0.0
    probs = jnp.where(allowed, jnp.exp(mm_t(rows, keys) - lse_ref[0]), 0.0)
    d_probs = mm_t(douts, vals)
    delta = jnp.sum(probs * d_probs, axis=1, keepdims=True)
    d_scores = (probs * (d_probs - delta)).astype(LOW)
    d_rows = mm(d_scores, keys)
    d_keys = t_mm(d_scores, rows)
    d_vals = t_mm(probs.astype(LOW), douts)
    per = kv_refs[0].shape[2]
    own_ref, side_refs, middle_refs = dkv_refs[0], dkv_refs[1:chunks], dkv_refs[chunks:]
    for part, at in ((d_keys, 0), (d_vals, width)):
        piece = lambda b, p: part[(b * chunks + p) * per : (b * chunks + p + 1) * per]
        for b in range(blocks):
            own_ref[b, 0, :, at : at + width] = piece(b, 0)
        for p in range(1, chunks):
            earlier = (place_ref[0] ^ p) < place_ref[0]
            for b in range(1, blocks - 1):
                middle_refs[p - 1][b - 1, 0, :, at : at + width] = piece(b, p).astype(LOW)
            side_refs[p - 1][0, :, at : at + width] = jnp.where(earlier, piece(0, p), piece(blocks - 1, p)).astype(LOW)
    gain_sum = jnp.zeros((1, width), F32)
    for h, q in enumerate(heads_of(q_ref[...], heads)):
        e = d_rows[h * count : (h + 1) * count] * scale
        e = e * cos_ref[...] + turn_back(e * sin_ref[...])
        d_q, d_g = rms_back(e, q, inverse_rms(q), gain_ref[...])
        gain_sum = gain_sum + column_sum(d_g)
        dq_ref[:, h * width : (h + 1) * width] = d_q.astype(LOW)
    dgain_ref[0] = gain_sum


def pair_sum_kernel(*refs):
    out = refs[-1]
    for i in range(out.shape[0]):
        out[i] = (refs[2 * i][...].astype(F32) + refs[2 * i + 1][...].astype(F32)).astype(LOW)


def pair_sum(*pairs):
    rows, width = pairs[0][0].shape
    step = rows // 4 if rows % 64 == 0 else rows
    arrays = [v for pair in pairs for v in pair]
    return pl.pallas_call(
        pair_sum_kernel,
        grid=(rows // step,),
        in_specs=[pl.BlockSpec((step, width), lambda j: (j, 0))] * len(arrays),
        out_specs=pl.BlockSpec((len(pairs), step, width), lambda j: (0, j, 0)),
        out_shape=struct((len(pairs), rows, width), LOW),
        compiler_params=ALL,
        name="pair_sum",
    )(*arrays)


def attention_specs(seqs, rows, spans, chunks, wide, width):
    whole = lambda *shape: pl.BlockSpec(shape, lambda s: (0,) * len(shape))
    return dict(
        qinfo=pl.BlockSpec((1, rows, 2), lambda s: (s, 0, 0)),
        kinfo=pl.BlockSpec((1, 2, spans), lambda s: (s, 0, 0)),
        q=pl.BlockSpec((rows, wide), lambda s: (s, 0)),
        gain=whole(1, width),
        table=whole(rows, width),
        own=pl.BlockSpec((chunks, 1, rows, 2 * width), lambda s: (0, s, 0, 0)),
        far=pl.BlockSpec((1, rows, 2 * width), lambda s: (s, 0, 0)),
        lse=pl.BlockSpec((1, rows * (wide // width), 1), lambda s: (s, 0, 0)),
        dgain=pl.BlockSpec((1, 1, width), lambda s: (s, 0, 0)),
    )


def mix_kernel(att_ref, out_ref, x_ref, gain_attn_ref, gain_ffn_ref, branch_ref, hidden_ref, ffn_ref):
    branch = mm_t(att_ref[...], out_ref[...])
    branch_ref[...] = branch
    hidden = x_ref[...].astype(F32) + branch * inverse_rms(branch) * gain_attn_ref[...]
    hidden_ref[...] = hidden
    ffn_ref[...] = (hidden * inverse_rms(hidden) * gain_ffn_ref[...]).astype(LOW)


def for_blocks(width, step, block):
    full, rest = divmod(width, step)

    @pl.when(pl.program_id(0) < full)
    def _():
        block(step)

    if rest:

        @pl.when(pl.program_id(0) == full)
        def _():
            block(rest)


def add_up(ref, values):
    @pl.when(pl.program_id(0) == 0)
    def _():
        ref[...] = values

    @pl.when(pl.program_id(0) > 0)
    def _():
        ref[...] += values


def ffn_kernel(units, chunks, *refs):
    rows_refs, (gate_ref, up_ref, down_ref) = refs[:chunks], refs[chunks : chunks + 3]
    part_refs, (act_ref, slope_ref, curve_ref, sums) = refs[chunks + 3 : 2 * chunks + 3], refs[2 * chunks + 3 :]

    def block(size):
        rows = jnp.concatenate([r[...] for r in rows_refs], axis=0)
        gate, up = mm(rows, gate_ref[0, :, :size]), mm(rows, up_ref[0, :, :size])
        root = (2.0 / math.pi) ** 0.5
        square = gate * gate
        bend = jnp.tanh(root * (gate + 0.044715 * (square * gate)))
        share = 0.5 * (1.0 + bend)
        curve = gate * share
        slope = share + 0.5 * gate * (1.0 - bend * bend) * (root * (1.0 + 3.0 * 0.044715 * square))
        act = (curve * up).astype(LOW)
        act_ref[:, :size] = act
        slope_ref[:, :size] = (slope * up).astype(LOW)
        curve_ref[:, :size] = curve.astype(LOW)
        add_up(sums, mm_t(act, down_ref[0, :, :size]))

    for_blocks(units, act_ref.shape[1], block)
    split_rows(sums, part_refs)


def split_rows(sums, part_refs):
    @pl.when(pl.program_id(0) == pl.num_programs(0) - 1)
    def _():
        count = part_refs[0].shape[0]
        for p, part in enumerate(part_refs):
            part[...] = sums[p * count : (p + 1) * count].astype(part.dtype)


def ffn_back_kernel(units, chunks, *refs):
    rows_refs, (gate_ref, up_ref, down_ref, slope_ref, curve_ref) = refs[:chunks], refs[chunks : chunks + 5]
    part_refs, (dgate_ref, dup_ref, sums) = refs[chunks + 5 : 2 * chunks + 5], refs[2 * chunks + 5 :]

    def block(size):
        rows = jnp.concatenate([r[...] for r in rows_refs], axis=0)
        d_act = mm(rows, down_ref[0, :, :size])
        d_gate = (d_act * slope_ref[:, :size].astype(F32)).astype(LOW)
        d_up = (d_act * curve_ref[:, :size].astype(F32)).astype(LOW)
        dgate_ref[:, :size] = d_gate
        dup_ref[:, :size] = d_up
        add_up(sums, mm_t(d_gate, gate_ref[0, :, :size]) + mm_t(d_up, up_ref[0, :, :size]))

    for_blocks(units, dgate_ref.shape[1], block)
    split_rows(sums, part_refs)


def ffn_call(kernel, name, rows, weights, saved, results, dtype, step=640):
    chunks = len(rows)
    count, width = rows[0].shape
    units = weights.shape[2]
    whole = pl.BlockSpec((count, width), lambda j: (0, 0))
    strip = pl.BlockSpec((chunks * count, step), lambda j: (0, j))
    flat = pl.pallas_call(
        functools.partial(kernel, units, chunks),
        grid=(pl.cdiv(units, step),),
        in_specs=[whole] * chunks
        + [pl.BlockSpec((1, width, step), lambda j, i=i: (i, 0, j)) for i in range(3)]
        + [strip] * len(saved),
        out_specs=[whole] * chunks + [strip] * results,
        out_shape=[struct((count, width), dtype)] * chunks + [struct((chunks * count, units), LOW)] * results,
        scratch_shapes=[pltpu.VMEM((chunks * count, width), F32)],
        compiler_params=ALL,
        cost_estimate=cost(3 * chunks * count * width * units, *rows, weights, *saved),
        name=name,
    )(*rows, weights, weights, weights, *saved)
    return flat[:chunks], flat[chunks:]


def loss_kernel(factor_ref, hidden_ref, target_ref, valid_ref, gain_ref, *refs):
    parts, (out_ref, dres_ref, dffn_ref, dgain_ref, error_ref) = refs[:-5], refs[-5:]
    ffn = sum(r[...].astype(F32) for r in parts)
    inverse = inverse_rms(ffn)
    result = hidden_ref[...] + ffn * inverse * gain_ref[...]
    out_ref[...] = result.astype(LOW)
    mismatch = result - target_ref[...].astype(F32)
    marked = valid_ref[...] * mismatch
    error_ref[...] = jnp.broadcast_to(column_sum(jnp.sum(marked * mismatch, axis=1, keepdims=True)), error_ref.shape)
    d_result = factor_ref[0] * marked
    dres_ref[...] = d_result
    d_ffn, d_gain = rms_back(d_result, ffn, inverse, gain_ref[...])
    dffn_ref[...] = d_ffn.astype(LOW)
    dgain_ref[...] = column_sum(d_gain)


def middle_kernel(dres_ref, hidden_ref, branch_ref, out_ref, gain_ffn_ref, gain_attn_ref, *refs):
    parts, (dhid_ref, dbranch_ref, datt_ref, dgain_ffn_ref, dgain_attn_ref) = refs[:-5], refs[-5:]
    d_ffn_in = sum(r[...].astype(F32) for r in parts)
    hidden = hidden_ref[...]
    d_add, d_gain = rms_back(d_ffn_in, hidden, inverse_rms(hidden), gain_ffn_ref[...])
    dgain_ffn_ref[...] = column_sum(d_gain)
    d_hidden = dres_ref[...] + d_add
    dhid_ref[...] = d_hidden
    branch = branch_ref[...]
    d_branch, d_gain = rms_back(d_hidden, branch, inverse_rms(branch), gain_attn_ref[...])
    dgain_attn_ref[...] = column_sum(d_gain)
    low = d_branch.astype(LOW)
    dbranch_ref[...] = low
    datt_ref[...] = mm(low, out_ref[...]).astype(LOW)


def pull_kernel(left_ref, right_ref, out_ref):
    out_ref[...] = mm_t(left_ref[...], right_ref[...])


def finish_kernel(chunks, place_ref, raw_ref, cos_ref, sin_ref, gain_key_ref, pulled_ref, kv_ref, dhid_ref, x_ref, gain_ref, normed_ref, *refs):
    parts, (din_ref, dgain_ref, dgain_key_ref, send_ref, own_ref, sums, turned) = refs[:-7], refs[-7:]
    head = raw_ref.shape[1]
    d_kv = sum(r[...].astype(F32) for r in parts)
    key = raw_ref[...]
    e = d_kv[:, :head]
    e = e * cos_ref[...] + turn_back(e * sin_ref[...])
    d_key, d_gain = rms_back(e, key, inverse_rms(key), gain_key_ref[...])
    dgain_key_ref[...] = column_sum(d_gain)
    low = jnp.concatenate([d_key.astype(LOW), d_kv[:, head:].astype(LOW)], axis=1)
    turned[...] = low
    part = low.shape[1] // chunks
    ordered = [turned[:, pl.ds(pl.multiple_of((place_ref[1] ^ p) * part, part), part)] for p in range(chunks)]
    sums[...] = mm(normed_ref[...].T, jnp.concatenate(ordered, axis=1))
    half = own_ref.shape[0]
    core = place_ref[0]
    own_ref[...] = sums[pl.ds(pl.multiple_of(core * half, half), half), :].astype(LOW)
    send_ref[...] = sums[pl.ds(pl.multiple_of((1 - core) * half, half), half), :].astype(LOW)
    d_normed = pulled_ref[...] + mm_t(low, kv_ref[...])
    x = x_ref[...].astype(F32)
    d_x, d_gain = rms_back(d_normed, x, inverse_rms(x), gain_ref[...])
    dgain_ref[...] = column_sum(d_gain)
    din_ref[...] = dhid_ref[...] + d_x


def weight_grad_kernel(chunks, sets, core_ref, *refs):
    lefts, refs = refs[:chunks], refs[chunks:]
    rights, refs = refs[: chunks * sets], refs[chunks * sets :]
    outs, turned = refs[: 2 * sets], refs[2 * sets]
    rows = lefts[0].shape[0]
    half = outs[0].shape[0]

    @pl.when(pl.program_id(0) == 0)
    def _():
        for p in range(chunks):
            turned[:, p * rows : (p + 1) * rows] = lefts[p][...].T

    core = core_ref[0]
    for i in range(sets):
        right = jnp.concatenate([r[...] for r in rights[i * chunks : (i + 1) * chunks]], axis=0)
        for place, out in ((1 - core, outs[2 * i]), (core, outs[2 * i + 1])):
            out[...] = mm(turned[pl.ds(pl.multiple_of(place * half, half), half), :], right).astype(LOW)


def weight_grad(core, rows, lefts, *rights):
    chunks, sets = len(lefts), len(rights)
    widest = rights[0][0][0].shape[1]
    step = 256 if sets > 1 or widest < 1024 else 512 if widest == 1024 else 896
    height = lefts[0][0].shape[1]
    width = rights[0][0][0].shape[1]
    rights = [pair for group in rights for pair in group]
    out = pl.BlockSpec((height // 2, step), lambda j: (0, j))
    flat = pl.pallas_call(
        functools.partial(weight_grad_kernel, chunks, sets),
        grid=(pl.cdiv(width, step),),
        in_specs=[SMEM]
        + [pl.BlockSpec((rows, height), lambda j, at=at: (at, 0)) for _, at in lefts]
        + [pl.BlockSpec((rows, step), lambda j, at=at: (at, j)) for _, at in rights],
        out_specs=[out] * (2 * sets),
        out_shape=[struct((height // 2, width), LOW)] * (2 * sets),
        scratch_shapes=[pltpu.VMEM((height, chunks * rows), LOW)],
        compiler_params=ALL,
        cost_estimate=None if width < height else cost(sets * chunks * rows * height * width, *[v for v, _ in lefts], struct((height, sets * width), LOW)),
        name="weight_grad",
    )(core.reshape(1), *[v for v, _ in lefts], *[v for v, _ in rights])
    return [flat[2 * i : 2 * i + 2] for i in range(sets)]


def shards(inputs, target, segment_ids, w_query, w_key, w_value, w_out, w_gate, w_up, w_down,
           gain_input, gain_query, gain_key, gain_post_attn, gain_pre_ffn, gain_post_ffn):
    F, C, T = (lax.axis_size(a) for a in ("fsdp", "ctx", "tp"))
    f, z, t = (lax.axis_index(a) for a in ("fsdp", "ctx", "tp"))
    me = f * C + z
    seqs, block_rows, width_model = inputs.shape
    piece = w_query.shape[0]
    head_width = w_key.shape[1]
    gain_piece = gain_query.shape[0]
    sub = block_rows // T
    own = seqs * sub
    half = C * piece
    halo = -(-(WIN - 1) // block_rows)
    spans = (halo + 1) * block_rows

    both = 2 * head_width
    blocks = jnp.stack([jnp.concatenate([w_query, w_out.T], axis=1), jnp.concatenate([w_key, w_value], axis=1)])
    near = lax.all_gather(blocks, "ctx", axis=1, tiled=True)
    weights = lax.all_gather(jnp.stack([w_gate, w_up, w_down.T]), ("fsdp", "ctx"), axis=1, tiled=True)
    packed = jnp.concatenate(
        [gain_input, gain_post_attn, gain_pre_ffn, gain_post_ffn, gain_query, gain_key, segment_ids.astype(LOW).reshape(-1)]
    )
    packed = exchange(jnp.broadcast_to(packed[None], (F * C, packed.shape[0])), ("fsdp", "ctx")).astype(F32)
    at = 4 * piece
    g_input, g_post_attn, g_pre_ffn, g_post_ffn = [
        packed[:, i * piece : (i + 1) * piece].reshape(1, width_model) for i in range(4)
    ]
    g_query, g_key = [
        packed[:, at + i * gain_piece : at + (i + 1) * gain_piece].reshape(1, head_width) for i in range(2)
    ]
    seg_blocks = packed[:, at + 2 * gain_piece :].astype(jnp.int32)
    count = jnp.sum((seg_blocks != 0).astype(F32))
    normed = norm_rows(t, inputs, g_input, T)
    def sub_rows(values):
        return [lax.dynamic_slice_in_dim(values, (t ^ p) * sub, sub, 1) for p in range(T)]

    x_own = lax.dynamic_slice_in_dim(inputs, t * sub, sub, 1).reshape(own, width_model)
    target_own = lax.dynamic_slice_in_dim(target, t * sub, sub, 1).reshape(own, width_model)
    positions = jnp.concatenate([z * block_rows + (t ^ p) * sub + jnp.arange(sub, dtype=jnp.int32) for p in range(T)])
    segs = [segment_ids + 1]
    for d in range(1, halo + 1):
        far = lax.dynamic_index_in_dim(seg_blocks, jnp.maximum(me - d, 0), 0, False).reshape(seqs, block_rows)
        segs.append(jnp.where(z >= d, far + 1, 0))
    key_seg = jnp.concatenate([v for seg in segs for v in sub_rows(seg)], axis=1)
    key_pos = jnp.concatenate([positions - d * block_rows for d in range(halo + 1)])
    kinfo = jnp.stack([jnp.broadcast_to(key_pos, (seqs, spans)), key_seg], axis=1)
    qinfo = jnp.stack([jnp.broadcast_to(positions[:sub], (seqs, sub)), key_seg[:, :sub]], axis=2)
    valid_own = (key_seg[:, :sub] != 1).astype(F32).reshape(own, 1)
    cos_all, sin_all = rotary_tables(positions, head_width)
    cos_own, sin_own = cos_all[:sub], sin_all[:sub]

    ready = (normed, kinfo, qinfo, cos_all, sin_all, cos_own, sin_own, g_query, g_key, g_post_attn, g_pre_ffn, x_own)
    (near, *ready) = lax.optimization_barrier((near,) + ready)
    normed, kinfo, qinfo, cos_all, sin_all, cos_own, sin_own, g_query, g_key, g_post_attn, g_pre_ffn, x_own = ready
    near_qo, near_kv = near
    far_kv = swap(near_kv, "fsdp", 1)
    near_qo = [near_qo] + [swap(near_qo, "tp", p) for p in range(1, T)]
    pair, first, key_own, kv_full = project_keys(f, normed.reshape(T, seqs, sub, width_model), near_kv, far_kv, g_key, cos_all, sin_all)
    q_full, out_full = assemble(f, near_qo, [swap(after(v, first), "fsdp", 1) for v in near_qo])
    kv_rows, far = [pair], first
    for d in range(halo):
        far = shifted(far, "ctx", 1)
        kv_rows += [swap(far, "tp", p) if p else far for p in range(T)]
    normed_own = normed[:own]
    q_raw = mm(normed_own, q_full)
    wide = q_raw.shape[1]
    heads = wide // head_width
    specs = attention_specs(seqs, sub, spans, T, wide, head_width)
    kv_specs = [specs["own"]] + [specs["far"]] * (halo * T)
    q_rot, attended, lse = pl.pallas_call(
        functools.partial(attend_kernel, heads),
        grid=(seqs,),
        in_specs=[specs[k] for k in ("qinfo", "kinfo", "q", "gain", "table", "table")] + kv_specs,
        out_specs=[specs["q"], specs["q"], specs["lse"]],
        out_shape=[struct((own, wide), LOW), struct((own, wide), LOW), struct((seqs, sub * heads, 1), F32)],
        compiler_params=ROOM,
        cost_estimate=cost(4 * own * spans * wide // seqs, *kv_rows, q_raw),
        name="attend",
    )(qinfo, kinfo, q_raw, g_query, cos_own, sin_own, *kv_rows)
    token = struct((own, width_model), F32)
    token_low = struct((own, width_model), LOW)
    gain_row = struct((1, width_model), F32)
    branch, hidden, ffn_in = pl.pallas_call(
        mix_kernel, out_shape=[token, token, token_low], compiler_params=ROOM, cost_estimate=cost(own * wide * width_model, out_full, out_full), name="mix"
    )(attended, out_full, x_own, g_post_attn, g_pre_ffn)

    from_tp = lambda parts: parts[:1] + [swap(v, "tp", p) for p, v in enumerate(parts) if p]
    ffn_ins = from_tp([ffn_in] * T)
    groups = [[0], [1], list(range(2, T))]
    place = {p: (g, i) for g, group in enumerate(groups) for i, p in enumerate(group)}
    done = [ffn_call(ffn_kernel, "ffn", [ffn_ins[p] for p in group], weights, (), 3, LOW if g else F32) for g, group in enumerate(groups)]
    parts = [done[place[p][0]][0][place[p][1]] for p in range(T)]
    acts, slopes, curves = zip(*[results for _, results in done])
    acts = [(acts[place[p][0]], place[p][1]) for p in range(T)]
    all_tokens = seqs * block_rows * F * C
    output, d_result, d_ffn_low, dg_post_ffn, error = pl.pallas_call(
        loss_kernel,
        in_specs=[SMEM] + [VMEM] * (4 + T),
        out_shape=[token_low, token, token_low, gain_row, struct((1, 128), F32)],
        compiler_params=ALL,
        cost_estimate=cost(own, *parts, *parts),
        name="loss",
    )((all_tokens / count).reshape(1), hidden, target_own, valid_own, g_post_ffn, *from_tp(parts))

    def collect_core(send, mine, *earlier):
        other = swap(send, "fsdp", 1)
        return mine.astype(F32) + (after(other, *earlier) if earlier else other).astype(F32)

    def scatter_ctx(sums):
        return lax.psum_scatter(sums, "ctx", scatter_dimension=1, tiled=True).astype(F32)

    d_outs = from_tp([d_ffn_low] * T)
    done = []
    for g, group in enumerate(groups):
        rows = [d_outs[p] for p in group]
        if g == 1:
            rows[0] = after(rows[0], done[0][0][0])
        if g == 2:
            rows[0] = after(rows[0], done[1][0][0])
        done.append(ffn_call(ffn_back_kernel, "ffn_back", rows, weights, (slopes[g], curves[g]), 2, LOW if g else F32))
    last = done[-1][0][-1]
    (down_halves,) = weight_grad(f, own, [(v if p else after(v, last), 0) for p, v in enumerate(d_outs)], acts)
    down_sum = pair_sum((down_halves[1], swap(down_halves[0], "fsdp", 1)))
    (grad_down,) = scatter_ctx(down_sum)
    parts = [done[place[p][0]][0][place[p][1]] for p in range(T)]
    d_gates, d_ups = [[(done[place[p][0]][1][i], place[p][1]) for p in range(T)] for i in range(2)]
    first_in = after(ffn_ins[0], down_sum)
    gate_halves, up_halves = weight_grad(f, own, [(v, 0) for v in [first_in] + ffn_ins[1:]], d_gates, d_ups)

    parts = [after(v, *gate_halves, *up_halves) if p == 0 else v for p, v in enumerate(from_tp(parts))]
    d_hidden, d_branch, d_attended, dg_pre_ffn, dg_post_attn = pl.pallas_call(
        middle_kernel,
        out_shape=[token, token_low, struct((own, wide), LOW), gain_row, gain_row],
        compiler_params=ALL,
        cost_estimate=cost(300 * own * wide * width_model, out_full),
        name="middle",
    )(d_result, hidden, branch, out_full, g_pre_ffn, g_post_attn, *parts)
    assert halo * block_rows == WIN
    others = [after(swap(after(v[0], *parts[1:]), "fsdp", 1), d_branch) for v in (gate_halves, up_halves)]
    both_sums = pair_sum((gate_halves[1], others[0]), (up_halves[1], others[1]))
    grad_gate, grad_up = scatter_ctx(both_sums)
    d_attended = after(d_attended, both_sums)
    (out_halves,) = weight_grad(f, own, [(d_branch, 0)], [(attended, 0)])
    out_sum = collect_core(*out_halves)
    out_low = out_sum.astype(LOW)
    d_attended = after(d_attended, *out_halves)
    d_query, dg_query, *d_pairs = pl.pallas_call(
        functools.partial(attend_back_kernel, heads, T, halo + 1),
        grid=(seqs,),
        in_specs=[SMEM] + [specs[k] for k in ("qinfo", "kinfo", "q", "gain", "table", "table", "q", "lse", "q")] + kv_specs,
        out_specs=[specs["q"], specs["dgain"]]
        + [pl.BlockSpec((halo + 1, 1, sub, 2 * head_width), lambda s: (0, s, 0, 0))]
        + [specs["far"]] * (T - 1)
        + [pl.BlockSpec((halo - 1, 1, sub, 2 * head_width), lambda s: (0, s, 0, 0))] * (T - 1),
        out_shape=[struct((own, wide), LOW), struct((seqs, 1, head_width), F32), struct((halo + 1, seqs, sub, 2 * head_width), F32)]
        + [struct((seqs, sub, 2 * head_width), LOW)] * (T - 1)
        + [struct((halo - 1, seqs, sub, 2 * head_width), LOW)] * (T - 1),
        compiler_params=ALL,
        name="attend_back",
    )(t.reshape(1), qinfo, kinfo, q_raw, g_query, cos_own, sin_own, q_rot, lse, d_attended, *kv_rows)
    d_own = after(d_pairs[0], out_low)
    d_blocks = [d_own[b] for b in range(halo + 1)]
    for p in range(1, T):
        got = swap(d_pairs[p], "tp", p).astype(F32)
        later = (t ^ p) > t
        d_blocks[0] = d_blocks[0] + jnp.where(later, got, 0.0)
        d_blocks[halo] = d_blocks[halo] + jnp.where(later, 0.0, got)
    d_kv = d_blocks[halo].astype(LOW)
    for p in range(1, T):
        middle = swap(after(d_pairs[T - 1 + p], d_kv), "tp", p)
        for b in range(1, halo):
            d_blocks[b] = d_blocks[b] + middle[b - 1].astype(F32)
    d_query_late, out_low = after(d_query, d_kv), after(out_low, d_kv)
    for d in range(halo, 0, -1):
        come = shifted(d_kv, "ctx", -1)
        if d > 1:
            d_kv = (d_blocks[d - 1] + come.astype(F32)).astype(LOW)
    d_kv = [d_blocks[0], come]
    head = lambda v, p: v[:, p * head_width : (p + 1) * head_width]
    heads_sent = [jnp.concatenate([head(d_query_late, p), head(out_low, p)], axis=0) for p in range(1, T)]
    heads_here = [swap(v, "tp", p + 1) for p, v in enumerate(heads_sent)]
    out_head = head(out_sum, 0)
    for v in heads_here:
        out_head = out_head + v[own:].astype(F32)
    normed_late = after(normed, come)
    (q_halves,) = weight_grad(f, own, [(normed_late, p) for p in range(T)], [(head(d_query, 0), 0)] + [(v, 0) for v in heads_here])
    pulled = pl.pallas_call(
        pull_kernel, out_shape=token, compiler_params=ROOM, name="pull"
    )(d_query, q_full)

    def pack(values, wide):
        top = lax.reduce_precision(values, 8, 7)
        flat = jnp.concatenate([top, values - top], axis=1).astype(LOW)
        rows = -(-flat.shape[1] // wide)
        return jnp.pad(flat, ((0, 0), (0, rows * wide - flat.shape[1]))).reshape(values.shape[0], rows, wide)

    def unpack(rows, n):
        flat = rows.reshape(-1)
        return flat[:n] + flat[n : 2 * n]

    def core_rows(values):
        rows = jnp.concatenate([v.reshape(F * C, -1) for v in values], axis=1).reshape(F, C, -1)
        return lax.dynamic_index_in_dim(rows, f, 0, False) + swap(lax.dynamic_index_in_dim(rows, f ^ 1, 0, False), "fsdp", 1)

    def owner_sums(weight_sums, rows, *earlier):
        wide = weight_sums.shape[1]
        sent = jnp.concatenate([weight_sums.reshape(C, piece, wide), pack(rows, wide)], axis=1)
        sums = jnp.sum(after(exchange(sent, "ctx"), *earlier).astype(F32), axis=0)
        return sums[:piece], unpack(sums[piece:], rows.shape[1])

    early = core_rows(
        [dg_post_attn, dg_pre_ffn, dg_post_ffn, jnp.sum(dg_query, axis=(0, 1)), jnp.broadcast_to(error[:, :1], (F * C, 1))]
    )
    both_heads = jnp.concatenate([collect_core(*q_halves).astype(LOW), out_head.astype(LOW)], axis=1)
    d_kv[0] = after(d_kv[0], both_heads, pulled)
    own_rows = lambda table: jnp.tile(table, (seqs, 1))
    grad_input, dg_input, dg_key, *kv_halves = pl.pallas_call(
        functools.partial(finish_kernel, T),
        in_specs=[SMEM] + [VMEM] * (10 + len(d_kv)),
        out_shape=[token, gain_row, struct((1, head_width), F32)] + [struct((half, 2 * head_width), LOW)] * 2,
        scratch_shapes=[pltpu.VMEM((2 * half, 2 * head_width), F32), pltpu.VMEM((own, 2 * head_width), LOW)],
        compiler_params=ROOM,
        name="finish",
    )(jnp.stack([f, t]), key_own, own_rows(cos_own), own_rows(sin_own), g_key, pulled, kv_full, d_hidden, x_own, g_input,
      normed_own, *[v.reshape(own, 2 * head_width) for v in d_kv])
    late = core_rows([dg_input, dg_key])
    part = 2 * head_width // T
    kv_sum = collect_core(*kv_halves)
    kv_low = kv_sum.astype(LOW)
    kv_part = kv_sum[:, :part]
    for p in range(1, T):
        kv_part = kv_part + swap(kv_low[:, p * part : (p + 1) * part], "tp", p).astype(F32)
    sums = jnp.concatenate([both_heads, kv_part.astype(LOW)], axis=1)
    sums, total = owner_sums(sums, jnp.concatenate([early, late], axis=1), grad_gate, grad_up)
    grad_query, grad_out = sums[:, :head_width], sums[:, head_width : 2 * head_width]
    n = total.shape[0]
    rows = -(-n // part)
    mine = jnp.concatenate([sums[:, 2 * head_width :], jnp.pad(total, (0, rows * part - n)).reshape(rows, part)], axis=0)
    pieces = [swap(mine, "tp", p) if p else mine for p in range(T)]
    whole = jnp.stack(pieces)
    grad_kv = jnp.concatenate([lax.dynamic_index_in_dim(whole, t ^ p, 0, False)[:piece] for p in range(T)], axis=1)
    totals = {p: v[piece:] for p, v in enumerate(pieces)}
    bit = 1
    while bit < T:
        totals = {p: totals[p] + totals[p ^ bit] for p in totals if not p & bit}
        bit *= 2
    total = totals[0].reshape(-1)[:n]
    early, late = total[: early.shape[1]], total[early.shape[1] :]
    loss = early[-1] / (2.0 * width_model * count)
    at = 3 * piece
    return (
        output.reshape(seqs, sub, width_model),
        loss,
        grad_input.reshape(seqs, sub, width_model),
        grad_query,
        grad_kv[:, :head_width],
        grad_kv[:, head_width:],
        grad_out.T,
        grad_gate,
        grad_up,
        grad_down.T,
        late[:piece],
        early[at : at + gain_piece],
        late[piece:],
        early[:piece],
        early[piece : 2 * piece],
        early[2 * piece : at],
    )


def solution(mesh):
    rows = P(("fsdp", "ctx"), "tp")
    cols = P("tp", ("fsdp", "ctx"))
    split = P(("fsdp", "ctx"), None)
    gain = P(("fsdp", "ctx"))
    token = P("fsdp", "ctx", None)
    own = P("fsdp", ("ctx", "tp"), None)
    weights = (rows, split, split, cols, rows, rows, cols)
    return jax.shard_map(
        shards,
        mesh=mesh,
        in_specs=(token, token, P("fsdp", "ctx")) + weights + (gain,) * 6,
        out_specs=(own, P(), own) + weights + (gain,) * 6,
        check_vma=False,
    )
```

```python
import functools
import math

import jax
import jax.numpy as jnp
from jax import lax
from jax.experimental import pallas as pl
from jax.experimental.pallas import tpu as pltpu
from jax.sharding import PartitionSpec as P

WIN = 512
EPS = 1e-06
MASKED = -1e30
LOW = jnp.bfloat16
F32 = jnp.float32


def swap(values, axis, bits):
    return lax.ppermute(values, axis, [(i, i ^ bits) for i in range(lax.axis_size(axis))])


def shifted(values, axis, by):
    size = lax.axis_size(axis)
    return lax.ppermute(values, axis, [(i, i + by) for i in range(size) if 0 <= i + by < size])


def exchange(values, axes):
    return lax.all_to_all(values, axes, 0, 0, tiled=True)


def after(value, *earlier):
    return lax.optimization_barrier((value,) + earlier)[0]


def dot(left, right, contract):
    return lax.dot_general(left, right, (contract, ((), ())), preferred_element_type=F32)


def mm(left, right):
    return dot(left, right, ((1,), (0,)))


def mm_t(left, right):
    return dot(left, right, ((1,), (1,)))


def t_mm(left, right):
    return dot(left, right, ((0,), (0,)))


def inverse_rms(values):
    return lax.rsqrt(jnp.mean(values * values, axis=-1, keepdims=True) + EPS)


def rms_back(grad, values, inverse, gain_row):
    n = values * inverse
    eg = grad * gain_row
    return inverse * (eg - n * jnp.mean(eg * n, axis=-1, keepdims=True)), grad * n


def turn(values):
    half = values.shape[-1] // 2
    return jnp.concatenate([-values[..., half:], values[..., :half]], axis=-1)


def turn_back(values):
    half = values.shape[-1] // 2
    return jnp.concatenate([values[..., half:], -values[..., :half]], axis=-1)


def rotary_tables(positions, head_width):
    frequency = 10000.0 ** (-2.0 * jnp.arange(head_width // 2, dtype=F32) / head_width)
    angles = positions.astype(F32)[:, None] * frequency[None, :]
    angles = jnp.concatenate([angles, angles], axis=-1)
    return jnp.cos(angles), jnp.sin(angles)


def heads_of(values, heads):
    width = values.shape[1] // heads
    return [values[:, h * width : (h + 1) * width] for h in range(heads)]


VMEM = pl.BlockSpec(memory_space=pltpu.VMEM)
SMEM = pl.BlockSpec(memory_space=pltpu.SMEM)
ROOM = pltpu.CompilerParams(vmem_limit_bytes=28 * 1024 * 1024)
ALL = pltpu.CompilerParams(vmem_limit_bytes=60 * 1024 * 1024)


def cost(multiply_adds, *arrays):
    moved = sum(math.prod(v.shape) * jnp.dtype(v.dtype).itemsize for v in arrays)
    return pl.CostEstimate(flops=2 * multiply_adds, bytes_accessed=moved, transcendentals=0)


def struct(shape, dtype):
    return jax.ShapeDtypeStruct(shape, dtype)


def column_sum(values):
    return jnp.sum(values, axis=0, keepdims=True)


def assemble_kernel(pieces, core_ref, *refs):
    width = refs[0].shape[1] // 2
    results = refs[2 * pieces :]
    for step in range(2):

        @pl.when(pl.program_id(0) == step)
        def _():
            for i, result in enumerate(results):
                for p in range(pieces):
                    result[0, :, p * width : (p + 1) * width] = refs[step * pieces + p][:, i * width : (i + 1) * width]


def assemble(core, mine, others):
    half, width = mine[0].shape
    pieces = len(mine)
    wide = pieces * width // 2
    out = pl.BlockSpec((1, half, wide), lambda i, core: (i ^ core[0], 0, 0))
    results = pl.pallas_call(
        functools.partial(assemble_kernel, pieces),
        grid_spec=pltpu.PrefetchScalarGridSpec(
            num_scalar_prefetch=1,
            grid=(2,),
            in_specs=[pl.BlockSpec((half, width), lambda i, core: (0, 0))] * (2 * pieces),
            out_specs=[out, out],
        ),
        out_shape=[struct((2, half, wide), LOW)] * 2,
        compiler_params=ROOM,
        cost_estimate=cost(0, *mine, *others, *mine, *others),
        name="assemble",
    )(core.reshape(1), *mine, *others)
    return [v.reshape(2 * half, wide) for v in results]


def norm_rows_kernel(chunks, place_ref, x_ref, gain_ref, out_ref):
    sub = x_ref.shape[1] // chunks
    for p in range(chunks):
        x = x_ref[0, pl.ds(pl.multiple_of((place_ref[0] ^ p) * sub, sub), sub), :].astype(F32)
        out_ref[p, 0] = (x * inverse_rms(x) * gain_ref[...]).astype(LOW)


def norm_rows(place, x, gain_row, chunks):
    seqs, rows, width = x.shape
    sub = rows // chunks
    return pl.pallas_call(
        functools.partial(norm_rows_kernel, chunks),
        grid=(seqs,),
        in_specs=[
            pl.BlockSpec(memory_space=pltpu.SMEM),
            pl.BlockSpec((1, rows, width), lambda s: (s, 0, 0)),
            pl.BlockSpec((1, width), lambda s: (0, 0)),
        ],
        out_specs=pl.BlockSpec((chunks, 1, sub, width), lambda s: (0, s, 0, 0)),
        out_shape=jax.ShapeDtypeStruct((chunks, seqs, sub, width), LOW),
        compiler_params=ROOM,
        cost_estimate=cost(0, x, x, x, x),
        name="norm_rows",
    )(place.reshape(1), x, gain_row).reshape(chunks * seqs * sub, width)


def keys_kernel(core_ref, x_ref, near_ref, far_ref, gain_ref, cos_ref, sin_ref, pair_ref, first_ref, raw_ref, full_ref):
    chunks, _, sub, width = x_ref.shape
    half = near_ref.shape[0]
    head = gain_ref.shape[1]

    @pl.when(pl.program_id(0) == 0)
    def _():
        for place, source in ((core_ref[0], near_ref), (1 - core_ref[0], far_ref)):
            full_ref[pl.ds(pl.multiple_of(place * half, half), half), :] = source[...]

    kv = mm(x_ref[...].reshape(chunks * sub, width), full_ref[...])
    key = kv[:, :head]
    n = key * inverse_rms(key) * gain_ref[...]
    rot = (n * cos_ref[...] + turn(n) * sin_ref[...]).astype(LOW)
    value = kv[:, head:].astype(LOW)
    raw_ref[...] = key[:sub]
    pair_ref[:, 0, :, :head] = rot.reshape(chunks, sub, head)
    pair_ref[:, 0, :, head:] = value.reshape(chunks, sub, head)
    first_ref[0, :, :head] = rot[:sub]
    first_ref[0, :, head:] = value[:sub]


def project_keys(core, normed, near, far, gain_row, cos, sin):
    chunks, seqs, sub, width = normed.shape
    half, both = near.shape
    head = both // 2
    whole = lambda *shape: pl.BlockSpec(shape, lambda s: (0,) * len(shape))
    return pl.pallas_call(
        keys_kernel,
        grid=(seqs,),
        in_specs=[
            SMEM,
            pl.BlockSpec((chunks, 1, sub, width), lambda s: (0, s, 0, 0)),
            whole(half, both),
            whole(half, both),
            whole(1, head),
            whole(chunks * sub, head),
            whole(chunks * sub, head),
        ],
        out_specs=[
            pl.BlockSpec((chunks, 1, sub, both), lambda s: (0, s, 0, 0)),
            pl.BlockSpec((1, sub, both), lambda s: (s, 0, 0)),
            pl.BlockSpec((sub, head), lambda s: (s, 0)),
            whole(2 * half, both),
        ],
        out_shape=[
            struct((chunks, seqs, sub, both), LOW),
            struct((seqs, sub, both), LOW),
            struct((seqs * sub, head), F32),
            struct((2 * half, both), LOW),
        ],
        compiler_params=ROOM,
        cost_estimate=cost(seqs * chunks * sub * width * both, normed, normed),
        name="project_keys",
    )(core.reshape(1), normed, near, far, gain_row, cos, sin)


def mask_of(qinfo_ref, kinfo_ref):
    qpos, qseg = qinfo_ref[0, :, 0:1], qinfo_ref[0, :, 1:2]
    kpos, kseg = kinfo_ref[0, 0:1, :], kinfo_ref[0, 1:2, :]
    return (kseg == qseg) & (kpos <= qpos) & (kpos > qpos - WIN)


def key_rows(kv_refs, width):
    own_ref, *far_refs = kv_refs
    sides = []
    for at in (0, width):
        own = own_ref[:, 0, :, at : at + width].reshape(own_ref.shape[0] * own_ref.shape[2], width)
        sides.append(jnp.concatenate([own] + [r[0, :, at : at + width] for r in far_refs], axis=0))
    return sides


def attend_kernel(heads, qinfo_ref, kinfo_ref, q_ref, gain_ref, cos_ref, sin_ref, *refs):
    kv_refs, (rot_ref, out_ref, lse_ref) = refs[:-3], refs[-3:]
    width = q_ref.shape[1] // heads
    scale = width ** (-0.5)
    rotated = []
    for h, q in enumerate(heads_of(q_ref[...], heads)):
        n = q * inverse_rms(q) * gain_ref[...]
        rot = ((n * cos_ref[...] + turn(n) * sin_ref[...]) * scale).astype(LOW)
        rot_ref[:, h * width : (h + 1) * width] = rot
        rotated.append(rot)
    rows = jnp.concatenate(rotated, axis=0)
    keys, vals = key_rows(kv_refs, width)
    bias = jnp.where(mask_of(qinfo_ref, kinfo_ref), 0.0, MASKED)
    allowed = jnp.concatenate([bias] * heads, axis=0) == 0.0
    scores = jnp.where(allowed, mm_t(rows, keys), MASKED)
    top = jnp.max(scores, axis=1, keepdims=True)
    expos = jnp.exp(scores - top)
    total = jnp.sum(expos, axis=1, keepdims=True)
    lse_ref[0] = top + jnp.log(total)
    probs = (expos / total).astype(LOW)
    attended = mm(probs, vals).astype(LOW)
    count = q_ref.shape[0]
    for h in range(heads):
        out_ref[:, h * width : (h + 1) * width] = attended[h * count : (h + 1) * count]


def attend_back_kernel(heads, chunks, blocks, place_ref, qinfo_ref, kinfo_ref, q_ref, gain_ref, cos_ref, sin_ref, rot_ref, lse_ref,
                       dout_ref, *refs):
    far_count = (blocks - 1) * chunks
    kv_refs, (dq_ref, dgain_ref), dkv_refs = refs[: far_count + 1], refs[far_count + 1 : far_count + 3], refs[far_count + 3 :]
    width = q_ref.shape[1] // heads
    scale = width ** (-0.5)
    count = q_ref.shape[0]
    rows = jnp.concatenate(heads_of(rot_ref[...], heads), axis=0)
    douts = jnp.concatenate(heads_of(dout_ref[...], heads), axis=0)
    keys, vals = key_rows(kv_refs, width)
    bias = jnp.where(mask_of(qinfo_ref, kinfo_ref), 0.0, MASKED)
    allowed = jnp.concatenate([bias] * heads, axis=0) == 0.0
    probs = jnp.where(allowed, jnp.exp(mm_t(rows, keys) - lse_ref[0]), 0.0)
    d_probs = mm_t(douts, vals)
    delta = jnp.sum(probs * d_probs, axis=1, keepdims=True)
    d_scores = (probs * (d_probs - delta)).astype(LOW)
    d_rows = mm(d_scores, keys)
    d_keys = t_mm(d_scores, rows)
    d_vals = t_mm(probs.astype(LOW), douts)
    per = kv_refs[0].shape[2]
    own_ref, side_refs, middle_refs = dkv_refs[0], dkv_refs[1:chunks], dkv_refs[chunks:]
    for part, at in ((d_keys, 0), (d_vals, width)):
        piece = lambda b, p: part[(b * chunks + p) * per : (b * chunks + p + 1) * per]
        for b in range(blocks):
            own_ref[b, 0, :, at : at + width] = piece(b, 0).astype(LOW)
        for p in range(1, chunks):
            earlier = (place_ref[0] ^ p) < place_ref[0]
            for b in range(1, blocks - 1):
                middle_refs[p - 1][b - 1, 0, :, at : at + width] = piece(b, p).astype(LOW)
            side_refs[p - 1][0, :, at : at + width] = jnp.where(earlier, piece(0, p), piece(blocks - 1, p)).astype(LOW)
    gain_sum = jnp.zeros((1, width), F32)
    for h, q in enumerate(heads_of(q_ref[...], heads)):
        e = d_rows[h * count : (h + 1) * count] * scale
        e = e * cos_ref[...] + turn_back(e * sin_ref[...])
        d_q, d_g = rms_back(e, q, inverse_rms(q), gain_ref[...])
        gain_sum = gain_sum + column_sum(d_g)
        dq_ref[:, h * width : (h + 1) * width] = d_q.astype(LOW)
    dgain_ref[0] = gain_sum


def pair_sum_kernel(*refs):
    out = refs[-1]
    for i in range(out.shape[0]):
        out[i] = (refs[2 * i][...].astype(F32) + refs[2 * i + 1][...].astype(F32)).astype(LOW)


def pair_sum(*pairs):
    rows, width = pairs[0][0].shape
    step = rows // 4 if rows % 64 == 0 else rows
    arrays = [v for pair in pairs for v in pair]
    return pl.pallas_call(
        pair_sum_kernel,
        grid=(rows // step,),
        in_specs=[pl.BlockSpec((step, width), lambda j: (j, 0))] * len(arrays),
        out_specs=pl.BlockSpec((len(pairs), step, width), lambda j: (0, j, 0)),
        out_shape=struct((len(pairs), rows, width), LOW),
        compiler_params=ALL,
        name="pair_sum",
    )(*arrays)


def attention_specs(seqs, rows, spans, chunks, wide, width):
    whole = lambda *shape: pl.BlockSpec(shape, lambda s: (0,) * len(shape))
    return dict(
        qinfo=pl.BlockSpec((1, rows, 2), lambda s: (s, 0, 0)),
        kinfo=pl.BlockSpec((1, 2, spans), lambda s: (s, 0, 0)),
        q=pl.BlockSpec((rows, wide), lambda s: (s, 0)),
        gain=whole(1, width),
        table=whole(rows, width),
        own=pl.BlockSpec((chunks, 1, rows, 2 * width), lambda s: (0, s, 0, 0)),
        far=pl.BlockSpec((1, rows, 2 * width), lambda s: (s, 0, 0)),
        lse=pl.BlockSpec((1, rows * (wide // width), 1), lambda s: (s, 0, 0)),
        dgain=pl.BlockSpec((1, 1, width), lambda s: (s, 0, 0)),
    )


def mix_kernel(att_ref, out_ref, x_ref, gain_attn_ref, gain_ffn_ref, branch_ref, hidden_ref, ffn_ref):
    branch = mm_t(att_ref[...], out_ref[...])
    branch_ref[...] = branch
    hidden = x_ref[...].astype(F32) + branch * inverse_rms(branch) * gain_attn_ref[...]
    hidden_ref[...] = hidden
    ffn_ref[...] = (hidden * inverse_rms(hidden) * gain_ffn_ref[...]).astype(LOW)


def for_blocks(width, step, block):
    full, rest = divmod(width, step)

    @pl.when(pl.program_id(0) < full)
    def _():
        block(step)

    if rest:

        @pl.when(pl.program_id(0) == full)
        def _():
            block(rest)


def ffn_kernel(units, chunks, *refs):
    rows_refs, (gate_ref, up_ref, down_ref) = refs[:chunks], refs[chunks : chunks + 3]
    part_refs, (act_ref, slope_ref, curve_ref, sums) = refs[chunks + 3 : 2 * chunks + 3], refs[2 * chunks + 3 :]

    @pl.when(pl.program_id(0) == 0)
    def _():
        sums[...] = jnp.zeros_like(sums)

    def block(size):
        rows = jnp.concatenate([r[...] for r in rows_refs], axis=0)
        gate, up = mm(rows, gate_ref[0, :, :size]), mm(rows, up_ref[0, :, :size])
        root = (2.0 / math.pi) ** 0.5
        square = gate * gate
        bend = jnp.tanh(root * (gate + 0.044715 * (square * gate)))
        share = 0.5 * (1.0 + bend)
        curve = gate * share
        slope = share + 0.5 * gate * (1.0 - bend * bend) * (root * (1.0 + 3.0 * 0.044715 * square))
        act = (curve * up).astype(LOW)
        act_ref[:, :size] = act
        slope_ref[:, :size] = (slope * up).astype(LOW)
        curve_ref[:, :size] = curve.astype(LOW)
        sums[...] += mm_t(act, down_ref[0, :, :size])

    for_blocks(units, act_ref.shape[1], block)
    split_rows(sums, part_refs)


def split_rows(sums, part_refs):
    @pl.when(pl.program_id(0) == pl.num_programs(0) - 1)
    def _():
        count = part_refs[0].shape[0]
        for p, part in enumerate(part_refs):
            part[...] = sums[p * count : (p + 1) * count].astype(part.dtype)


def ffn_back_kernel(units, chunks, *refs):
    rows_refs, (gate_ref, up_ref, down_ref, slope_ref, curve_ref) = refs[:chunks], refs[chunks : chunks + 5]
    part_refs, (dgate_ref, dup_ref, sums) = refs[chunks + 5 : 2 * chunks + 5], refs[2 * chunks + 5 :]

    @pl.when(pl.program_id(0) == 0)
    def _():
        sums[...] = jnp.zeros_like(sums)

    def block(size):
        rows = jnp.concatenate([r[...] for r in rows_refs], axis=0)
        d_act = mm(rows, down_ref[0, :, :size])
        d_gate = (d_act * slope_ref[:, :size].astype(F32)).astype(LOW)
        d_up = (d_act * curve_ref[:, :size].astype(F32)).astype(LOW)
        dgate_ref[:, :size] = d_gate
        dup_ref[:, :size] = d_up
        sums[...] += mm_t(d_gate, gate_ref[0, :, :size]) + mm_t(d_up, up_ref[0, :, :size])

    for_blocks(units, dgate_ref.shape[1], block)
    split_rows(sums, part_refs)


def ffn_call(kernel, name, rows, weights, saved, results, dtype, step=640):
    chunks = len(rows)
    count, width = rows[0].shape
    units = weights.shape[2]
    whole = pl.BlockSpec((count, width), lambda j: (0, 0))
    strip = pl.BlockSpec((chunks * count, step), lambda j: (0, j))
    flat = pl.pallas_call(
        functools.partial(kernel, units, chunks),
        grid=(pl.cdiv(units, step),),
        in_specs=[whole] * chunks
        + [pl.BlockSpec((1, width, step), lambda j, i=i: (i, 0, j)) for i in range(3)]
        + [strip] * len(saved),
        out_specs=[whole] * chunks + [strip] * results,
        out_shape=[struct((count, width), dtype)] * chunks + [struct((chunks * count, units), LOW)] * results,
        scratch_shapes=[pltpu.VMEM((chunks * count, width), F32)],
        compiler_params=ALL,
        cost_estimate=cost(3 * chunks * count * width * units, *rows, weights, *saved),
        name=name,
    )(*rows, weights, weights, weights, *saved)
    return flat[:chunks], flat[chunks:]


def loss_kernel(factor_ref, hidden_ref, target_ref, valid_ref, gain_ref, *refs):
    parts, (out_ref, dres_ref, dffn_ref, dgain_ref, error_ref) = refs[:-5], refs[-5:]
    ffn = sum(r[...].astype(F32) for r in parts)
    inverse = inverse_rms(ffn)
    result = hidden_ref[...] + ffn * inverse * gain_ref[...]
    out_ref[...] = result.astype(LOW)
    mismatch = result - target_ref[...].astype(F32)
    marked = valid_ref[...] * mismatch
    error_ref[...] = jnp.broadcast_to(column_sum(jnp.sum(marked * mismatch, axis=1, keepdims=True)), error_ref.shape)
    d_result = factor_ref[0] * marked
    dres_ref[...] = d_result
    d_ffn, d_gain = rms_back(d_result, ffn, inverse, gain_ref[...])
    dffn_ref[...] = d_ffn.astype(LOW)
    dgain_ref[...] = column_sum(d_gain)


def middle_kernel(dres_ref, hidden_ref, branch_ref, out_ref, gain_ffn_ref, gain_attn_ref, *refs):
    parts, (dhid_ref, dbranch_ref, datt_ref, dgain_ffn_ref, dgain_attn_ref) = refs[:-5], refs[-5:]
    d_ffn_in = sum(r[...].astype(F32) for r in parts)
    hidden = hidden_ref[...]
    d_add, d_gain = rms_back(d_ffn_in, hidden, inverse_rms(hidden), gain_ffn_ref[...])
    dgain_ffn_ref[...] = column_sum(d_gain)
    d_hidden = dres_ref[...] + d_add
    dhid_ref[...] = d_hidden
    branch = branch_ref[...]
    d_branch, d_gain = rms_back(d_hidden, branch, inverse_rms(branch), gain_attn_ref[...])
    dgain_attn_ref[...] = column_sum(d_gain)
    low = d_branch.astype(LOW)
    dbranch_ref[...] = low
    datt_ref[...] = mm(low, out_ref[...]).astype(LOW)


def pull_kernel(left_ref, right_ref, out_ref):
    out_ref[...] = mm_t(left_ref[...], right_ref[...])


def finish_kernel(chunks, place_ref, raw_ref, cos_ref, sin_ref, gain_key_ref, pulled_ref, kv_ref, dhid_ref, x_ref, gain_ref, normed_ref, *refs):
    parts, (din_ref, dgain_ref, dgain_key_ref, send_ref, own_ref, sums, turned) = refs[:-7], refs[-7:]
    head = raw_ref.shape[1]
    d_kv = sum(r[...].astype(F32) for r in parts)
    key = raw_ref[...]
    e = d_kv[:, :head]
    e = e * cos_ref[...] + turn_back(e * sin_ref[...])
    d_key, d_gain = rms_back(e, key, inverse_rms(key), gain_key_ref[...])
    dgain_key_ref[...] = column_sum(d_gain)
    low = jnp.concatenate([d_key.astype(LOW), d_kv[:, head:].astype(LOW)], axis=1)
    turned[...] = low
    part = low.shape[1] // chunks
    ordered = [turned[:, pl.ds(pl.multiple_of((place_ref[1] ^ p) * part, part), part)] for p in range(chunks)]
    sums[...] = mm(normed_ref[...].T, jnp.concatenate(ordered, axis=1))
    half = own_ref.shape[0]
    core = place_ref[0]
    own_ref[...] = sums[pl.ds(pl.multiple_of(core * half, half), half), :].astype(LOW)
    send_ref[...] = sums[pl.ds(pl.multiple_of((1 - core) * half, half), half), :].astype(LOW)
    d_normed = pulled_ref[...] + mm_t(low, kv_ref[...])
    x = x_ref[...].astype(F32)
    d_x, d_gain = rms_back(d_normed, x, inverse_rms(x), gain_ref[...])
    dgain_ref[...] = column_sum(d_gain)
    din_ref[...] = dhid_ref[...] + d_x


def weight_grad_kernel(chunks, sets, core_ref, *refs):
    lefts, refs = refs[:chunks], refs[chunks:]
    rights, refs = refs[: chunks * sets], refs[chunks * sets :]
    outs, turned = refs[: 2 * sets], refs[2 * sets]
    rows = lefts[0].shape[0]
    half = outs[0].shape[0]

    @pl.when(pl.program_id(0) == 0)
    def _():
        for p in range(chunks):
            turned[:, p * rows : (p + 1) * rows] = lefts[p][...].T

    core = core_ref[0]
    for i in range(sets):
        right = jnp.concatenate([r[...] for r in rights[i * chunks : (i + 1) * chunks]], axis=0)
        for place, out in ((1 - core, outs[2 * i]), (core, outs[2 * i + 1])):
            out[...] = mm(turned[pl.ds(pl.multiple_of(place * half, half), half), :], right).astype(LOW)


def weight_grad(core, rows, lefts, *rights):
    chunks, sets = len(lefts), len(rights)
    widest = rights[0][0][0].shape[1]
    step = 256 if sets > 1 or widest < 1024 else 1024 if widest == 1024 else 896
    height = lefts[0][0].shape[1]
    width = rights[0][0][0].shape[1]
    rights = [pair for group in rights for pair in group]
    out = pl.BlockSpec((height // 2, step), lambda j: (0, j))
    flat = pl.pallas_call(
        functools.partial(weight_grad_kernel, chunks, sets),
        grid=(pl.cdiv(width, step),),
        in_specs=[SMEM]
        + [pl.BlockSpec((rows, height), lambda j, at=at: (at, 0)) for _, at in lefts]
        + [pl.BlockSpec((rows, step), lambda j, at=at: (at, j)) for _, at in rights],
        out_specs=[out] * (2 * sets),
        out_shape=[struct((height // 2, width), LOW)] * (2 * sets),
        scratch_shapes=[pltpu.VMEM((height, chunks * rows), LOW)],
        compiler_params=ALL,
        cost_estimate=None if width < height else cost(sets * chunks * rows * height * width, *[v for v, _ in lefts], struct((height, sets * width), LOW)),
        name="weight_grad",
    )(core.reshape(1), *[v for v, _ in lefts], *[v for v, _ in rights])
    return [flat[2 * i : 2 * i + 2] for i in range(sets)]


def shards(inputs, target, segment_ids, w_query, w_key, w_value, w_out, w_gate, w_up, w_down,
           gain_input, gain_query, gain_key, gain_post_attn, gain_pre_ffn, gain_post_ffn):
    F, C, T = (lax.axis_size(a) for a in ("fsdp", "ctx", "tp"))
    f, z, t = (lax.axis_index(a) for a in ("fsdp", "ctx", "tp"))
    me = f * C + z
    seqs, block_rows, width_model = inputs.shape
    piece = w_query.shape[0]
    head_width = w_key.shape[1]
    gain_piece = gain_query.shape[0]
    sub = block_rows // T
    own = seqs * sub
    half = C * piece
    halo = -(-(WIN - 1) // block_rows)
    spans = (halo + 1) * block_rows

    both = 2 * head_width
    blocks = jnp.stack([jnp.concatenate([w_query, w_out.T], axis=1), jnp.concatenate([w_key, w_value], axis=1)])
    near = lax.all_gather(blocks, "ctx", axis=1, tiled=True)
    weights = lax.all_gather(jnp.stack([w_gate, w_up, w_down.T]), ("fsdp", "ctx"), axis=1, tiled=True)
    packed = jnp.concatenate(
        [gain_input, gain_post_attn, gain_pre_ffn, gain_post_ffn, gain_query, gain_key, segment_ids.astype(LOW).reshape(-1)]
    )
    packed = exchange(jnp.broadcast_to(packed[None], (F * C, packed.shape[0])), ("fsdp", "ctx")).astype(F32)
    at = 4 * piece
    g_input, g_post_attn, g_pre_ffn, g_post_ffn = [
        packed[:, i * piece : (i + 1) * piece].reshape(1, width_model) for i in range(4)
    ]
    g_query, g_key = [
        packed[:, at + i * gain_piece : at + (i + 1) * gain_piece].reshape(1, head_width) for i in range(2)
    ]
    seg_blocks = packed[:, at + 2 * gain_piece :].astype(jnp.int32)
    count = jnp.sum((seg_blocks != 0).astype(F32))
    normed = norm_rows(t, inputs, g_input, T)
    def sub_rows(values):
        return [lax.dynamic_slice_in_dim(values, (t ^ p) * sub, sub, 1) for p in range(T)]

    x_own = lax.dynamic_slice_in_dim(inputs, t * sub, sub, 1).reshape(own, width_model)
    target_own = lax.dynamic_slice_in_dim(target, t * sub, sub, 1).reshape(own, width_model)
    positions = jnp.concatenate([z * block_rows + (t ^ p) * sub + jnp.arange(sub, dtype=jnp.int32) for p in range(T)])
    segs = [segment_ids + 1]
    for d in range(1, halo + 1):
        far = lax.dynamic_index_in_dim(seg_blocks, jnp.maximum(me - d, 0), 0, False).reshape(seqs, block_rows)
        segs.append(jnp.where(z >= d, far + 1, 0))
    key_seg = jnp.concatenate([v for seg in segs for v in sub_rows(seg)], axis=1)
    key_pos = jnp.concatenate([positions - d * block_rows for d in range(halo + 1)])
    kinfo = jnp.stack([jnp.broadcast_to(key_pos, (seqs, spans)), key_seg], axis=1)
    qinfo = jnp.stack([jnp.broadcast_to(positions[:sub], (seqs, sub)), key_seg[:, :sub]], axis=2)
    valid_own = (key_seg[:, :sub] != 1).astype(F32).reshape(own, 1)
    cos_all, sin_all = rotary_tables(positions, head_width)
    cos_own, sin_own = cos_all[:sub], sin_all[:sub]

    ready = (normed, kinfo, qinfo, cos_all, sin_all, cos_own, sin_own, g_query, g_key, g_post_attn, g_pre_ffn, x_own)
    (near, *ready) = lax.optimization_barrier((near,) + ready)
    normed, kinfo, qinfo, cos_all, sin_all, cos_own, sin_own, g_query, g_key, g_post_attn, g_pre_ffn, x_own = ready
    near_qo, near_kv = near
    far_kv = swap(near_kv, "fsdp", 1)
    near_qo = [near_qo] + [swap(near_qo, "tp", p) for p in range(1, T)]
    pair, first, key_own, kv_full = project_keys(f, normed.reshape(T, seqs, sub, width_model), near_kv, far_kv, g_key, cos_all, sin_all)
    q_full, out_full = assemble(f, near_qo, [swap(after(v, first), "fsdp", 1) for v in near_qo])
    kv_rows, far = [pair], first
    for d in range(halo):
        far = shifted(far, "ctx", 1)
        kv_rows += [swap(far, "tp", p) if p else far for p in range(T)]
    normed_own = normed[:own]
    q_raw = mm(normed_own, q_full)
    wide = q_raw.shape[1]
    heads = wide // head_width
    specs = attention_specs(seqs, sub, spans, T, wide, head_width)
    kv_specs = [specs["own"]] + [specs["far"]] * (halo * T)
    q_rot, attended, lse = pl.pallas_call(
        functools.partial(attend_kernel, heads),
        grid=(seqs,),
        in_specs=[specs[k] for k in ("qinfo", "kinfo", "q", "gain", "table", "table")] + kv_specs,
        out_specs=[specs["q"], specs["q"], specs["lse"]],
        out_shape=[struct((own, wide), LOW), struct((own, wide), LOW), struct((seqs, sub * heads, 1), F32)],
        compiler_params=ROOM,
        cost_estimate=cost(4 * own * spans * wide // seqs, *kv_rows, q_raw),
        name="attend",
    )(qinfo, kinfo, q_raw, g_query, cos_own, sin_own, *kv_rows)
    token = struct((own, width_model), F32)
    token_low = struct((own, width_model), LOW)
    gain_row = struct((1, width_model), F32)
    branch, hidden, ffn_in = pl.pallas_call(
        mix_kernel, out_shape=[token, token, token_low], compiler_params=ROOM, cost_estimate=cost(own * wide * width_model, out_full, out_full), name="mix"
    )(attended, out_full, x_own, g_post_attn, g_pre_ffn)

    from_tp = lambda parts: parts[:1] + [swap(v, "tp", p) for p, v in enumerate(parts) if p]
    ffn_ins = from_tp([ffn_in] * T)
    groups = [[0], [1], list(range(2, T))]
    place = {p: (g, i) for g, group in enumerate(groups) for i, p in enumerate(group)}
    done = [ffn_call(ffn_kernel, "ffn", [ffn_ins[p] for p in group], weights, (), 3, LOW if g else F32) for g, group in enumerate(groups)]
    parts = [done[place[p][0]][0][place[p][1]] for p in range(T)]
    acts, slopes, curves = zip(*[results for _, results in done])
    acts = [(acts[place[p][0]], place[p][1]) for p in range(T)]
    all_tokens = seqs * block_rows * F * C
    output, d_result, d_ffn_low, dg_post_ffn, error = pl.pallas_call(
        loss_kernel,
        in_specs=[SMEM] + [VMEM] * (4 + T),
        out_shape=[token_low, token, token_low, gain_row, struct((1, 128), F32)],
        compiler_params=ALL,
        cost_estimate=cost(own, *parts, *parts),
        name="loss",
    )((all_tokens / count).reshape(1), hidden, target_own, valid_own, g_post_ffn, *from_tp(parts))

    def collect_core(send, mine, *earlier):
        other = swap(send, "fsdp", 1)
        return mine.astype(F32) + (after(other, *earlier) if earlier else other).astype(F32)

    def scatter_ctx(sums):
        return lax.psum_scatter(sums, "ctx", scatter_dimension=1, tiled=True).astype(F32)

    d_outs = from_tp([d_ffn_low] * T)
    done = []
    for g, group in enumerate(groups):
        rows = [d_outs[p] for p in group]
        if g == 1:
            rows[0] = after(rows[0], done[0][0][0])
        if g == 2:
            rows[0] = after(rows[0], done[1][0][0])
        done.append(ffn_call(ffn_back_kernel, "ffn_back", rows, weights, (slopes[g], curves[g]), 2, LOW if g else F32))
    last = done[-1][0][-1]
    (down_halves,) = weight_grad(f, own, [(v if p else after(v, last), 0) for p, v in enumerate(d_outs)], acts)
    down_sum = pair_sum((down_halves[1], swap(down_halves[0], "fsdp", 1)))
    (grad_down,) = scatter_ctx(down_sum)
    parts = [done[place[p][0]][0][place[p][1]] for p in range(T)]
    d_gates, d_ups = [[(done[place[p][0]][1][i], place[p][1]) for p in range(T)] for i in range(2)]
    first_in = after(ffn_ins[0], down_sum)
    gate_halves, up_halves = weight_grad(f, own, [(v, 0) for v in [first_in] + ffn_ins[1:]], d_gates, d_ups)

    parts = [after(v, *gate_halves, *up_halves) if p == 0 else v for p, v in enumerate(from_tp(parts))]
    d_hidden, d_branch, d_attended, dg_pre_ffn, dg_post_attn = pl.pallas_call(
        middle_kernel,
        out_shape=[token, token_low, struct((own, wide), LOW), gain_row, gain_row],
        compiler_params=ALL,
        cost_estimate=cost(300 * own * wide * width_model, out_full),
        name="middle",
    )(d_result, hidden, branch, out_full, g_pre_ffn, g_post_attn, *parts)
    assert halo * block_rows == WIN
    others = [after(swap(after(v[0], *parts[1:]), "fsdp", 1), d_branch) for v in (gate_halves, up_halves)]
    both_sums = pair_sum((gate_halves[1], others[0]), (up_halves[1], others[1]))
    grad_gate, grad_up = scatter_ctx(both_sums)
    d_attended = after(d_attended, both_sums)
    (out_halves,) = weight_grad(f, own, [(d_branch, 0)], [(attended, 0)])
    out_sum = collect_core(*out_halves)
    out_low = out_sum.astype(LOW)
    d_attended = after(d_attended, *out_halves)
    d_query, dg_query, *d_pairs = pl.pallas_call(
        functools.partial(attend_back_kernel, heads, T, halo + 1),
        grid=(seqs,),
        in_specs=[SMEM] + [specs[k] for k in ("qinfo", "kinfo", "q", "gain", "table", "table", "q", "lse", "q")] + kv_specs,
        out_specs=[specs["q"], specs["dgain"]]
        + [pl.BlockSpec((halo + 1, 1, sub, 2 * head_width), lambda s: (0, s, 0, 0))]
        + [specs["far"]] * (T - 1)
        + [pl.BlockSpec((halo - 1, 1, sub, 2 * head_width), lambda s: (0, s, 0, 0))] * (T - 1),
        out_shape=[struct((own, wide), LOW), struct((seqs, 1, head_width), F32), struct((halo + 1, seqs, sub, 2 * head_width), LOW)]
        + [struct((seqs, sub, 2 * head_width), LOW)] * (T - 1)
        + [struct((halo - 1, seqs, sub, 2 * head_width), LOW)] * (T - 1),
        compiler_params=ALL,
        name="attend_back",
    )(t.reshape(1), qinfo, kinfo, q_raw, g_query, cos_own, sin_own, q_rot, lse, d_attended, *kv_rows)
    d_own = after(d_pairs[0], out_low)
    d_blocks = [d_own[b].astype(F32) for b in range(halo + 1)]
    for p in range(1, T):
        got = swap(d_pairs[p], "tp", p).astype(F32)
        later = (t ^ p) > t
        d_blocks[0] = d_blocks[0] + jnp.where(later, got, 0.0)
        d_blocks[halo] = d_blocks[halo] + jnp.where(later, 0.0, got)
    d_kv = d_blocks[halo].astype(LOW)
    for p in range(1, T):
        middle = swap(after(d_pairs[T - 1 + p], d_kv), "tp", p)
        for b in range(1, halo):
            d_blocks[b] = d_blocks[b] + middle[b - 1].astype(F32)
    d_query_late, out_low = after(d_query, d_kv), after(out_low, d_kv)
    for d in range(halo, 0, -1):
        come = shifted(d_kv, "ctx", -1)
        if d > 1:
            d_kv = (d_blocks[d - 1] + come.astype(F32)).astype(LOW)
    d_kv = [d_blocks[0], come]
    head = lambda v, p: v[:, p * head_width : (p + 1) * head_width]
    heads_sent = [jnp.concatenate([head(d_query_late, p), head(out_low, p)], axis=0) for p in range(1, T)]
    heads_here = [swap(v, "tp", p + 1) for p, v in enumerate(heads_sent)]
    out_head = head(out_sum, 0)
    for v in heads_here:
        out_head = out_head + v[own:].astype(F32)
    normed_late = after(normed, come)
    (q_halves,) = weight_grad(f, own, [(normed_late, p) for p in range(T)], [(head(d_query, 0), 0)] + [(v, 0) for v in heads_here])
    pulled = pl.pallas_call(
        pull_kernel, out_shape=token, compiler_params=ROOM, name="pull"
    )(d_query, q_full)

    def pack(values, wide):
        top = lax.reduce_precision(values, 8, 7)
        flat = jnp.concatenate([top, values - top], axis=1).astype(LOW)
        rows = -(-flat.shape[1] // wide)
        return jnp.pad(flat, ((0, 0), (0, rows * wide - flat.shape[1]))).reshape(values.shape[0], rows, wide)

    def unpack(rows, n):
        flat = rows.reshape(-1)
        return flat[:n] + flat[n : 2 * n]

    def core_rows(values):
        rows = jnp.concatenate([v.reshape(F * C, -1) for v in values], axis=1).reshape(F, C, -1)
        return lax.dynamic_index_in_dim(rows, f, 0, False) + swap(lax.dynamic_index_in_dim(rows, f ^ 1, 0, False), "fsdp", 1)

    def owner_sums(weight_sums, rows, *earlier):
        wide = weight_sums.shape[1]
        sent = jnp.concatenate([weight_sums.reshape(C, piece, wide), pack(rows, wide)], axis=1)
        sums = jnp.sum(after(exchange(sent, "ctx"), *earlier).astype(F32), axis=0)
        return sums[:piece], unpack(sums[piece:], rows.shape[1])

    early = core_rows(
        [dg_post_attn, dg_pre_ffn, dg_post_ffn, jnp.sum(dg_query, axis=(0, 1)), jnp.broadcast_to(error[:, :1], (F * C, 1))]
    )
    both_heads = jnp.concatenate([collect_core(*q_halves).astype(LOW), out_head.astype(LOW)], axis=1)
    d_kv[0] = after(d_kv[0], both_heads, pulled)
    own_rows = lambda table: jnp.tile(table, (seqs, 1))
    grad_input, dg_input, dg_key, *kv_halves = pl.pallas_call(
        functools.partial(finish_kernel, T),
        in_specs=[SMEM] + [VMEM] * (10 + len(d_kv)),
        out_shape=[token, gain_row, struct((1, head_width), F32)] + [struct((half, 2 * head_width), LOW)] * 2,
        scratch_shapes=[pltpu.VMEM((2 * half, 2 * head_width), F32), pltpu.VMEM((own, 2 * head_width), LOW)],
        compiler_params=ROOM,
        name="finish",
    )(jnp.stack([f, t]), key_own, own_rows(cos_own), own_rows(sin_own), g_key, pulled, kv_full, d_hidden, x_own, g_input,
      normed_own, *[v.reshape(own, 2 * head_width) for v in d_kv])
    late = core_rows([dg_input, dg_key])
    part = 2 * head_width // T
    kv_sum = collect_core(*kv_halves)
    kv_low = kv_sum.astype(LOW)
    kv_part = kv_sum[:, :part]
    for p in range(1, T):
        kv_part = kv_part + swap(kv_low[:, p * part : (p + 1) * part], "tp", p).astype(F32)
    sums = jnp.concatenate([both_heads, kv_part.astype(LOW)], axis=1)
    sums, total = owner_sums(sums, jnp.concatenate([early, late], axis=1), grad_gate, grad_up)
    grad_query, grad_out = sums[:, :head_width], sums[:, head_width : 2 * head_width]
    n = total.shape[0]
    rows = -(-n // part)
    mine = jnp.concatenate([sums[:, 2 * head_width :], jnp.pad(total, (0, rows * part - n)).reshape(rows, part)], axis=0)
    pieces = [swap(mine, "tp", p) if p else mine for p in range(T)]
    whole = jnp.stack(pieces)
    grad_kv = jnp.concatenate([lax.dynamic_index_in_dim(whole, t ^ p, 0, False)[:piece] for p in range(T)], axis=1)
    totals = {p: v[piece:] for p, v in enumerate(pieces)}
    bit = 1
    while bit < T:
        totals = {p: totals[p] + totals[p ^ bit] for p in totals if not p & bit}
        bit *= 2
    total = totals[0].reshape(-1)[:n]
    early, late = total[: early.shape[1]], total[early.shape[1] :]
    loss = early[-1] / (2.0 * width_model * count)
    at = 3 * piece
    return (
        output.reshape(seqs, sub, width_model),
        loss,
        grad_input.reshape(seqs, sub, width_model),
        grad_query,
        grad_kv[:, :head_width],
        grad_kv[:, head_width:],
        grad_out.T,
        grad_gate,
        grad_up,
        grad_down.T,
        late[:piece],
        early[at : at + gain_piece],
        late[piece:],
        early[:piece],
        early[piece : 2 * piece],
        early[2 * piece : at],
    )


def solution(mesh):
    rows = P(("fsdp", "ctx"), "tp")
    cols = P("tp", ("fsdp", "ctx"))
    split = P(("fsdp", "ctx"), None)
    gain = P(("fsdp", "ctx"))
    token = P("fsdp", "ctx", None)
    own = P("fsdp", ("ctx", "tp"), None)
    weights = (rows, split, split, cols, rows, rows, cols)
    return jax.shard_map(
        shards,
        mesh=mesh,
        in_specs=(token, token, P("fsdp", "ctx")) + weights + (gain,) * 6,
        out_specs=(own, P(), own) + weights + (gain,) * 6,
        check_vma=False,
    )
```
